128 devices in a mesh: row: 8 (over z_lo, y), col: 16 (over x, z_hi, core).
Axes of the slice: x: 4, y: 4, z: 4 (z_hi: 2, z_lo: 2; z = z_hi * 2 + z_lo), core: 2. Of those that a mesh axis runs over, the one named last changes fastest.
Arguments:
- positions: int32 [8, 16, 16, 2], P('row', 'col'), may hold values from -128 to 3967, as said below
- counts: int32 [8, 16], P('row', 'col'), may hold values from 1 to 16, as said below
- amplitudes: bfloat16 [8, 16, 16, 256, 256], P('row', 'col'), may hold values from 0.19921875 to 5
- object_field: float32 [2, 2048, 4096], P(None, 'row', 'col'), may hold values from -6 to 6
- probe: float32 [2, 256, 256], replicated, may hold values from -6 to 6
Outputs:
- object_new: float32 [2, 2048, 4096], P(None, 'row', 'col')
- probe_new: float32 [2, 256, 256], replicated
The draws below stay inside these ranges and needn't reach their ends.
Inputs may be any that keep to these rules, and one draw needn't show every extreme that they name: `positions`: slot k of tile (i, j) holds the corner of a patch whose centre (corner plus 256/2 in each coordinate) lies in that tile: rows i * 256 to (i + 1) * 256 - 1 and columns j * 256 to (j + 1) * 256 - 1. Slots at or beyond the tile's count are not read. `counts`: some tile has exactly 16 live positions.
All inputs are finite; a program needn't handle non-finite values.
Results may differ from the reference program's by a relative error of at most 0.0039.
Values sent between devices are 32-bit elements; how exact they have to be, the bound alone decides.
A program may use at most 192 MiB of HBM per device.

```python
import math
import jax
import jax.numpy as jnp
from jax import lax

F = 256
TR = 256
TC = 256
MOST = 16
ITERS = 2
NR = 2048
NC = 4096
N_ROW = 8
N_COL = 16


def draw_counts(key, part):
    key = jax.random.fold_in(key, 11)
    keys = jax.random.split(key, 4)
    tile_total = N_ROW * N_COL
    light = jax.random.randint(keys[0], (tile_total,), 1, max(MOST // 4, 1) + 1)
    heavy = jax.random.randint(keys[1], (tile_total,), MOST - MOST // 4, MOST + 1)
    chosen = jax.random.randint(keys[2], (tile_total,), 0, 4) != 0
    fullest = jax.random.randint(keys[3], (), 0, tile_total)
    tile_loads = jnp.where(chosen, heavy, light)
    tile_loads = jnp.where(jnp.arange(tile_total) == fullest, MOST, tile_loads)
    return tile_loads.reshape(N_ROW, N_COL).astype(jnp.int32)


def draw_positions(key, part):
    key = jax.random.fold_in(key, 12)
    keys = jax.random.split(key, 2)
    shape = (N_ROW, N_COL, MOST)
    row_offset = jax.random.randint(keys[0], shape, 0, TR)
    col_offset = jax.random.randint(keys[1], shape, 0, TC)
    row_offset = row_offset.at[0, 0, 0].set(0).at[N_ROW - 1, N_COL - 1, 0].set(TR - 1)
    col_offset = col_offset.at[0, 0, 0].set(0).at[N_ROW - 1, N_COL - 1, 0].set(TC - 1)
    tile_row = jnp.arange(N_ROW)[:, None, None] * TR
    tile_col = jnp.arange(N_COL)[None, :, None] * TC
    return jnp.stack([tile_row + row_offset - F // 2, tile_col + col_offset - F // 2], -1).astype(jnp.int32)


def steps_of(stream_key, shape, cuts, least, largest):
    loudness = 1.0
    for dim, parts in cuts:
        draws = jax.random.uniform(jax.random.fold_in(jax.random.fold_in(stream_key, 6), dim), (parts,), jnp.float32, least / len(cuts), largest / len(cuts))
        loudness = loudness * jnp.repeat(jnp.exp(draws), shape[dim] // parts).reshape((-1,) + (1,) * (len(shape) - 1 - dim))
    return loudness


def normal_values(own_key, extent, deviation, bound, shards=(), kind=jnp.bfloat16):
    entries = deviation * jax.random.normal(own_key, extent, jnp.float32)
    if shards:
        entries = entries * steps_of(own_key, extent, shards, -0.22, 0.18)
    return jnp.clip(entries, -bound, bound).astype(kind)


def setup_inputs(seed: int = 0) -> dict:
    splits = jax.random.split(jax.random.key(seed), 6)
    positions = draw_positions(jax.random.fold_in(splits[5], 71), 0)
    counts = draw_counts(jax.random.fold_in(splits[5], 71), 0)
    amplitudes = jnp.clip(jnp.exp(math.log(5.0) - 3.2227897 * jax.random.uniform(splits[2], (N_ROW, N_COL, MOST, F, F), jnp.float32) ** steps_of(splits[2], (N_ROW, N_COL, MOST, F, F), ((0, 8), (1, 16)), -0.2, 0.2)), 0.19921875, 5.0).astype(jnp.bfloat16)
    object_field = normal_values(splits[3], (2, NR, NC), 0.7, 6.0, ((1, 8), (2, 16)), jnp.float32)
    probe = normal_values(splits[4], (2, F, F), 1.0, 6.0, (), jnp.float32)
    return {"positions": positions, "counts": counts, "amplitudes": amplitudes, "object_field": object_field, "probe": probe}


def dft_tables():
    counter = jnp.arange(F, dtype=jnp.int32)
    phases = counter[:, None] * counter[None, :] % F
    angles = phases.astype(jnp.float32) * (2.0 * math.pi / F)
    factor = 1.0 / math.sqrt(F)
    table_re = (jnp.cos(angles) * factor).astype(jnp.bfloat16)
    table_im = (-jnp.sin(angles) * factor).astype(jnp.bfloat16)
    return (table_re, table_im)

def complex_product(left_re, left_im, right_re, right_im):
    real_part = jnp.dot(left_re, right_re, preferred_element_type=jnp.float32) - jnp.dot(left_im, right_im, preferred_element_type=jnp.float32)
    imag_part = jnp.dot(left_re, right_im, preferred_element_type=jnp.float32) + jnp.dot(left_im, right_re, preferred_element_type=jnp.float32)
    return (real_part, imag_part)

def slot_update(patch_cells, amplitude, probe, table_re, table_im):
    probe_re = probe[0]
    probe_im = probe[1]
    patch_re = patch_cells[0]
    patch_im = patch_cells[1]
    exit_re = (probe_re * patch_re - probe_im * patch_im).astype(jnp.bfloat16)
    exit_im = (probe_re * patch_im + probe_im * patch_re).astype(jnp.bfloat16)
    half_re, half_im = complex_product(table_re, table_im, exit_re, exit_im)
    far_re, far_im = complex_product(half_re.astype(jnp.bfloat16), half_im.astype(jnp.bfloat16), table_re, table_im)
    ratio_term = amplitude.astype(jnp.float32) / jnp.sqrt(far_re * far_re + far_im * far_im + 1.0)
    miss_re = (far_re - ratio_term * far_re).astype(jnp.bfloat16)
    miss_im = (far_im - ratio_term * far_im).astype(jnp.bfloat16)
    back_re, back_im = complex_product(table_re, -table_im, miss_re, miss_im)
    chi_re, chi_im = complex_product(back_re.astype(jnp.bfloat16), back_im.astype(jnp.bfloat16), table_re, -table_im)
    object_grad = jnp.stack([probe_re * chi_re + probe_im * chi_im, probe_re * chi_im - probe_im * chi_re])
    probe_grad = jnp.stack([patch_re * chi_re + patch_im * chi_im, patch_re * chi_im - patch_im * chi_re])
    weight = patch_re * patch_re + patch_im * patch_im
    return (object_grad, probe_grad, weight)

def reference(positions, counts, amplitudes, object_field, probe):
    half_width = F // 2
    table_re, table_im = dft_tables()
    tile_total = N_ROW * N_COL
    places = positions.reshape(tile_total, MOST, 2)
    tile_loads = counts.reshape(tile_total)
    measured = amplitudes.reshape(tile_total, MOST, F, F)
    rows_all = object_field.shape[1]
    cols_all = object_field.shape[2]
    zero_index = jnp.zeros((), jnp.int32)
    for iteration in range(ITERS):
        padded = jnp.pad(object_field, ((0, 0), (half_width, half_width), (half_width, half_width)))
        coverage = probe[0] * probe[0] + probe[1] * probe[1]
        current_probe = probe

        def tile_loop(tile_index, carried):

            def slot_loop(slot_index, inner_carry):
                gradient, probe_sum, weight_sum = inner_carry
                corner_row = (places[tile_index, slot_index, 0] + half_width).astype(jnp.int32)
                corner_col = (places[tile_index, slot_index, 1] + half_width).astype(jnp.int32)
                patch_cells = lax.dynamic_slice(padded, (zero_index, corner_row, corner_col), (2, F, F))
                object_grad, probe_grad, weight = slot_update(patch_cells, measured[tile_index, slot_index], current_probe, table_re, table_im)
                update = jnp.concatenate([object_grad, coverage[None]], 0)
                present = lax.dynamic_slice(gradient, (zero_index, corner_row, corner_col), (3, F, F))
                gradient = lax.dynamic_update_slice(gradient, present + update, (zero_index, corner_row, corner_col))
                return (gradient, probe_sum + probe_grad, weight_sum + weight)
            return lax.fori_loop(0, tile_loads[tile_index], slot_loop, carried)
        initial = (jnp.zeros((3, rows_all + F, cols_all + F), jnp.float32), jnp.zeros((2, F, F), jnp.float32), jnp.zeros((F, F), jnp.float32))
        gradient, probe_sum, weight_sum = lax.fori_loop(0, tile_total, tile_loop, initial)
        inside = gradient[:, half_width:half_width + rows_all, half_width:half_width + cols_all]
        object_field = object_field - inside[:2] / (inside[2] + 1.0)
        probe = probe - probe_sum / (weight_sum + 1.0)
    return (object_field, probe)
```

```python
import functools, math
import numpy as np
import jax, jax.numpy as jnp
from jax import lax
from jax.experimental import pallas as pl
from jax.experimental.pallas import tpu as pltpu
from jax.sharding import PartitionSpec as P

F = 256
ITERS = 2
f32=jnp.float32; bf16=jnp.bfloat16

def tables():
    c=np.arange(F,dtype=np.int32)
    ang=(c[:,None]*c[None,:]%F).astype(np.float32)*np.float32(2*math.pi/F)
    re=(np.cos(ang)/np.float32(16)).astype(np.float32)
    im=(-np.sin(ang)/np.float32(16)).astype(np.float32)
    fwd=np.block([[re,-im],[im,re]]); inv=np.block([[re,im],[-im,re]])
    return jnp.asarray(fwd,bf16), jnp.asarray(inv,bf16)

CH=16
def slots_kernel(corner, load, amp, ext, probe, fwd, inv, grad, psum,
                 patch, cov, exit_s, half_s, miss_s, chi_s):
    grad[...]=jnp.zeros(grad.shape,f32)
    psum[...]=jnp.zeros(psum.shape,f32)
    cov[...]=probe[0]*probe[0]+probe[1]*probe[1]
    lane=lax.broadcasted_iota(jnp.int32,(CH,128),1)
    def slot(k,_):
        r=corner[k,0]; c=corner[k,1]
        q=c//128; s=c-q*128
        back=jnp.where(s==0,0,128-s)
        keep=lane<128-s
        for i in range(F//CH):
            rows=pl.ds(i*CH,CH)
            got=[]
            for ch in range(2):
                t=[pltpu.roll(ext[ch,q+j,pl.ds(r+i*CH,CH),:],back,1) for j in range(3)]
                got.append(jnp.concatenate([jnp.where(keep,t[0],t[1]),jnp.where(keep,t[1],t[2])],1))
            re,im=got
            patch[0,rows,:]=re; patch[1,rows,:]=im
            pr=probe[0,rows,:]; pi=probe[1,rows,:]
            exit_s[rows,:]=(pr*re-pi*im).astype(bf16)
            exit_s[pl.ds(F+i*CH,CH),:]=(pr*im+pi*re).astype(bf16)
            psum[2,rows,:]+=re*re+im*im
        half=jnp.dot(fwd[...],exit_s[...],preferred_element_type=f32).astype(bf16)
        half_s[:,:F]=half[:F]; half_s[:,F:]=half[F:]
        far=jnp.dot(half_s[...],inv[...],preferred_element_type=f32)
        fr=far[:,:F]; fi=far[:,F:]
        ratio=1.0-amp[k].astype(f32)*lax.rsqrt(fr*fr+fi*fi+1.0)
        miss_s[:F,:]=(fr*ratio).astype(bf16)
        miss_s[F:,:]=(fi*ratio).astype(bf16)
        back_=jnp.dot(inv[...],miss_s[...],preferred_element_type=f32).astype(bf16)
        half_s[:,:F]=back_[:F]; half_s[:,F:]=back_[F:]
        chi_s[...]=jnp.dot(half_s[...],fwd[...],preferred_element_type=f32)
        put=lane>=s
        for i in range(F//CH):
            rows=pl.ds(i*CH,CH)
            cr=chi_s[rows,:F]; ci=chi_s[rows,F:]
            pr=probe[0,rows,:]; pi=probe[1,rows,:]
            re=patch[0,rows,:]; im=patch[1,rows,:]
            psum[0,rows,:]+=re*cr+im*ci
            psum[1,rows,:]+=re*ci-im*cr
            for ch,u in ((0,pr*cr+pi*ci),(1,pr*ci-pi*cr),(2,cov[rows,:])):
                u0=pltpu.roll(u[:,:128],s,1); u1=pltpu.roll(u[:,128:],s,1)
                at=pl.ds(r+i*CH,CH)
                grad[ch,q,at,:]+=jnp.where(put,u0,0.0)
                grad[ch,q+1,at,:]+=jnp.where(put,u1,u0)
                grad[ch,q+2,at,:]+=jnp.where(put,0.0,u1)
        return 0
    lax.fori_loop(0,load[0],slot,0)

def slots(corner,load,amp,ext,probe,fwd,inv):
    V=pl.BlockSpec(memory_space=pltpu.VMEM); S=pl.BlockSpec(memory_space=pltpu.SMEM)
    return pl.pallas_call(slots_kernel,
        out_shape=(jax.ShapeDtypeStruct((3,4,512,128),f32),jax.ShapeDtypeStruct((3,F,F),f32)),
        in_specs=[S,S,V,V,V,V,V], out_specs=(V,V),
        scratch_shapes=[pltpu.VMEM((2,F,F),f32),pltpu.VMEM((F,F),f32),pltpu.VMEM((2*F,F),bf16),
            pltpu.VMEM((F,2*F),bf16),pltpu.VMEM((2*F,F),bf16),pltpu.VMEM((F,2*F),f32)],
        compiler_params=pltpu.CompilerParams(vmem_limit_bytes=48*2**20),
    )(corner,load,amp,ext,probe,fwd,inv)
MESH = pl.DeviceIdType.MESH
HALF = F // 2
TILE = slice(HALF, HALF + F)


class Places:
    def __init__(self):
        row, col = lax.axis_index("row"), lax.axis_index("col")
        n_row, n_col = lax.axis_size("row"), lax.axis_size("col")
        self.row, self.col, self.n_row, self.n_col = row, col, n_row, n_col
        z_lo, self.y = row // 4, row % 4
        self.x, z_hi, self.core = col // 4, col // 2 % 2, col % 2
        self.z = z_hi * 2 + z_lo
        self.up, self.down = ((row + n_row - 1) % n_row, col), ((row + 1) % n_row, col)
        self.left, self.right = (row, (col + n_col - 1) % n_col), (row, (col + 1) % n_col)
        self.sides = (self.up, self.down, self.left, self.right)
        self.twin = (row, col + 1 - 2 * self.core)
        self.along_x = [(row, (self.x + d) % 4 * 4 + col % 4) for d in (1, 2, 3)]
        self.along_y = [(z_lo * 4 + (self.y + d) % 4, col) for d in (1, 2, 3)]
        self.along_z = []
        for d in (1, 2, 3):
            z = (self.z + d) % 4
            self.along_z.append((z % 2 * 4 + self.y, self.x * 4 + z // 2 * 2 + self.core))


def meet(peers):
    barrier = pltpu.get_barrier_semaphore()
    for peer in peers:
        pl.semaphore_signal(barrier, inc=1, device_id=peer, device_id_type=MESH)
    pl.semaphore_wait(barrier, len(peers))


class Sender:
    def __init__(self, send_sem, recv_sem):
        self.send_sem, self.recv_sem, self.used = send_sem, recv_sem, 0
        self.open = []

    def __call__(self, src, dst, peer):
        copy = pltpu.make_async_remote_copy(
            src_ref=src,
            dst_ref=dst,
            send_sem=self.send_sem.at[self.used],
            recv_sem=self.recv_sem.at[self.used],
            device_id=peer,
            device_id_type=MESH,
        )
        self.used += 1
        copy.start()
        self.open.append(copy)
        return copy

    def close(self):
        for copy in self.open:
            copy.wait_send()


def arrive(copies):
    for copy in copies:
        copy.wait_recv()


TOP, BOTTOM = pl.ds(HALF, HALF), pl.ds(F, HALF)
ABOVE, BELOW = pl.ds(0, HALF), pl.ds(F + HALF, HALF)
INNER, BOTH, ALL = pl.ds(HALF, F), pl.ds(1, 2), pl.ds(0, 4)


def halo_first(send, at, ext):
    return [
        send(ext.at[0, BOTH, TOP, :], ext.at[0, BOTH, BELOW, :], at.up),
        send(ext.at[0, BOTH, BOTTOM, :], ext.at[0, BOTH, ABOVE, :], at.down),
        send(ext.at[1, 1, INNER, :], ext.at[1, 3, INNER, :], at.left),
        send(ext.at[1, 2, INNER, :], ext.at[1, 0, INNER, :], at.right),
    ]


def halo_second(send, at, ext):
    return [
        send(ext.at[0, 1, :, :], ext.at[0, 3, :, :], at.left),
        send(ext.at[0, 2, :, :], ext.at[0, 0, :, :], at.right),
        send(ext.at[1, ALL, TOP, :], ext.at[1, ALL, BELOW, :], at.up),
        send(ext.at[1, ALL, BOTTOM, :], ext.at[1, ALL, ABOVE, :], at.down),
    ]


def clear_outside(at, ext):
    @pl.when(at.row == 0)
    def _():
        ext[:, :, :HALF, :] = jnp.zeros((2, 4, HALF, 128), f32)

    @pl.when(at.row == at.n_row - 1)
    def _():
        ext[:, :, F + HALF :, :] = jnp.zeros((2, 4, HALF, 128), f32)

    @pl.when(at.col == 0)
    def _():
        ext[:, 0, :, :] = jnp.zeros((2, 2 * F, 128), f32)

    @pl.when(at.col == at.n_col - 1)
    def _():
        ext[:, 3, :, :] = jnp.zeros((2, 2 * F, 128), f32)


def open_kernel(cells, ext, send_sem, recv_sem):
    at = Places()
    meet(at.sides)
    for part in range(2):
        for j in range(2):
            ext[part, 1 + j, TILE, :] = cells[part, :, 128 * j : 128 * j + 128]
    send = Sender(send_sem, recv_sem)
    arrive(halo_first(send, at, ext))
    arrive(halo_second(send, at, ext))
    send.close()
    clear_outside(at, ext)


def step_kernel(last, grad, psum, old, probe, new, probe_new, *scratch):
    acc, rows_in, cols_in, acc0, buf0, acc1, buf1, acc2, buf2, buf3, send_sem, recv_sem = scratch
    at = Places()
    meet((*at.sides, at.twin, *at.along_x, *at.along_y, *at.along_z))
    send = Sender(send_sem, recv_sem)
    above, below = at.row > 0, at.row < at.n_row - 1
    before, after = at.col > 0, at.col < at.n_col - 1
    base = at.core * 128
    base_x = base + at.x * 32
    base_y = base_x + at.y * 8

    s0 = send(psum.at[:, pl.ds(128 - base, 128), :], buf0, at.twin)
    rims = []
    for ch in (0, 2):
        rims.append(send(grad.at[ch, :, ABOVE, :], rows_in.at[ch, 1], at.up))
        rims.append(send(grad.at[ch, :, BELOW, :], rows_in.at[ch, 0], at.down))
    rims.append(send(grad.at[1, 0, :, :], cols_in.at[1, 1], at.left))
    rims.append(send(grad.at[1, 3, :, :], cols_in.at[1, 0], at.right))

    s0.wait_recv()
    acc0[...] = psum[:, pl.ds(base, 128), :] + buf0[...]
    s1 = [
        send(acc0.at[:, pl.ds((at.x + d) % 4 * 32, 32), :], buf1.at[d - 1], at.along_x[d - 1])
        for d in (1, 2, 3)
    ]

    arrive(rims)
    for ch in (0, 2):
        acc[ch, :, BOTTOM, :] = grad[ch, :, BOTTOM, :] + jnp.where(below, rows_in[ch, 1], 0.0)
        acc[ch, :, TOP, :] = grad[ch, :, TOP, :] + jnp.where(above, rows_in[ch, 0], 0.0)
    acc[1, 2, :, :] = grad[1, 2, :, :] + jnp.where(after, cols_in[1, 1], 0.0)
    acc[1, 1, :, :] = grad[1, 1, :, :] + jnp.where(before, cols_in[1, 0], 0.0)
    rims = []
    for ch in (0, 2):
        rims.append(send(acc.at[ch, 0, INNER, :], cols_in.at[ch, 1, INNER, :], at.left))
        rims.append(send(acc.at[ch, 3, INNER, :], cols_in.at[ch, 0, INNER, :], at.right))
    rims.append(send(acc.at[1, BOTH, ABOVE, :], rows_in.at[1, 1, BOTH], at.up))
    rims.append(send(acc.at[1, BOTH, BELOW, :], rows_in.at[1, 0, BOTH], at.down))

    arrive(s1)
    acc1[...] = acc0[:, pl.ds(at.x * 32, 32), :] + buf1[0] + buf1[1] + buf1[2]
    s2 = [
        send(acc1.at[:, pl.ds((at.y + d) % 4 * 8, 8), :], buf2.at[d - 1], at.along_y[d - 1])
        for d in (1, 2, 3)
    ]

    arrive(rims)
    for ch in (0, 2):
        acc[ch, 2, INNER, :] += jnp.where(after, cols_in[ch, 1, INNER, :], 0.0)
        acc[ch, 1, INNER, :] += jnp.where(before, cols_in[ch, 0, INNER, :], 0.0)
    acc[1, BOTH, BOTTOM, :] += jnp.where(below, rows_in[1, 1, BOTH], 0.0)
    acc[1, BOTH, TOP, :] += jnp.where(above, rows_in[1, 0, BOTH], 0.0)
    for j in range(2):
        weight = acc[2, 1 + j, TILE, :] + 1.0
        for part in range(2):
            cells = old[part, 1 + j, TILE, :] - acc[part, 1 + j, TILE, :] / weight
            if last:
                new[part, :, 128 * j : 128 * j + 128] = cells
            else:
                new[part, 1 + j, TILE, :] = cells
    if not last:
        halo = halo_first(send, at, new)

    arrive(s2)
    acc2[...] = acc1[:, pl.ds(at.y * 8, 8), :] + buf2[0] + buf2[1] + buf2[2]
    buf3[at.z] = acc2[...]
    s3 = [send(acc2, buf3.at[at.z], at.along_z[d - 1]) for d in (1, 2, 3)]

    if not last:
        arrive(halo)
        halo = halo_second(send, at, new)

    arrive(s3)
    total = buf3[0] + buf3[1] + buf3[2] + buf3[3]
    mine = pl.ds(base_y, 8)
    probe_new[:, mine, :] = probe[:, mine, :] - total[:2] / (total[2:] + 1.0)
    part = probe_new.at[:, mine, :]
    arrive([send(part, part, peer) for peer in at.along_y])
    part = probe_new.at[:, pl.ds(base_x, 32), :]
    arrive([send(part, part, peer) for peer in at.along_x])
    part = probe_new.at[:, pl.ds(base, 128), :]
    arrive([send(part, part, at.twin)])
    if not last:
        arrive(halo)
    send.close()
    if not last:
        clear_outside(at, new)


VMEM = pl.BlockSpec(memory_space=pltpu.VMEM)
SMEM = pl.BlockSpec(memory_space=pltpu.SMEM)
LIMIT = 48 * 2**20


def open_halo(cells):
    return pl.pallas_call(
        open_kernel,
        out_shape=jax.ShapeDtypeStruct((2, 4, 2 * F, 128), f32),
        in_specs=[VMEM],
        out_specs=VMEM,
        scratch_shapes=[pltpu.SemaphoreType.DMA((8,)), pltpu.SemaphoreType.DMA((8,))],
        compiler_params=pltpu.CompilerParams(
            collective_id=0, has_side_effects=True, vmem_limit_bytes=LIMIT
        ),
    )(cells)


def step(last, grad, psum, old, probe):
    shape = (2, F, F) if last else (2, 4, 2 * F, 128)
    copies = 29 if last else 37
    return pl.pallas_call(
        functools.partial(step_kernel, last),
        out_shape=(jax.ShapeDtypeStruct(shape, f32), jax.ShapeDtypeStruct((2, F, F), f32)),
        in_specs=[VMEM] * 4,
        out_specs=(VMEM, VMEM),
        scratch_shapes=[
            pltpu.VMEM((3, 4, 2 * F, 128), f32),
            pltpu.VMEM((3, 2, 4, HALF, 128), f32),
            pltpu.VMEM((3, 2, 2 * F, 128), f32),
            pltpu.VMEM((3, 128, F), f32),
            pltpu.VMEM((3, 128, F), f32),
            pltpu.VMEM((3, 32, F), f32),
            pltpu.VMEM((3, 3, 32, F), f32),
            pltpu.VMEM((3, 8, F), f32),
            pltpu.VMEM((3, 3, 8, F), f32),
            pltpu.VMEM((4, 3, 8, F), f32),
            pltpu.SemaphoreType.DMA((copies,)),
            pltpu.SemaphoreType.DMA((copies,)),
        ],
        compiler_params=pltpu.CompilerParams(
            collective_id=2 if last else 1, has_side_effects=True, vmem_limit_bytes=LIMIT
        ),
    )(grad, psum, old, probe)


def body(positions, counts, amplitudes, object_field, probe):
    fwd, inv = tables()
    anchor = jnp.stack([lax.axis_index("row") * F - HALF, lax.axis_index("col") * F - HALF])
    corners = positions[0, 0] - anchor[None, :]
    load = counts[0]
    ext = open_halo(object_field)
    for iteration in range(ITERS):
        grad, psum = slots(corners, load, amplitudes[0, 0], ext, probe, fwd, inv)
        ext, probe = step(iteration == ITERS - 1, grad, psum, ext, probe)
    return ext, probe


def solution(mesh):
    return jax.shard_map(
        body,
        mesh=mesh,
        in_specs=(
            P("row", "col", None, None),
            P("row", "col"),
            P("row", "col", None, None, None),
            P(None, "row", "col"),
            P(),
        ),
        out_specs=(P(None, "row", "col"), P()),
        check_vma=False,
    )
```

```python
import functools, math
import numpy as np
import jax, jax.numpy as jnp
from jax import lax
from jax.experimental import pallas as pl
from jax.experimental.pallas import tpu as pltpu
from jax.sharding import PartitionSpec as P

F = 256
ITERS = 2
f32=jnp.float32; bf16=jnp.bfloat16

def tables():
    c=np.arange(F,dtype=np.int32)
    ang=(c[:,None]*c[None,:]%F).astype(np.float32)*np.float32(2*math.pi/F)
    re=(np.cos(ang)/np.float32(16)).astype(np.float32)
    im=(-np.sin(ang)/np.float32(16)).astype(np.float32)
    fwd=np.block([[re,-im],[im,re]]); inv=np.block([[re,im],[-im,re]])
    return jnp.asarray(fwd,bf16), jnp.asarray(inv,bf16)

CH=16
def slots_kernel(corner, load, amp, ext, probe, fwd, inv, grad, psum,
                 patch, cov, exit_s, half_s, miss_s, chi_s):
    grad[...]=jnp.zeros(grad.shape,f32)
    psum[...]=jnp.zeros(psum.shape,f32)
    cov[...]=probe[0]*probe[0]+probe[1]*probe[1]
    lane=lax.broadcasted_iota(jnp.int32,(CH,128),1)
    def slot(k,_):
        r=corner[0,k]-(lax.axis_index("row")*F-F//2)
        c=corner[1,k]-(lax.axis_index("col")*F-F//2)
        q=c//128; s=c-q*128
        back=jnp.where(s==0,0,128-s)
        keep=lane<128-s
        for i in range(F//CH):
            rows=pl.ds(i*CH,CH)
            got=[]
            for ch in range(2):
                t=[pltpu.roll(ext[ch,q+j,pl.ds(r+i*CH,CH),:],back,1) for j in range(3)]
                got.append(jnp.concatenate([jnp.where(keep,t[0],t[1]),jnp.where(keep,t[1],t[2])],1))
            re,im=got
            patch[0,rows,:]=re; patch[1,rows,:]=im
            pr=probe[0,rows,:]; pi=probe[1,rows,:]
            exit_s[rows,:]=(pr*re-pi*im).astype(bf16)
            exit_s[pl.ds(F+i*CH,CH),:]=(pr*im+pi*re).astype(bf16)
            psum[2,rows,:]+=re*re+im*im
        half=jnp.dot(fwd[...],exit_s[...],preferred_element_type=f32).astype(bf16)
        half_s[:,:F]=half[:F]; half_s[:,F:]=half[F:]
        far=jnp.dot(half_s[...],inv[...],preferred_element_type=f32)
        fr=far[:,:F]; fi=far[:,F:]
        ratio=1.0-amp[k].astype(f32)*lax.rsqrt(fr*fr+fi*fi+1.0)
        miss_s[:F,:]=(fr*ratio).astype(bf16)
        miss_s[F:,:]=(fi*ratio).astype(bf16)
        back_=jnp.dot(inv[...],miss_s[...],preferred_element_type=f32).astype(bf16)
        half_s[:,:F]=back_[:F]; half_s[:,F:]=back_[F:]
        chi_s[...]=jnp.dot(half_s[...],fwd[...],preferred_element_type=f32)
        put=lane>=s
        for i in range(F//CH):
            rows=pl.ds(i*CH,CH)
            cr=chi_s[rows,:F]; ci=chi_s[rows,F:]
            pr=probe[0,rows,:]; pi=probe[1,rows,:]
            re=patch[0,rows,:]; im=patch[1,rows,:]
            psum[0,rows,:]+=re*cr+im*ci
            psum[1,rows,:]+=re*ci-im*cr
            for ch,u in ((0,pr*cr+pi*ci),(1,pr*ci-pi*cr),(2,cov[rows,:])):
                u0=pltpu.roll(u[:,:128],s,1); u1=pltpu.roll(u[:,128:],s,1)
                at=pl.ds(r+i*CH,CH)
                grad[ch,q,at,:]+=jnp.where(put,u0,0.0)
                grad[ch,q+1,at,:]+=jnp.where(put,u1,u0)
                grad[ch,q+2,at,:]+=jnp.where(put,0.0,u1)
        return 0
    lax.fori_loop(0,load[0],slot,0)

def slots(corner,load,amp,ext,probe,fwd,inv):
    V=pl.BlockSpec(memory_space=pltpu.VMEM); S=pl.BlockSpec(memory_space=pltpu.SMEM)
    return pl.pallas_call(slots_kernel,
        out_shape=(jax.ShapeDtypeStruct((3,4,512,128),f32),jax.ShapeDtypeStruct((3,F,F),f32)),
        in_specs=[S,S,V,V,V,V,V], out_specs=(V,V),
        scratch_shapes=[pltpu.VMEM((2,F,F),f32),pltpu.VMEM((F,F),f32),pltpu.VMEM((2*F,F),bf16),
            pltpu.VMEM((F,2*F),bf16),pltpu.VMEM((2*F,F),bf16),pltpu.VMEM((F,2*F),f32)],
        compiler_params=pltpu.CompilerParams(vmem_limit_bytes=24*2**20),
    )(corner,load,amp,ext,probe,fwd,inv)
MESH = pl.DeviceIdType.MESH
HALF = F // 2
TILE = slice(HALF, HALF + F)


class Places:
    def __init__(self):
        row, col = lax.axis_index("row"), lax.axis_index("col")
        n_row, n_col = lax.axis_size("row"), lax.axis_size("col")
        self.row, self.col, self.n_row, self.n_col = row, col, n_row, n_col
        z_lo, self.y = row // 4, row % 4
        self.x, z_hi, self.core = col // 4, col // 2 % 2, col % 2
        self.z = z_hi * 2 + z_lo
        self.up, self.down = ((row + n_row - 1) % n_row, col), ((row + 1) % n_row, col)
        self.left, self.right = (row, (col + n_col - 1) % n_col), (row, (col + 1) % n_col)
        north, south = self.up[0], self.down[0]
        west, east = self.left[1], self.right[1]
        self.around = (
            self.up, self.down, self.left, self.right,
            (north, west), (north, east), (south, west), (south, east),
        )
        self.twin = (row, col + 1 - 2 * self.core)
        self.along_x = [(row, (self.x + d) % 4 * 4 + col % 4) for d in (1, 2, 3)]
        self.along_y = [(z_lo * 4 + (self.y + d) % 4, col) for d in (1, 2, 3)]
        self.along_z = []
        for d in (1, 2, 3):
            z = (self.z + d) % 4
            self.along_z.append((z % 2 * 4 + self.y, self.x * 4 + z // 2 * 2 + self.core))


def meet(peers):
    barrier = pltpu.get_barrier_semaphore()
    for peer in peers:
        pl.semaphore_signal(barrier, inc=1, device_id=peer, device_id_type=MESH)
    pl.semaphore_wait(barrier, len(peers))


class Sender:
    def __init__(self, send_sem, recv_sem):
        self.send_sem, self.recv_sem, self.used = send_sem, recv_sem, 0
        self.open = []

    def __call__(self, src, dst, peer):
        copy = pltpu.make_async_remote_copy(
            src_ref=src,
            dst_ref=dst,
            send_sem=self.send_sem.at[self.used],
            recv_sem=self.recv_sem.at[self.used],
            device_id=peer,
            device_id_type=MESH,
        )
        self.used += 1
        copy.start()
        self.open.append(copy)
        return copy

    def close(self):
        for copy in self.open:
            copy.wait_send()


def arrive(copies):
    for copy in copies:
        copy.wait_recv()


TOP, BOTTOM = pl.ds(HALF, HALF), pl.ds(F, HALF)
ABOVE, BELOW = pl.ds(0, HALF), pl.ds(F + HALF, HALF)
INNER = pl.ds(HALF, F)
WEST, EAST = pl.ds(0, 1), pl.ds(3, 1)
FIRST, SECOND, BOTH = pl.ds(1, 1), pl.ds(2, 1), pl.ds(1, 2)
OUTSIDE = (
    (BOTH, ABOVE), (BOTH, BELOW), (WEST, INNER), (EAST, INNER),
    (WEST, ABOVE), (EAST, ABOVE), (WEST, BELOW), (EAST, BELOW),
)
INSIDE = (
    (BOTH, TOP), (BOTH, BOTTOM), (FIRST, INNER), (SECOND, INNER),
    (FIRST, TOP), (SECOND, TOP), (FIRST, BOTTOM), (SECOND, BOTTOM),
)
OPPOSITE = (1, 0, 3, 2, 7, 6, 5, 4)


def send_halo(send, at, ext):
    copies = []
    for k, peer in enumerate(at.around):
        tiles, rows = INSIDE[k]
        there, below = OUTSIDE[OPPOSITE[k]]
        copies.append(send(ext.at[:, tiles, rows, :], ext.at[:, there, below, :], peer))
    return copies


def clear_outside(at, ext):
    @pl.when(at.row == 0)
    def _():
        ext[:, :, :HALF, :] = jnp.zeros((2, 4, HALF, 128), f32)

    @pl.when(at.row == at.n_row - 1)
    def _():
        ext[:, :, F + HALF :, :] = jnp.zeros((2, 4, HALF, 128), f32)

    @pl.when(at.col == 0)
    def _():
        ext[:, 0, :, :] = jnp.zeros((2, 2 * F, 128), f32)

    @pl.when(at.col == at.n_col - 1)
    def _():
        ext[:, 3, :, :] = jnp.zeros((2, 2 * F, 128), f32)


def open_kernel(cells, ext, send_sem, recv_sem):
    at = Places()
    meet(at.around)
    for part in range(2):
        for j in range(2):
            ext[part, 1 + j, TILE, :] = cells[part, :, 128 * j : 128 * j + 128]
    send = Sender(send_sem, recv_sem)
    arrive(send_halo(send, at, ext))
    send.close()
    clear_outside(at, ext)


def step_kernel(last, grad, psum, old, probe, new, probe_new, *scratch):
    rims_in, (acc0, buf0, acc1, buf1, acc2, buf2, buf3, send_sem, recv_sem) = scratch[:8], scratch[8:]
    at = Places()
    meet((*at.around, at.twin, *at.along_x, *at.along_y, *at.along_z))
    send = Sender(send_sem, recv_sem)
    above, below = at.row > 0, at.row < at.n_row - 1
    before, after = at.col > 0, at.col < at.n_col - 1
    base = at.core * 128
    base_x = base + at.x * 32
    base_y = base_x + at.y * 8

    s0 = send(psum.at[:, pl.ds(128 - base, 128), :], buf0, at.twin)
    rims = []
    for k, peer in enumerate(at.around):
        tiles, rows = OUTSIDE[k]
        rims.append(send(grad.at[:, tiles, rows, :], rims_in[OPPOSITE[k]], peer))

    s0.wait_recv()
    acc0[...] = psum[:, pl.ds(base, 128), :] + buf0[...]
    s1 = [
        send(acc0.at[:, pl.ds((at.x + d) % 4 * 32, 32), :], buf1.at[d - 1], at.along_x[d - 1])
        for d in (1, 2, 3)
    ]
    arrive(s1)
    acc1[...] = acc0[:, pl.ds(at.x * 32, 32), :] + buf1[0] + buf1[1] + buf1[2]
    s2 = [
        send(acc1.at[:, pl.ds((at.y + d) % 4 * 8, 8), :], buf2.at[d - 1], at.along_y[d - 1])
        for d in (1, 2, 3)
    ]
    arrive(s2)
    acc2[...] = acc1[:, pl.ds(at.y * 8, 8), :] + buf2[0] + buf2[1] + buf2[2]
    buf3[at.z] = acc2[...]
    s3 = [send(acc2, buf3.at[at.z], at.along_z[d - 1]) for d in (1, 2, 3)]

    def finish_object():
        arrive(rims)
        for j, (side, near) in enumerate(((before, 2), (after, 3))):
            for half, (level, over, corner) in enumerate(
                ((above, 0, 4 + j), (below, 1, 6 + j))
            ):
                rows = pl.ds(HALF * half, HALF)
                sums = []
                for ch in range(3):
                    sums.append(
                        grad[ch, 1 + j, pl.ds(HALF + HALF * half, HALF), :]
                        + jnp.where(level, rims_in[over][ch, j], 0.0)
                        + jnp.where(side, rims_in[near][ch, 0, rows, :], 0.0)
                        + jnp.where(side & level, rims_in[corner][ch, 0], 0.0)
                    )
                weight = sums[2] + 1.0
                for part in range(2):
                    place = pl.ds(HALF + HALF * half, HALF)
                    cells = old[part, 1 + j, place, :] - sums[part] / weight
                    if last:
                        new[part, rows, 128 * j : 128 * j + 128] = cells
                    else:
                        new[part, 1 + j, place, :] = cells

    if not last:
        finish_object()
        halo = send_halo(send, at, new)
    arrive(s3)
    total = buf3[0] + buf3[1] + buf3[2] + buf3[3]
    mine = pl.ds(base_y, 8)
    probe_new[:, mine, :] = probe[:, mine, :] - total[:2] / (total[2:] + 1.0)
    part = probe_new.at[:, mine, :]
    arrive([send(part, part, peer) for peer in at.along_y])
    part = probe_new.at[:, pl.ds(base_x, 32), :]
    s5 = [send(part, part, peer) for peer in at.along_x]
    if last:
        finish_object()
    arrive(s5)
    part = probe_new.at[:, pl.ds(base, 128), :]
    arrive([send(part, part, at.twin)])
    if not last:
        arrive(halo)
    send.close()
    if not last:
        clear_outside(at, new)


VMEM = pl.BlockSpec(memory_space=pltpu.VMEM)
SMEM = pl.BlockSpec(memory_space=pltpu.SMEM)
LIMIT = 20 * 2**20


def open_halo(cells):
    return pl.pallas_call(
        open_kernel,
        out_shape=jax.ShapeDtypeStruct((2, 4, 2 * F, 128), f32),
        in_specs=[VMEM],
        out_specs=VMEM,
        scratch_shapes=[pltpu.SemaphoreType.DMA((8,)), pltpu.SemaphoreType.DMA((8,))],
        compiler_params=pltpu.CompilerParams(
            collective_id=0, has_side_effects=True, vmem_limit_bytes=LIMIT
        ),
    )(cells)


def step(last, grad, psum, old, probe):
    shape = (2, F, F) if last else (2, 4, 2 * F, 128)
    copies = 25 if last else 33
    return pl.pallas_call(
        functools.partial(step_kernel, last),
        out_shape=(jax.ShapeDtypeStruct(shape, f32), jax.ShapeDtypeStruct((2, F, F), f32)),
        in_specs=[VMEM] * 4,
        out_specs=(VMEM, VMEM),
        scratch_shapes=[
            *(pltpu.VMEM((3, 2, HALF, 128), f32) for _ in range(2)),
            *(pltpu.VMEM((3, 1, F, 128), f32) for _ in range(2)),
            *(pltpu.VMEM((3, 1, HALF, 128), f32) for _ in range(4)),
            pltpu.VMEM((3, 128, F), f32),
            pltpu.VMEM((3, 128, F), f32),
            pltpu.VMEM((3, 32, F), f32),
            pltpu.VMEM((3, 3, 32, F), f32),
            pltpu.VMEM((3, 8, F), f32),
            pltpu.VMEM((3, 3, 8, F), f32),
            pltpu.VMEM((4, 3, 8, F), f32),
            pltpu.SemaphoreType.DMA((copies,)),
            pltpu.SemaphoreType.DMA((copies,)),
        ],
        compiler_params=pltpu.CompilerParams(
            collective_id=2 if last else 1, has_side_effects=True, vmem_limit_bytes=LIMIT
        ),
    )(grad, psum, old, probe)


def body(positions, counts, amplitudes, object_field, probe):
    fwd, inv = tables()
    corners = positions[0, 0].T
    load = counts[0]
    ext = open_halo(object_field)
    for iteration in range(ITERS):
        grad, psum = slots(corners, load, amplitudes[0, 0], ext, probe, fwd, inv)
        ext, probe = step(iteration == ITERS - 1, grad, psum, ext, probe)
    return ext, probe


def solution(mesh):
    return jax.shard_map(
        body,
        mesh=mesh,
        in_specs=(
            P("row", "col", None, None),
            P("row", "col"),
            P("row", "col", None, None, None),
            P(None, "row", "col"),
            P(),
        ),
        out_specs=(P(None, "row", "col"), P()),
        check_vma=False,
    )
```

```python
import functools, math
import numpy as np
import jax, jax.numpy as jnp
from jax import lax
from jax.experimental import pallas as pl
from jax.experimental.pallas import tpu as pltpu
from jax.sharding import PartitionSpec as P

F = 256
ITERS = 2
f32=jnp.float32; bf16=jnp.bfloat16

def tables():
    c=np.arange(F,dtype=np.int32)
    ang=(c[:,None]*c[None,:]%F).astype(np.float32)*np.float32(2*math.pi/F)
    re=(np.cos(ang)/np.float32(16)).astype(np.float32)
    im=(-np.sin(ang)/np.float32(16)).astype(np.float32)
    fwd=np.block([[re,-im],[im,re]]); inv=np.block([[re,im],[-im,re]])
    return jnp.asarray(fwd,bf16), jnp.asarray(inv,bf16)

CH=16; B=2; ROWS=3*F
def both_sides(table, other, cells):
    re = jnp.dot(table[:F, :], cells[...], preferred_element_type=f32).astype(bf16)
    im = jnp.dot(table[F:, :], cells[...], preferred_element_type=f32).astype(bf16)
    stacked = jnp.concatenate(
        [jnp.concatenate([re[:, F * b : F * b + F], im[:, F * b : F * b + F]], 1) for b in range(B)], 0
    )
    return jnp.dot(stacked, other[...], preferred_element_type=f32)


def slots_kernel(corner, load, amp, ext, probe, fwd, inv, grad, psum,
                 patch0, patch1, cov, exit_s, miss0, miss1, chi_s):
    lane=lax.broadcasted_iota(jnp.int32,(CH,128),1)
    n=load[0]
    top=lax.axis_index("row")*F-F//2; left=lax.axis_index("col")*F-F//2
    def place(k):
        kk=jnp.minimum(k,15)
        live=k<n
        r=jnp.where(live,corner[0,kk]-top,2*F); c=jnp.where(live,corner[1,kk]-left,0)
        q=c//128; s=c-q*128
        return r,q,s,kk
    def front(g,patch,miss):
        for b in range(B):
            r,q,s,kk=place(B*g+b)
            back=jnp.where(s==0,0,128-s)
            keep=lane<128-s
            for i in range(F//CH):
                rows=pl.ds(i*CH,CH)
                got=[]
                for ch in range(2):
                    t=[pltpu.roll(ext[ch,q+j,pl.ds(r+i*CH,CH),:],back,1) for j in range(3)]
                    got.append(jnp.concatenate([jnp.where(keep,t[0],t[1]),jnp.where(keep,t[1],t[2])],1))
                re,im=got
                patch[b,0,rows,:]=re; patch[b,1,rows,:]=im
                pr=probe[0,rows,:]; pi=probe[1,rows,:]
                exit_s[rows,F*b:F*b+F]=(pr*re-pi*im).astype(bf16)
                exit_s[pl.ds(F+i*CH,CH),F*b:F*b+F]=(pr*im+pi*re).astype(bf16)
        far=both_sides(fwd,inv,exit_s)
        for b in range(B):
            kk=jnp.minimum(B*g+b,15)
            fr=far[F*b:F*b+F,:F]; fi=far[F*b:F*b+F,F:]
            ratio=1.0-amp[kk].astype(f32)*lax.rsqrt(fr*fr+fi*fi+1.0)
            miss[:F,F*b:F*b+F]=(fr*ratio).astype(bf16)
            miss[F:,F*b:F*b+F]=(fi*ratio).astype(bf16)
    def back_(g,patch,miss):
        chi=both_sides(inv,fwd,miss)
        chi_s[...]=chi
        for i in range(F//CH):
            rows=pl.ds(i*CH,CH)
            pr=probe[0,rows,:]; pi=probe[1,rows,:]
            p0=p1=p2=0.0
            for b in range(B):
                at_=pl.ds(F*b+i*CH,CH)
                cr=chi_s[at_,:F]; ci=chi_s[at_,F:]
                re=patch[b,0,rows,:]; im=patch[b,1,rows,:]
                p0+=re*cr+im*ci; p1+=re*ci-im*cr; p2+=re*re+im*im
            psum[0,rows,:]+=p0; psum[1,rows,:]+=p1; psum[2,rows,:]+=p2
        for b in range(B):
            r,q,s,kk=place(B*g+b)
            put=lane>=s
            for i in range(F//CH):
                rows=pl.ds(i*CH,CH); at_=pl.ds(F*b+i*CH,CH)
                cr=chi_s[at_,:F]; ci=chi_s[at_,F:]
                pr=probe[0,rows,:]; pi=probe[1,rows,:]
                for ch,u in ((0,pr*cr+pi*ci),(1,pr*ci-pi*cr),(2,cov[rows,:])):
                    u0=pltpu.roll(u[:,:128],s,1); u1=pltpu.roll(u[:,128:],s,1)
                    at=pl.ds(r+i*CH,CH)
                    grad[ch,q,at,:]+=jnp.where(put,u0,0.0)
                    grad[ch,q+1,at,:]+=jnp.where(put,u1,u0)
                    grad[ch,q+2,at,:]+=jnp.where(put,0.0,u1)
    for ch in range(3):
        for j in range(4):
            grad[ch,j,:2*F,:]=jnp.zeros((2*F,128),f32)
    psum[...]=jnp.zeros(psum.shape,f32)
    cov[...]=probe[0]*probe[0]+probe[1]*probe[1]
    front(0,patch0,miss0)
    pairs=(n+2*B-1)//(2*B)
    def it(j,_):
        back_(2*j,patch0,miss0)
        front(2*j+1,patch1,miss1)
        back_(2*j+1,patch1,miss1)
        front(2*j+2,patch0,miss0)
        return 0
    lax.fori_loop(0,pairs,it,0)
def slots(corner,load,amp,ext,probe,fwd,inv):
    V=pl.BlockSpec(memory_space=pltpu.VMEM); S=pl.BlockSpec(memory_space=pltpu.SMEM)
    return pl.pallas_call(slots_kernel,
        out_shape=(jax.ShapeDtypeStruct((3,4,ROWS,128),f32),jax.ShapeDtypeStruct((3,F,F),f32)),
        in_specs=[S,S,V,V,V,V,V], out_specs=(V,V),
        scratch_shapes=[pltpu.VMEM((B,2,F,F),f32),pltpu.VMEM((B,2,F,F),f32),pltpu.VMEM((F,F),f32),pltpu.VMEM((2*F,B*F),bf16),
            pltpu.VMEM((2*F,B*F),bf16),pltpu.VMEM((2*F,B*F),bf16),pltpu.VMEM((B*F,2*F),f32)],
        compiler_params=pltpu.CompilerParams(vmem_limit_bytes=24*2**20),
    )(corner,load,amp,ext,probe,fwd,inv)


MESH = pl.DeviceIdType.MESH
HALF = F // 2
TILE = slice(HALF, HALF + F)


class Places:
    def __init__(self):
        row, col = lax.axis_index("row"), lax.axis_index("col")
        n_row, n_col = lax.axis_size("row"), lax.axis_size("col")
        self.row, self.col, self.n_row, self.n_col = row, col, n_row, n_col
        z_lo, self.y = row // 4, row % 4
        self.x, z_hi, self.core = col // 4, col // 2 % 2, col % 2
        self.z = z_hi * 2 + z_lo
        self.up, self.down = ((row + n_row - 1) % n_row, col), ((row + 1) % n_row, col)
        self.left, self.right = (row, (col + n_col - 1) % n_col), (row, (col + 1) % n_col)
        north, south = self.up[0], self.down[0]
        west, east = self.left[1], self.right[1]
        self.around = (
            self.up, self.down, self.left, self.right,
            (north, west), (north, east), (south, west), (south, east),
        )
        self.twin = (row, col + 1 - 2 * self.core)
        self.along_x = [(row, (self.x + d) % 4 * 4 + col % 4) for d in (1, 2, 3)]
        self.along_y = [(z_lo * 4 + (self.y + d) % 4, col) for d in (1, 2, 3)]
        self.along_z = []
        for d in (1, 2, 3):
            z = (self.z + d) % 4
            self.along_z.append((z % 2 * 4 + self.y, self.x * 4 + z // 2 * 2 + self.core))


def meet(peers):
    barrier = pltpu.get_barrier_semaphore()
    for peer in peers:
        pl.semaphore_signal(barrier, inc=1, device_id=peer, device_id_type=MESH)
    pl.semaphore_wait(barrier, len(peers))


class Sender:
    def __init__(self, send_sem, recv_sem):
        self.send_sem, self.recv_sem, self.used = send_sem, recv_sem, 0
        self.open = []

    def __call__(self, src, dst, peer):
        copy = pltpu.make_async_remote_copy(
            src_ref=src,
            dst_ref=dst,
            send_sem=self.send_sem.at[self.used],
            recv_sem=self.recv_sem.at[self.used],
            device_id=peer,
            device_id_type=MESH,
        )
        self.used += 1
        copy.start()
        self.open.append(copy)
        return copy

    def close(self):
        for copy in self.open:
            copy.wait_send()


def arrive(copies):
    for copy in copies:
        copy.wait_recv()


TOP, BOTTOM = pl.ds(HALF, HALF), pl.ds(F, HALF)
ABOVE, BELOW = pl.ds(0, HALF), pl.ds(F + HALF, HALF)
INNER = pl.ds(HALF, F)
WEST, EAST = pl.ds(0, 1), pl.ds(3, 1)
FIRST, SECOND, BOTH = pl.ds(1, 1), pl.ds(2, 1), pl.ds(1, 2)
OUTSIDE = (
    (BOTH, ABOVE), (BOTH, BELOW), (WEST, INNER), (EAST, INNER),
    (WEST, ABOVE), (EAST, ABOVE), (WEST, BELOW), (EAST, BELOW),
)
INSIDE = (
    (BOTH, TOP), (BOTH, BOTTOM), (FIRST, INNER), (SECOND, INNER),
    (FIRST, TOP), (SECOND, TOP), (FIRST, BOTTOM), (SECOND, BOTTOM),
)
OPPOSITE = (1, 0, 3, 2, 7, 6, 5, 4)


def send_halo(send, at, ext):
    copies = []
    for k, peer in enumerate(at.around):
        tiles, rows = INSIDE[k]
        there, below = OUTSIDE[OPPOSITE[k]]
        copies.append(send(ext.at[:, tiles, rows, :], ext.at[:, there, below, :], peer))
    return copies


def clear_outside(at, ext):
    ext[:, :, 2 * F :, :] = jnp.zeros((2, 4, ROWS - 2 * F, 128), f32)

    @pl.when(at.row == 0)
    def _():
        ext[:, :, :HALF, :] = jnp.zeros((2, 4, HALF, 128), f32)

    @pl.when(at.row == at.n_row - 1)
    def _():
        ext[:, :, F + HALF : 2 * F, :] = jnp.zeros((2, 4, HALF, 128), f32)

    @pl.when(at.col == 0)
    def _():
        ext[:, 0, : 2 * F, :] = jnp.zeros((2, 2 * F, 128), f32)

    @pl.when(at.col == at.n_col - 1)
    def _():
        ext[:, 3, : 2 * F, :] = jnp.zeros((2, 2 * F, 128), f32)


def open_kernel(cells, ext, send_sem, recv_sem):
    at = Places()
    meet(at.around)
    for part in range(2):
        for j in range(2):
            ext[part, 1 + j, TILE, :] = cells[part, :, 128 * j : 128 * j + 128]
    send = Sender(send_sem, recv_sem)
    arrive(send_halo(send, at, ext))
    send.close()
    clear_outside(at, ext)


def step_kernel(last, grad, psum, old, probe, new, probe_new, *scratch):
    rims_in, (acc0, buf0, acc1, buf1, acc2, buf2, buf3, send_sem, recv_sem) = scratch[:8], scratch[8:]
    at = Places()
    meet((*at.around, at.twin, *at.along_x, *at.along_y, *at.along_z))
    send = Sender(send_sem, recv_sem)
    above, below = at.row > 0, at.row < at.n_row - 1
    before, after = at.col > 0, at.col < at.n_col - 1
    base = at.core * 128
    base_x = base + at.x * 32
    base_y = base_x + at.y * 8

    s0 = send(psum.at[:, pl.ds(128 - base, 128), :], buf0, at.twin)
    rims = []
    for k, peer in enumerate(at.around):
        tiles, rows = OUTSIDE[k]
        rims.append(send(grad.at[:, tiles, rows, :], rims_in[OPPOSITE[k]], peer))

    s0.wait_recv()
    acc0[...] = psum[:, pl.ds(base, 128), :] + buf0[...]
    s1 = [
        send(acc0.at[:, pl.ds((at.x + d) % 4 * 32, 32), :], buf1.at[d - 1], at.along_x[d - 1])
        for d in (1, 2, 3)
    ]
    arrive(s1)
    acc1[...] = acc0[:, pl.ds(at.x * 32, 32), :] + buf1[0] + buf1[1] + buf1[2]
    s2 = [
        send(acc1.at[:, pl.ds((at.y + d) % 4 * 8, 8), :], buf2.at[d - 1], at.along_y[d - 1])
        for d in (1, 2, 3)
    ]
    arrive(s2)
    acc2[...] = acc1[:, pl.ds(at.y * 8, 8), :] + buf2[0] + buf2[1] + buf2[2]
    buf3[at.z] = acc2[...]
    s3 = [send(acc2, buf3.at[at.z], at.along_z[d - 1]) for d in (1, 2, 3)]

    def finish_object():
        arrive(rims)
        for j, (side, near) in enumerate(((before, 2), (after, 3))):
            for half, (level, over, corner) in enumerate(
                ((above, 0, 4 + j), (below, 1, 6 + j))
            ):
                rows = pl.ds(HALF * half, HALF)
                sums = []
                for ch in range(3):
                    sums.append(
                        grad[ch, 1 + j, pl.ds(HALF + HALF * half, HALF), :]
                        + jnp.where(level, rims_in[over][ch, j], 0.0)
                        + jnp.where(side, rims_in[near][ch, 0, rows, :], 0.0)
                        + jnp.where(side & level, rims_in[corner][ch, 0], 0.0)
                    )
                weight = sums[2] + 1.0
                for part in range(2):
                    place = pl.ds(HALF + HALF * half, HALF)
                    cells = old[part, 1 + j, place, :] - sums[part] / weight
                    if last:
                        new[part, rows, 128 * j : 128 * j + 128] = cells
                    else:
                        new[part, 1 + j, place, :] = cells

    if not last:
        finish_object()
        halo = send_halo(send, at, new)
    arrive(s3)
    total = buf3[0] + buf3[1] + buf3[2] + buf3[3]
    mine = pl.ds(base_y, 8)
    probe_new[:, mine, :] = probe[:, mine, :] - total[:2] / (total[2:] + 1.0)
    part = probe_new.at[:, mine, :]
    arrive([send(part, part, peer) for peer in at.along_y])
    part = probe_new.at[:, pl.ds(base_x, 32), :]
    s5 = [send(part, part, peer) for peer in at.along_x]
    if last:
        finish_object()
    arrive(s5)
    part = probe_new.at[:, pl.ds(base, 128), :]
    arrive([send(part, part, at.twin)])
    if not last:
        arrive(halo)
    send.close()
    if not last:
        clear_outside(at, new)


VMEM = pl.BlockSpec(memory_space=pltpu.VMEM)
SMEM = pl.BlockSpec(memory_space=pltpu.SMEM)
LIMIT = 20 * 2**20


def open_halo(cells):
    return pl.pallas_call(
        open_kernel,
        out_shape=jax.ShapeDtypeStruct((2, 4, ROWS, 128), f32),
        in_specs=[VMEM],
        out_specs=VMEM,
        scratch_shapes=[pltpu.SemaphoreType.DMA((8,)), pltpu.SemaphoreType.DMA((8,))],
        compiler_params=pltpu.CompilerParams(
            collective_id=0, has_side_effects=True, vmem_limit_bytes=LIMIT
        ),
    )(cells)


def step(last, grad, psum, old, probe):
    shape = (2, F, F) if last else (2, 4, ROWS, 128)
    copies = 25 if last else 33
    return pl.pallas_call(
        functools.partial(step_kernel, last),
        out_shape=(jax.ShapeDtypeStruct(shape, f32), jax.ShapeDtypeStruct((2, F, F), f32)),
        in_specs=[VMEM] * 4,
        out_specs=(VMEM, VMEM),
        scratch_shapes=[
            *(pltpu.VMEM((3, 2, HALF, 128), f32) for _ in range(2)),
            *(pltpu.VMEM((3, 1, F, 128), f32) for _ in range(2)),
            *(pltpu.VMEM((3, 1, HALF, 128), f32) for _ in range(4)),
            pltpu.VMEM((3, 128, F), f32),
            pltpu.VMEM((3, 128, F), f32),
            pltpu.VMEM((3, 32, F), f32),
            pltpu.VMEM((3, 3, 32, F), f32),
            pltpu.VMEM((3, 8, F), f32),
            pltpu.VMEM((3, 3, 8, F), f32),
            pltpu.VMEM((4, 3, 8, F), f32),
            pltpu.SemaphoreType.DMA((copies,)),
            pltpu.SemaphoreType.DMA((copies,)),
        ],
        compiler_params=pltpu.CompilerParams(
            collective_id=2 if last else 1, has_side_effects=True, vmem_limit_bytes=LIMIT
        ),
    )(grad, psum, old, probe)


def body(positions, counts, amplitudes, object_field, probe):
    fwd, inv = tables()
    corners = positions[0, 0].T
    load = counts[0]
    ext = open_halo(object_field)
    for iteration in range(ITERS):
        grad, psum = slots(corners, load, amplitudes[0, 0], ext, probe, fwd, inv)
        ext, probe = step(iteration == ITERS - 1, grad, psum, ext, probe)
    return ext, probe


def solution(mesh):
    return jax.shard_map(
        body,
        mesh=mesh,
        in_specs=(
            P("row", "col", None, None),
            P("row", "col"),
            P("row", "col", None, None, None),
            P(None, "row", "col"),
            P(),
        ),
        out_specs=(P(None, "row", "col"), P()),
        check_vma=False,
    )
```

```python
import functools, math
import numpy as np
import jax, jax.numpy as jnp
from jax import lax
from jax.experimental import pallas as pl
from jax.experimental.pallas import tpu as pltpu
from jax.sharding import PartitionSpec as P

F = 256
ITERS = 2
f32=jnp.float32; bf16=jnp.bfloat16

def tables():
    c=np.arange(F,dtype=np.int32)
    ang=(c[:,None]*c[None,:]%F).astype(np.float32)*np.float32(2*math.pi/F)
    re=(np.cos(ang)/np.float32(16)).astype(np.float32)
    im=(-np.sin(ang)/np.float32(16)).astype(np.float32)
    fwd=np.block([[re,-im],[im,re]]); inv=np.block([[re,im],[-im,re]])
    return jnp.asarray(fwd,bf16), jnp.asarray(inv,bf16)

CH=16; B=2; ROWS=3*F
def both_sides(table, other, cells):
    re = jnp.dot(table[:F, :], cells[...], preferred_element_type=f32).astype(bf16)
    im = jnp.dot(table[F:, :], cells[...], preferred_element_type=f32).astype(bf16)
    stacked = jnp.concatenate(
        [jnp.concatenate([re[:, F * b : F * b + F], im[:, F * b : F * b + F]], 1) for b in range(B)], 0
    )
    return jnp.dot(stacked, other[...], preferred_element_type=f32)


def slots_kernel(corner, load, amp, ext, probe, fwd, inv, grad, psum,
                 patch0, patch1, cov, exit_s, miss0, miss1, chi_s):
    lane=lax.broadcasted_iota(jnp.int32,(CH,128),1)
    n=load[0]
    top=lax.axis_index("row")*F-F//2; left=lax.axis_index("col")*F-F//2
    def place(k):
        kk=jnp.minimum(k,15)
        live=k<n
        r=jnp.where(live,corner[0,kk]-top,2*F); c=jnp.where(live,corner[1,kk]-left,0)
        q=c//128; s=c-q*128
        return r,q,s,kk
    def front(g,patch,miss):
        for b in range(B):
            r,q,s,kk=place(B*g+b)
            back=jnp.where(s==0,0,128-s)
            keep=lane<128-s
            for i in range(F//CH):
                rows=pl.ds(i*CH,CH)
                got=[]
                for ch in range(2):
                    t=[pltpu.roll(ext[ch,q+j,pl.ds(r+i*CH,CH),:],back,1) for j in range(3)]
                    got.append(jnp.concatenate([jnp.where(keep,t[0],t[1]),jnp.where(keep,t[1],t[2])],1))
                re,im=got
                patch[b,0,rows,:]=re; patch[b,1,rows,:]=im
                pr=probe[0,rows,:]; pi=probe[1,rows,:]
                exit_s[rows,F*b:F*b+F]=(pr*re-pi*im).astype(bf16)
                exit_s[pl.ds(F+i*CH,CH),F*b:F*b+F]=(pr*im+pi*re).astype(bf16)
        far=both_sides(fwd,inv,exit_s)
        for b in range(B):
            kk=jnp.minimum(B*g+b,15)
            fr=far[F*b:F*b+F,:F]; fi=far[F*b:F*b+F,F:]
            ratio=1.0-amp[kk].astype(f32)*lax.rsqrt(fr*fr+fi*fi+1.0)
            miss[:F,F*b:F*b+F]=(fr*ratio).astype(bf16)
            miss[F:,F*b:F*b+F]=(fi*ratio).astype(bf16)
    def back_(g,patch,miss):
        chi=both_sides(inv,fwd,miss)
        chi_s[...]=chi
        for i in range(F//CH):
            rows=pl.ds(i*CH,CH)
            pr=probe[0,rows,:]; pi=probe[1,rows,:]
            p0=p1=p2=0.0
            for b in range(B):
                at_=pl.ds(F*b+i*CH,CH)
                cr=chi_s[at_,:F]; ci=chi_s[at_,F:]
                re=patch[b,0,rows,:]; im=patch[b,1,rows,:]
                p0+=re*cr+im*ci; p1+=re*ci-im*cr; p2+=re*re+im*im
            psum[0,rows,:]+=p0; psum[1,rows,:]+=p1; psum[2,rows,:]+=p2
        for b in range(B):
            r,q,s,kk=place(B*g+b)
            put=lane>=s
            for i in range(F//CH):
                rows=pl.ds(i*CH,CH); at_=pl.ds(F*b+i*CH,CH)
                cr=chi_s[at_,:F]; ci=chi_s[at_,F:]
                pr=probe[0,rows,:]; pi=probe[1,rows,:]
                for ch,u in ((0,pr*cr+pi*ci),(1,pr*ci-pi*cr),(2,cov[rows,:])):
                    u0=pltpu.roll(u[:,:128],s,1); u1=pltpu.roll(u[:,128:],s,1)
                    at=pl.ds(r+i*CH,CH)
                    grad[ch,q,at,:]+=jnp.where(put,u0,0.0)
                    grad[ch,q+1,at,:]+=jnp.where(put,u1,u0)
                    grad[ch,q+2,at,:]+=jnp.where(put,0.0,u1)
    for ch in range(3):
        for j in range(4):
            grad[ch,j,:2*F,:]=jnp.zeros((2*F,128),f32)
    psum[...]=jnp.zeros(psum.shape,f32)
    cov[...]=probe[0]*probe[0]+probe[1]*probe[1]
    front(0,patch0,miss0)
    pairs=(n+2*B-1)//(2*B)
    def it(j,_):
        back_(2*j,patch0,miss0)
        front(2*j+1,patch1,miss1)
        back_(2*j+1,patch1,miss1)
        front(2*j+2,patch0,miss0)
        return 0
    lax.fori_loop(0,pairs,it,0)
def slots(corner,load,amp,ext,probe,fwd,inv):
    V=pl.BlockSpec(memory_space=pltpu.VMEM); S=pl.BlockSpec(memory_space=pltpu.SMEM)
    return pl.pallas_call(slots_kernel,
        out_shape=(jax.ShapeDtypeStruct((3,4,ROWS,128),f32),jax.ShapeDtypeStruct((3,F,F),f32)),
        in_specs=[S,S,V,V,V,V,V], out_specs=(V,V),
        scratch_shapes=[pltpu.VMEM((B,2,F,F),f32),pltpu.VMEM((B,2,F,F),f32),pltpu.VMEM((F,F),f32),pltpu.VMEM((2*F,B*F),bf16),
            pltpu.VMEM((2*F,B*F),bf16),pltpu.VMEM((2*F,B*F),bf16),pltpu.VMEM((B*F,2*F),f32)],
        compiler_params=pltpu.CompilerParams(vmem_limit_bytes=24*2**20),
    )(corner,load,amp,ext,probe,fwd,inv)


MESH = pl.DeviceIdType.MESH
HALF = F // 2
TILE = slice(HALF, HALF + F)


TOP, BOTTOM = pl.ds(HALF, HALF), pl.ds(F, HALF)
ABOVE, BELOW = pl.ds(0, HALF), pl.ds(F + HALF, HALF)


class Places:
    def __init__(self):
        row, col = lax.axis_index("row"), lax.axis_index("col")
        n_row, n_col = lax.axis_size("row"), lax.axis_size("col")
        self.row, self.col, self.n_row, self.n_col = row, col, n_row, n_col
        z_lo, self.y = row // 4, row % 4
        self.x, z_hi, self.core = col // 4, col // 2 % 2, col % 2
        self.z = z_hi * 2 + z_lo
        self.up, self.down = ((row + n_row - 1) % n_row, col), ((row + 1) % n_row, col)
        self.left, self.right = (row, (col + n_col - 1) % n_col), (row, (col + 1) % n_col)
        north, south = self.up[0], self.down[0]
        west, east = self.left[1], self.right[1]
        self.around = (
            self.up, self.down, self.left, self.right,
            (north, west), (north, east), (south, west), (south, east),
        )
        self.twin = (row, col + 1 - 2 * self.core)
        beside = (col + n_col - 1 + 2 * self.core) % n_col
        inner, outer = 3 - 3 * self.core, 3 * self.core
        self.near_corners = (
            ((north, self.twin[1]), ABOVE, inner, 2 + self.core),
            ((south, self.twin[1]), BELOW, inner, self.core),
        )
        self.far_corners = (
            ((north, beside), ABOVE, outer, 3 - self.core),
            ((south, beside), BELOW, outer, 1 - self.core),
        )
        self.along_x = [(row, (self.x + d) % 4 * 4 + col % 4) for d in (1, 2, 3)]
        self.along_y = [(z_lo * 4 + (self.y + d) % 4, col) for d in (1, 2, 3)]
        self.along_z = []
        for d in (1, 2, 3):
            z = (self.z + d) % 4
            self.along_z.append((z % 2 * 4 + self.y, self.x * 4 + z // 2 * 2 + self.core))


def meet(peers):
    barrier = pltpu.get_barrier_semaphore()
    for peer in peers:
        pl.semaphore_signal(barrier, inc=1, device_id=peer, device_id_type=MESH)
    pl.semaphore_wait(barrier, len(peers))


class Sender:
    def __init__(self, send_sem, recv_sem):
        self.send_sem, self.recv_sem, self.used = send_sem, recv_sem, 0
        self.open = []

    def __call__(self, src, dst, peer):
        copy = pltpu.make_async_remote_copy(
            src_ref=src,
            dst_ref=dst,
            send_sem=self.send_sem.at[self.used],
            recv_sem=self.recv_sem.at[self.used],
            device_id=peer,
            device_id_type=MESH,
        )
        self.used += 1
        copy.start()
        self.open.append(copy)
        return copy

    def close(self):
        for copy in self.open:
            copy.wait_send()


def arrive(copies):
    for copy in copies:
        copy.wait_recv()


INNER = pl.ds(HALF, F)
WEST, EAST = pl.ds(0, 1), pl.ds(3, 1)
FIRST, SECOND, BOTH = pl.ds(1, 1), pl.ds(2, 1), pl.ds(1, 2)
OUTSIDE = (
    (BOTH, ABOVE), (BOTH, BELOW), (WEST, INNER), (EAST, INNER),
    (WEST, ABOVE), (EAST, ABOVE), (WEST, BELOW), (EAST, BELOW),
)
INSIDE = (
    (BOTH, TOP), (BOTH, BOTTOM), (FIRST, INNER), (SECOND, INNER),
    (FIRST, TOP), (SECOND, TOP), (FIRST, BOTTOM), (SECOND, BOTTOM),
)
OPPOSITE = (1, 0, 3, 2, 7, 6, 5, 4)


def send_halo(send, at, ext):
    copies = []
    for k, peer in enumerate(at.around):
        tiles, rows = INSIDE[k]
        there, below = OUTSIDE[OPPOSITE[k]]
        copies.append(send(ext.at[:, tiles, rows, :], ext.at[:, there, below, :], peer))
    return copies


def clear_outside(at, ext):
    ext[:, :, 2 * F :, :] = jnp.zeros((2, 4, ROWS - 2 * F, 128), f32)

    @pl.when(at.row == 0)
    def _():
        ext[:, :, :HALF, :] = jnp.zeros((2, 4, HALF, 128), f32)

    @pl.when(at.row == at.n_row - 1)
    def _():
        ext[:, :, F + HALF : 2 * F, :] = jnp.zeros((2, 4, HALF, 128), f32)

    @pl.when(at.col == 0)
    def _():
        ext[:, 0, : 2 * F, :] = jnp.zeros((2, 2 * F, 128), f32)

    @pl.when(at.col == at.n_col - 1)
    def _():
        ext[:, 3, : 2 * F, :] = jnp.zeros((2, 2 * F, 128), f32)


def open_kernel(cells, ext, send_sem, recv_sem):
    at = Places()
    meet(at.around)
    for part in range(2):
        for j in range(2):
            ext[part, 1 + j, TILE, :] = cells[part, :, 128 * j : 128 * j + 128]
    send = Sender(send_sem, recv_sem)
    arrive(send_halo(send, at, ext))
    send.close()
    clear_outside(at, ext)


def step_kernel(last, grad, psum, old, probe, new, probe_new, *scratch):
    rims_in, corners_in = scratch[:4], scratch[4]
    acc0, buf0, acc1, buf1, acc2, buf2, buf3, send_sem, recv_sem = scratch[5:]
    at = Places()
    meet((*at.around, at.twin, *at.along_x, *at.along_y, *at.along_z))
    send = Sender(send_sem, recv_sem)
    above, below = at.row > 0, at.row < at.n_row - 1
    before, after = at.col > 0, at.col < at.n_col - 1
    base = at.core * 128
    base_y = base + at.y * 32
    base_x = base_y + at.x * 8
    rims = []

    def send_rims(channels, sides):
        for k in sides:
            tiles, rows = OUTSIDE[k]
            there = rims_in[OPPOSITE[k]].at[channels]
            rims.append(send(grad.at[channels, tiles, rows, :], there, at.around[k]))

    def send_corners(corners):
        for peer, rows, tile, there in corners:
            rims.append(send(grad.at[:, pl.ds(tile, 1), rows, :], corners_in.at[there], peer))

    s0 = send(psum.at[:, pl.ds(128 - base, 128), :], buf0, at.twin)
    send_rims(pl.ds(0, 1), (0, 1))
    send_rims(pl.ds(0, 3), (2, 3))
    s0.wait_recv()
    acc0[...] = psum[:, pl.ds(base, 128), :] + buf0[...]
    s1 = [
        send(acc0.at[:, pl.ds((at.y + d) % 4 * 32, 32), :], buf1.at[d - 1], at.along_y[d - 1])
        for d in (1, 2, 3)
    ]
    send_rims(pl.ds(1, 2), (0, 1))
    send_corners(at.near_corners)
    arrive(s1)
    acc1[...] = acc0[:, pl.ds(at.y * 32, 32), :] + buf1[0] + buf1[1] + buf1[2]
    s2 = [
        send(acc1.at[:, pl.ds((at.x + d) % 4 * 8, 8), :], buf2.at[d - 1], at.along_x[d - 1])
        for d in (1, 2, 3)
    ]
    arrive(s2)
    acc2[...] = acc1[:, pl.ds(at.x * 8, 8), :] + buf2[0] + buf2[1] + buf2[2]
    buf3[at.z] = acc2[...]
    s3 = [send(acc2, buf3.at[at.z], at.along_z[d - 1]) for d in (1, 2, 3)]
    send_corners(at.far_corners)

    def finish_object():
        arrive(rims)
        for j, (side, near) in enumerate(((before, 2), (after, 3))):
            for half, (level, over, corner) in enumerate(
                ((above, 0, j), (below, 1, 2 + j))
            ):
                rows = pl.ds(HALF * half, HALF)
                sums = []
                for ch in range(3):
                    sums.append(
                        grad[ch, 1 + j, pl.ds(HALF + HALF * half, HALF), :]
                        + jnp.where(level, rims_in[over][ch, j], 0.0)
                        + jnp.where(side, rims_in[near][ch, 0, rows, :], 0.0)
                        + jnp.where(side & level, corners_in[corner, ch, 0], 0.0)
                    )
                weight = sums[2] + 1.0
                for part in range(2):
                    place = pl.ds(HALF + HALF * half, HALF)
                    cells = old[part, 1 + j, place, :] - sums[part] / weight
                    if last:
                        new[part, rows, 128 * j : 128 * j + 128] = cells
                    else:
                        new[part, 1 + j, place, :] = cells

    arrive(s3)
    total = buf3[0] + buf3[1] + buf3[2] + buf3[3]
    mine = pl.ds(base_x, 8)
    probe_new[:, mine, :] = probe[:, mine, :] - total[:2] / (total[2:] + 1.0)
    part = probe_new.at[:, mine, :]
    arrive([send(part, part, peer) for peer in at.along_x])
    part = probe_new.at[:, pl.ds(base_y, 32), :]
    s5 = [send(part, part, peer) for peer in at.along_y]
    if not last:
        finish_object()
        halo = send_halo(send, at, new)
    arrive(s5)
    part = probe_new.at[:, pl.ds(base, 128), :]
    s6 = send(part, part, at.twin)
    if last:
        finish_object()
    s6.wait_recv()
    if not last:
        arrive(halo)
    send.close()
    if not last:
        clear_outside(at, new)


VMEM = pl.BlockSpec(memory_space=pltpu.VMEM)
SMEM = pl.BlockSpec(memory_space=pltpu.SMEM)
LIMIT = 20 * 2**20


def open_halo(cells):
    return pl.pallas_call(
        open_kernel,
        out_shape=jax.ShapeDtypeStruct((2, 4, ROWS, 128), f32),
        in_specs=[VMEM],
        out_specs=VMEM,
        scratch_shapes=[pltpu.SemaphoreType.DMA((8,)), pltpu.SemaphoreType.DMA((8,))],
        compiler_params=pltpu.CompilerParams(
            collective_id=0, has_side_effects=True, vmem_limit_bytes=LIMIT
        ),
    )(cells)


def step(last, grad, psum, old, probe):
    shape = (2, F, F) if last else (2, 4, ROWS, 128)
    copies = 27 if last else 35
    return pl.pallas_call(
        functools.partial(step_kernel, last),
        out_shape=(jax.ShapeDtypeStruct(shape, f32), jax.ShapeDtypeStruct((2, F, F), f32)),
        in_specs=[VMEM] * 4,
        out_specs=(VMEM, VMEM),
        scratch_shapes=[
            *(pltpu.VMEM((3, 2, HALF, 128), f32) for _ in range(2)),
            *(pltpu.VMEM((3, 1, F, 128), f32) for _ in range(2)),
            pltpu.VMEM((4, 3, 1, HALF, 128), f32),
            pltpu.VMEM((3, 128, F), f32),
            pltpu.VMEM((3, 128, F), f32),
            pltpu.VMEM((3, 32, F), f32),
            pltpu.VMEM((3, 3, 32, F), f32),
            pltpu.VMEM((3, 8, F), f32),
            pltpu.VMEM((3, 3, 8, F), f32),
            pltpu.VMEM((4, 3, 8, F), f32),
            pltpu.SemaphoreType.DMA((copies,)),
            pltpu.SemaphoreType.DMA((copies,)),
        ],
        compiler_params=pltpu.CompilerParams(
            collective_id=2 if last else 1, has_side_effects=True, vmem_limit_bytes=LIMIT
        ),
    )(grad, psum, old, probe)


def body(positions, counts, amplitudes, object_field, probe):
    fwd, inv = tables()
    corners = positions[0, 0].T
    load = counts[0]
    ext = open_halo(object_field)
    for iteration in range(ITERS):
        grad, psum = slots(corners, load, amplitudes[0, 0], ext, probe, fwd, inv)
        ext, probe = step(iteration == ITERS - 1, grad, psum, ext, probe)
    return ext, probe


def solution(mesh):
    return jax.shard_map(
        body,
        mesh=mesh,
        in_specs=(
            P("row", "col", None, None),
            P("row", "col"),
            P("row", "col", None, None, None),
            P(None, "row", "col"),
            P(),
        ),
        out_specs=(P(None, "row", "col"), P()),
        check_vma=False,
    )
```

```python
import functools, math
import numpy as np
import jax, jax.numpy as jnp
from jax import lax
from jax.experimental import pallas as pl
from jax.experimental.pallas import tpu as pltpu
from jax.sharding import PartitionSpec as P

F = 256
ITERS = 2
f32=jnp.float32; bf16=jnp.bfloat16

def tables():
    c=np.arange(F,dtype=np.int32)
    ang=(c[:,None]*c[None,:]%F).astype(np.float32)*np.float32(2*math.pi/F)
    re=(np.cos(ang)/np.float32(16)).astype(np.float32)
    im=(-np.sin(ang)/np.float32(16)).astype(np.float32)
    fwd=np.block([[re,-im],[im,re]]); inv=np.block([[re,im],[-im,re]])
    return jnp.asarray(fwd,bf16), jnp.asarray(inv,bf16)

CH=16; B=2; ROWS=3*F
def both_sides(table, other, cells):
    re = jnp.dot(table[:F, :], cells[...], preferred_element_type=f32).astype(bf16)
    im = jnp.dot(table[F:, :], cells[...], preferred_element_type=f32).astype(bf16)
    stacked = jnp.concatenate(
        [jnp.concatenate([re[:, F * b : F * b + F], im[:, F * b : F * b + F]], 1) for b in range(B)], 0
    )
    return jnp.dot(stacked, other[...], preferred_element_type=f32)


def slots_kernel(corner, load, amp, ext, probe, fwd, inv, grad, psum,
                 patch0, patch1, cov, exit_s, miss0, miss1, chi_s):
    lane=lax.broadcasted_iota(jnp.int32,(CH,128),1)
    n=load[0]
    top=lax.axis_index("row")*F-F//2; left=lax.axis_index("col")*F-F//2
    def place(k):
        kk=jnp.minimum(k,15)
        live=k<n
        r=jnp.where(live,corner[0,kk]-top,2*F); c=jnp.where(live,corner[1,kk]-left,0)
        q=c//128; s=c-q*128
        return r,q,s,kk
    def front(g,patch,miss):
        for b in range(B):
            r,q,s,kk=place(B*g+b)
            back=jnp.where(s==0,0,128-s)
            keep=lane<128-s
            for i in range(F//CH):
                rows=pl.ds(i*CH,CH)
                got=[]
                for ch in range(2):
                    t=[pltpu.roll(ext[ch,q+j,pl.ds(r+i*CH,CH),:],back,1) for j in range(3)]
                    got.append(jnp.concatenate([jnp.where(keep,t[0],t[1]),jnp.where(keep,t[1],t[2])],1))
                re,im=got
                patch[b,0,rows,:]=re; patch[b,1,rows,:]=im
                pr=probe[0,rows,:]; pi=probe[1,rows,:]
                exit_s[rows,F*b:F*b+F]=(pr*re-pi*im).astype(bf16)
                exit_s[pl.ds(F+i*CH,CH),F*b:F*b+F]=(pr*im+pi*re).astype(bf16)
        far=both_sides(fwd,inv,exit_s)
        for b in range(B):
            kk=jnp.minimum(B*g+b,15)
            fr=far[F*b:F*b+F,:F]; fi=far[F*b:F*b+F,F:]
            ratio=1.0-amp[kk].astype(f32)*lax.rsqrt(fr*fr+fi*fi+1.0)
            miss[:F,F*b:F*b+F]=(fr*ratio).astype(bf16)
            miss[F:,F*b:F*b+F]=(fi*ratio).astype(bf16)
    def back_(g,patch,miss):
        chi=both_sides(inv,fwd,miss)
        chi_s[...]=chi
        for i in range(F//CH):
            rows=pl.ds(i*CH,CH)
            pr=probe[0,rows,:]; pi=probe[1,rows,:]
            p0=p1=p2=0.0
            for b in range(B):
                at_=pl.ds(F*b+i*CH,CH)
                cr=chi_s[at_,:F]; ci=chi_s[at_,F:]
                re=patch[b,0,rows,:]; im=patch[b,1,rows,:]
                p0+=re*cr+im*ci; p1+=re*ci-im*cr; p2+=re*re+im*im
            psum[0,rows,:]+=p0; psum[1,rows,:]+=p1; psum[2,rows,:]+=p2
        for b in range(B):
            r,q,s,kk=place(B*g+b)
            put=lane>=s
            for i in range(F//CH):
                rows=pl.ds(i*CH,CH); at_=pl.ds(F*b+i*CH,CH)
                cr=chi_s[at_,:F]; ci=chi_s[at_,F:]
                pr=probe[0,rows,:]; pi=probe[1,rows,:]
                for ch,u in ((0,pr*cr+pi*ci),(1,pr*ci-pi*cr),(2,cov[rows,:])):
                    u0=pltpu.roll(u[:,:128],s,1); u1=pltpu.roll(u[:,128:],s,1)
                    at=pl.ds(r+i*CH,CH)
                    grad[ch,q,at,:]+=jnp.where(put,u0,0.0)
                    grad[ch,q+1,at,:]+=jnp.where(put,u1,u0)
                    grad[ch,q+2,at,:]+=jnp.where(put,0.0,u1)
    for ch in range(3):
        for j in range(4):
            grad[ch,j,:2*F,:]=jnp.zeros((2*F,128),f32)
    psum[...]=jnp.zeros(psum.shape,f32)
    cov[...]=probe[0]*probe[0]+probe[1]*probe[1]
    front(0,patch0,miss0)
    pairs=(n+2*B-1)//(2*B)
    def it(j,_):
        back_(2*j,patch0,miss0)
        front(2*j+1,patch1,miss1)
        back_(2*j+1,patch1,miss1)
        front(2*j+2,patch0,miss0)
        return 0
    lax.fori_loop(0,pairs,it,0)
def slots(corner,load,amp,ext,probe,fwd,inv):
    V=pl.BlockSpec(memory_space=pltpu.VMEM); S=pl.BlockSpec(memory_space=pltpu.SMEM)
    return pl.pallas_call(slots_kernel,
        out_shape=(jax.ShapeDtypeStruct((3,4,ROWS,128),f32),jax.ShapeDtypeStruct((3,F,F),f32)),
        in_specs=[S,S,V,V,V,V,V], out_specs=(V,V),
        scratch_shapes=[pltpu.VMEM((B,2,F,F),f32),pltpu.VMEM((B,2,F,F),f32),pltpu.VMEM((F,F),f32),pltpu.VMEM((2*F,B*F),bf16),
            pltpu.VMEM((2*F,B*F),bf16),pltpu.VMEM((2*F,B*F),bf16),pltpu.VMEM((B*F,2*F),f32)],
        compiler_params=pltpu.CompilerParams(vmem_limit_bytes=24*2**20),
    )(corner,load,amp,ext,probe,fwd,inv)


MESH = pl.DeviceIdType.MESH
HALF = F // 2
TILE = slice(HALF, HALF + F)


TOP, BOTTOM = pl.ds(HALF, HALF), pl.ds(F, HALF)
ABOVE, BELOW = pl.ds(0, HALF), pl.ds(F + HALF, HALF)


class Places:
    def __init__(self):
        row, col = lax.axis_index("row"), lax.axis_index("col")
        n_row, n_col = lax.axis_size("row"), lax.axis_size("col")
        self.row, self.col, self.n_row, self.n_col = row, col, n_row, n_col
        z_lo, self.y = row // 4, row % 4
        self.x, z_hi, self.core = col // 4, col // 2 % 2, col % 2
        self.z = z_hi * 2 + z_lo
        self.up, self.down = ((row + n_row - 1) % n_row, col), ((row + 1) % n_row, col)
        self.twin = (row, col + 1 - 2 * self.core)
        self.far = (row, (col + n_col - 1 + 2 * self.core) % n_col)
        self.near_north, self.near_south = (self.up[0], self.twin[1]), (self.down[0], self.twin[1])
        self.far_north, self.far_south = (self.up[0], self.far[1]), (self.down[0], self.far[1])
        self.around = (
            self.up, self.down, self.twin, self.far,
            self.near_north, self.near_south, self.far_north, self.far_south,
        )
        self.near_rim, self.far_rim = 3 - 3 * self.core, 3 * self.core
        self.near_edge, self.far_edge = 2 - self.core, 1 + self.core
        self.along_x = [(row, (self.x + d) % 4 * 4 + col % 4) for d in (1, 2, 3)]
        self.along_y = [(z_lo * 4 + (self.y + d) % 4, col) for d in (1, 2, 3)]
        self.along_z = []
        for d in (1, 2, 3):
            z = (self.z + d) % 4
            self.along_z.append((z % 2 * 4 + self.y, self.x * 4 + z // 2 * 2 + self.core))


def meet(peers):
    barrier = pltpu.get_barrier_semaphore()
    for peer in peers:
        pl.semaphore_signal(barrier, inc=1, device_id=peer, device_id_type=MESH)
    pl.semaphore_wait(barrier, len(peers))


class Sender:
    def __init__(self, send_sem, recv_sem):
        self.send_sem, self.recv_sem, self.used = send_sem, recv_sem, 0
        self.open = []

    def __call__(self, src, dst, peer):
        copy = pltpu.make_async_remote_copy(
            src_ref=src,
            dst_ref=dst,
            send_sem=self.send_sem.at[self.used],
            recv_sem=self.recv_sem.at[self.used],
            device_id=peer,
            device_id_type=MESH,
        )
        self.used += 1
        copy.start()
        self.open.append(copy)
        return copy

    def close(self):
        for copy in self.open:
            copy.wait_send()


def arrive(copies):
    for copy in copies:
        copy.wait_recv()


INNER = pl.ds(HALF, F)
BOTH = pl.ds(1, 2)


def send_halo(send, at, ext):
    near, far = pl.ds(at.near_edge, 1), pl.ds(at.far_edge, 1)
    there_near, there_far = pl.ds(at.far_rim, 1), pl.ds(at.near_rim, 1)
    return [
        send(ext.at[:, far, INNER, :], ext.at[:, there_far, INNER, :], at.far),
        send(ext.at[:, BOTH, TOP, :], ext.at[:, BOTH, BELOW, :], at.up),
        send(ext.at[:, BOTH, BOTTOM, :], ext.at[:, BOTH, ABOVE, :], at.down),
        send(ext.at[:, far, TOP, :], ext.at[:, there_far, BELOW, :], at.far_north),
        send(ext.at[:, far, BOTTOM, :], ext.at[:, there_far, ABOVE, :], at.far_south),
        send(ext.at[:, near, INNER, :], ext.at[:, there_near, INNER, :], at.twin),
        send(ext.at[:, near, TOP, :], ext.at[:, there_near, BELOW, :], at.near_north),
        send(ext.at[:, near, BOTTOM, :], ext.at[:, there_near, ABOVE, :], at.near_south),
    ]


def clear_outside(at, ext):
    ext[:, :, 2 * F :, :] = jnp.zeros((2, 4, ROWS - 2 * F, 128), f32)

    @pl.when(at.row == 0)
    def _():
        ext[:, :, :HALF, :] = jnp.zeros((2, 4, HALF, 128), f32)

    @pl.when(at.row == at.n_row - 1)
    def _():
        ext[:, :, F + HALF : 2 * F, :] = jnp.zeros((2, 4, HALF, 128), f32)

    @pl.when(at.col == 0)
    def _():
        ext[:, 0, : 2 * F, :] = jnp.zeros((2, 2 * F, 128), f32)

    @pl.when(at.col == at.n_col - 1)
    def _():
        ext[:, 3, : 2 * F, :] = jnp.zeros((2, 2 * F, 128), f32)


def open_kernel(cells, ext, send_sem, recv_sem):
    at = Places()
    meet(at.around)
    for part in range(2):
        for j in range(2):
            ext[part, 1 + j, TILE, :] = cells[part, :, 128 * j : 128 * j + 128]
    send = Sender(send_sem, recv_sem)
    arrive(send_halo(send, at, ext))
    send.close()
    clear_outside(at, ext)


def step_kernel(last, grad, psum, old, probe, new, probe_new, *scratch):
    from_up, from_down, sides_in, far_in, side, strips = scratch[:6]
    acc0, buf0, acc1, buf1, acc2, buf2, buf3, send_sem, recv_sem = scratch[6:]
    at = Places()
    meet((*at.around, *at.along_x, *at.along_y, *at.along_z))
    send = Sender(send_sem, recv_sem)
    above, below = at.row > 0, at.row < at.n_row - 1
    before, after = at.col > 0, at.col < at.n_col - 1
    base = at.core * 128
    base_x = base + at.x * 32
    base_y = base_x + at.y * 8
    near_rim, far_rim = pl.ds(at.near_rim, 1), pl.ds(at.far_rim, 1)
    far_edge = pl.ds(at.far_edge, 1)
    near_part, far_part = pl.ds(at.near_edge - 1, 1), pl.ds(at.far_edge - 1, 1)

    s0 = send(psum.at[:, pl.ds(128 - base, 128), :], buf0, at.twin)
    twins = send(grad.at[:, near_rim, : 2 * F, :], sides_in.at[at.core], at.twin)
    corners = [
        send(grad.at[:, far_rim, ABOVE, :], far_in.at[1], at.up),
        send(grad.at[:, far_rim, BELOW, :], far_in.at[0], at.down),
    ]
    rims = [
        send(grad.at[:, far_edge, ABOVE, :], from_down.at[:, far_part], at.up),
        send(grad.at[:, far_edge, BELOW, :], from_up.at[:, far_part], at.down),
    ]
    s0.wait_recv()
    acc0[...] = psum[:, pl.ds(base, 128), :] + buf0[...]
    s1 = [
        send(acc0.at[:, pl.ds((at.x + d) % 4 * 32, 32), :], buf1.at[d - 1], at.along_x[d - 1])
        for d in (1, 2, 3)
    ]
    twins.wait_recv()
    for ch in range(3):
        for k, rows in enumerate((ABOVE, BELOW)):
            strips[k, ch, 0] = grad[ch, at.near_edge, rows, :] + sides_in[1 - at.core, ch, 0, rows, :]

    def send_side():
        rims.append(send(side, sides_in.at[1 - at.core, :, :, INNER, :], at.far))

    arrive(corners)
    for ch in range(3):
        side[ch, 0, :HALF, :] = grad[ch, at.far_rim, TOP, :] + jnp.where(above, far_in[0, ch, 0], 0.0)
        side[ch, 0, HALF:, :] = grad[ch, at.far_rim, BOTTOM, :] + jnp.where(below, far_in[1, ch, 0], 0.0)
    if not last:
        send_side()
    arrive(s1)
    acc1[...] = acc0[:, pl.ds(at.x * 32, 32), :] + buf1[0] + buf1[1] + buf1[2]
    s2 = [
        send(acc1.at[:, pl.ds((at.y + d) % 4 * 8, 8), :], buf2.at[d - 1], at.along_y[d - 1])
        for d in (1, 2, 3)
    ]
    rims.append(send(strips.at[0], from_down.at[:, near_part], at.up))
    rims.append(send(strips.at[1], from_up.at[:, near_part], at.down))
    arrive(s2)
    acc2[...] = acc1[:, pl.ds(at.y * 8, 8), :] + buf2[0] + buf2[1] + buf2[2]
    buf3[at.z] = acc2[...]
    s3 = [send(acc2, buf3.at[at.z], at.along_z[d - 1]) for d in (1, 2, 3)]
    if last:
        send_side()

    def finish_object():
        arrive(rims)
        for j, beside in enumerate((before, after)):
            for half, (level, rim) in enumerate(((above, from_up), (below, from_down))):
                rows = pl.ds(HALF * half, HALF)
                place = pl.ds(HALF + HALF * half, HALF)
                sums = []
                for ch in range(3):
                    sums.append(
                        grad[ch, 1 + j, place, :]
                        + jnp.where(level, rim[ch, j], 0.0)
                        + jnp.where(beside, sides_in[j, ch, 0, place, :], 0.0)
                    )
                weight = sums[2] + 1.0
                for part in range(2):
                    cells = old[part, 1 + j, place, :] - sums[part] / weight
                    if last:
                        new[part, rows, 128 * j : 128 * j + 128] = cells
                    else:
                        new[part, 1 + j, place, :] = cells

    arrive(s3)
    total = buf3[0] + buf3[1] + buf3[2] + buf3[3]
    mine = pl.ds(base_y, 8)
    probe_new[:, mine, :] = probe[:, mine, :] - total[:2] / (total[2:] + 1.0)
    part = probe_new.at[:, mine, :]
    s4 = [send(part, part, peer) for peer in at.along_y]
    if not last:
        finish_object()
        halo = send_halo(send, at, new)
    arrive(s4)
    part = probe_new.at[:, pl.ds(base_x, 32), :]
    arrive([send(part, part, peer) for peer in at.along_x])
    part = probe_new.at[:, pl.ds(base, 128), :]
    s6 = send(part, part, at.twin)
    if last:
        finish_object()
    s6.wait_recv()
    if not last:
        arrive(halo)
    send.close()
    if not last:
        clear_outside(at, new)


VMEM = pl.BlockSpec(memory_space=pltpu.VMEM)
SMEM = pl.BlockSpec(memory_space=pltpu.SMEM)
LIMIT = 20 * 2**20


def open_halo(cells):
    return pl.pallas_call(
        open_kernel,
        out_shape=jax.ShapeDtypeStruct((2, 4, ROWS, 128), f32),
        in_specs=[VMEM],
        out_specs=VMEM,
        scratch_shapes=[pltpu.SemaphoreType.DMA((8,)), pltpu.SemaphoreType.DMA((8,))],
        compiler_params=pltpu.CompilerParams(
            collective_id=0, has_side_effects=True, vmem_limit_bytes=LIMIT
        ),
    )(cells)


def step(last, grad, psum, old, probe):
    shape = (2, F, F) if last else (2, 4, ROWS, 128)
    copies = 25 if last else 33
    return pl.pallas_call(
        functools.partial(step_kernel, last),
        out_shape=(jax.ShapeDtypeStruct(shape, f32), jax.ShapeDtypeStruct((2, F, F), f32)),
        in_specs=[VMEM] * 4,
        out_specs=(VMEM, VMEM),
        scratch_shapes=[
            pltpu.VMEM((3, 2, HALF, 128), f32),
            pltpu.VMEM((3, 2, HALF, 128), f32),
            pltpu.VMEM((2, 3, 1, 2 * F, 128), f32),
            pltpu.VMEM((2, 3, 1, HALF, 128), f32),
            pltpu.VMEM((3, 1, F, 128), f32),
            pltpu.VMEM((2, 3, 1, HALF, 128), f32),
            pltpu.VMEM((3, 128, F), f32),
            pltpu.VMEM((3, 128, F), f32),
            pltpu.VMEM((3, 32, F), f32),
            pltpu.VMEM((3, 3, 32, F), f32),
            pltpu.VMEM((3, 8, F), f32),
            pltpu.VMEM((3, 3, 8, F), f32),
            pltpu.VMEM((4, 3, 8, F), f32),
            pltpu.SemaphoreType.DMA((copies,)),
            pltpu.SemaphoreType.DMA((copies,)),
        ],
        compiler_params=pltpu.CompilerParams(
            collective_id=2 if last else 1, has_side_effects=True, vmem_limit_bytes=LIMIT
        ),
    )(grad, psum, old, probe)


def body(positions, counts, amplitudes, object_field, probe):
    fwd, inv = tables()
    corners = positions[0, 0].T
    load = counts[0]
    ext = open_halo(object_field)
    for iteration in range(ITERS):
        grad, psum = slots(corners, load, amplitudes[0, 0], ext, probe, fwd, inv)
        ext, probe = step(iteration == ITERS - 1, grad, psum, ext, probe)
    return ext, probe


def solution(mesh):
    return jax.shard_map(
        body,
        mesh=mesh,
        in_specs=(
            P("row", "col", None, None),
            P("row", "col"),
            P("row", "col", None, None, None),
            P(None, "row", "col"),
            P(),
        ),
        out_specs=(P(None, "row", "col"), P()),
        check_vma=False,
    )
```

```python
import functools, math
import numpy as np
import jax, jax.numpy as jnp
from jax import lax
from jax.experimental import pallas as pl
from jax.experimental.pallas import tpu as pltpu
from jax.sharding import PartitionSpec as P

F = 256
ITERS = 2
f32=jnp.float32; bf16=jnp.bfloat16

def tables():
    c=np.arange(F,dtype=np.int32)
    ang=(c[:,None]*c[None,:]%F).astype(np.float32)*np.float32(2*math.pi/F)
    re=(np.cos(ang)/np.float32(16)).astype(np.float32)
    im=(-np.sin(ang)/np.float32(16)).astype(np.float32)
    fwd=np.block([[re,-im],[im,re]]); inv=np.block([[re,im],[-im,re]])
    return jnp.asarray(fwd,bf16), jnp.asarray(inv,bf16)

CH=16; B=2; ROWS=3*F
def both_sides(table, other, cells):
    re = jnp.dot(table[:F, :], cells[...], preferred_element_type=f32).astype(bf16)
    im = jnp.dot(table[F:, :], cells[...], preferred_element_type=f32).astype(bf16)
    stacked = jnp.concatenate(
        [jnp.concatenate([re[:, F * b : F * b + F], im[:, F * b : F * b + F]], 1) for b in range(B)], 0
    )
    return jnp.dot(stacked, other[...], preferred_element_type=f32)


def slots_kernel(corner, load, amp, ext, probe, fwd, inv, grad, psum,
                 patch0, patch1, cov, exit_s, miss0, miss1, chi_s):
    lane=lax.broadcasted_iota(jnp.int32,(CH,128),1)
    n=load[0]
    top=lax.axis_index("row")*F-F//2; left=lax.axis_index("col")*F-F//2
    def place(k):
        kk=jnp.minimum(k,15)
        live=k<n
        r=jnp.where(live,corner[0,kk]-top,2*F); c=jnp.where(live,corner[1,kk]-left,0)
        q=c//128; s=c-q*128
        return r,q,s,kk
    def front(g,patch,miss):
        for b in range(B):
            r,q,s,kk=place(B*g+b)
            back=jnp.where(s==0,0,128-s)
            keep=lane<128-s
            for i in range(F//CH):
                rows=pl.ds(i*CH,CH)
                got=[]
                for ch in range(2):
                    t=[pltpu.roll(ext[ch,q+j,pl.ds(r+i*CH,CH),:],back,1) for j in range(3)]
                    got.append(jnp.concatenate([jnp.where(keep,t[0],t[1]),jnp.where(keep,t[1],t[2])],1))
                re,im=got
                patch[b,0,rows,:]=re; patch[b,1,rows,:]=im
                pr=probe[0,rows,:]; pi=probe[1,rows,:]
                exit_s[rows,F*b:F*b+F]=(pr*re-pi*im).astype(bf16)
                exit_s[pl.ds(F+i*CH,CH),F*b:F*b+F]=(pr*im+pi*re).astype(bf16)
        far=both_sides(fwd,inv,exit_s)
        for b in range(B):
            kk=jnp.minimum(B*g+b,15)
            fr=far[F*b:F*b+F,:F]; fi=far[F*b:F*b+F,F:]
            ratio=1.0-amp[kk].astype(f32)*lax.rsqrt(fr*fr+fi*fi+1.0)
            miss[:F,F*b:F*b+F]=(fr*ratio).astype(bf16)
            miss[F:,F*b:F*b+F]=(fi*ratio).astype(bf16)
    def back_(g,patch,miss):
        chi=both_sides(inv,fwd,miss)
        chi_s[...]=chi
        for i in range(F//CH):
            rows=pl.ds(i*CH,CH)
            pr=probe[0,rows,:]; pi=probe[1,rows,:]
            p0=p1=p2=0.0
            for b in range(B):
                at_=pl.ds(F*b+i*CH,CH)
                cr=chi_s[at_,:F]; ci=chi_s[at_,F:]
                re=patch[b,0,rows,:]; im=patch[b,1,rows,:]
                p0+=re*cr+im*ci; p1+=re*ci-im*cr; p2+=re*re+im*im
            psum[0,rows,:]+=p0; psum[1,rows,:]+=p1; psum[2,rows,:]+=p2
        for b in range(B):
            r,q,s,kk=place(B*g+b)
            put=lane>=s
            for i in range(F//CH):
                rows=pl.ds(i*CH,CH); at_=pl.ds(F*b+i*CH,CH)
                cr=chi_s[at_,:F]; ci=chi_s[at_,F:]
                pr=probe[0,rows,:]; pi=probe[1,rows,:]
                for ch,u in ((0,pr*cr+pi*ci),(1,pr*ci-pi*cr),(2,cov[rows,:])):
                    u0=pltpu.roll(u[:,:128],s,1); u1=pltpu.roll(u[:,128:],s,1)
                    at=pl.ds(r+i*CH,CH)
                    grad[ch,q,at,:]+=jnp.where(put,u0,0.0)
                    grad[ch,q+1,at,:]+=jnp.where(put,u1,u0)
                    grad[ch,q+2,at,:]+=jnp.where(put,0.0,u1)
    for ch in range(3):
        for j in range(4):
            grad[ch,j,:2*F,:]=jnp.zeros((2*F,128),f32)
    psum[...]=jnp.zeros(psum.shape,f32)
    cov[...]=probe[0]*probe[0]+probe[1]*probe[1]
    front(0,patch0,miss0)
    pairs=(n+2*B-1)//(2*B)
    def it(j,_):
        back_(2*j,patch0,miss0)
        front(2*j+1,patch1,miss1)
        back_(2*j+1,patch1,miss1)
        front(2*j+2,patch0,miss0)
        return 0
    lax.fori_loop(0,pairs,it,0)
def slots(corner,load,amp,ext,probe,fwd,inv):
    V=pl.BlockSpec(memory_space=pltpu.VMEM); S=pl.BlockSpec(memory_space=pltpu.SMEM)
    return pl.pallas_call(slots_kernel,
        out_shape=(jax.ShapeDtypeStruct((3,4,ROWS,128),f32),jax.ShapeDtypeStruct((3,F,F),f32)),
        in_specs=[S,S,V,V,V,V,V], out_specs=(V,V),
        scratch_shapes=[pltpu.VMEM((B,2,F,F),f32),pltpu.VMEM((B,2,F,F),f32),pltpu.VMEM((F,F),f32),pltpu.VMEM((2*F,B*F),bf16),
            pltpu.VMEM((2*F,B*F),bf16),pltpu.VMEM((2*F,B*F),bf16),pltpu.VMEM((B*F,2*F),f32)],
        compiler_params=pltpu.CompilerParams(vmem_limit_bytes=24*2**20),
    )(corner,load,amp,ext,probe,fwd,inv)


MESH = pl.DeviceIdType.MESH
HALF = F // 2
TILE = slice(HALF, HALF + F)


TOP, BOTTOM = pl.ds(HALF, HALF), pl.ds(F, HALF)
ABOVE, BELOW = pl.ds(0, HALF), pl.ds(F + HALF, HALF)


class Places:
    def __init__(self):
        row, col = lax.axis_index("row"), lax.axis_index("col")
        n_row, n_col = lax.axis_size("row"), lax.axis_size("col")
        self.row, self.col, self.n_row, self.n_col = row, col, n_row, n_col
        z_lo, self.y = row // 4, row % 4
        self.x, z_hi, self.core = col // 4, col // 2 % 2, col % 2
        self.z = z_hi * 2 + z_lo
        self.up, self.down = ((row + n_row - 1) % n_row, col), ((row + 1) % n_row, col)
        self.twin = (row, col + 1 - 2 * self.core)
        self.far = (row, (col + n_col - 1 + 2 * self.core) % n_col)
        self.near_north, self.near_south = (self.up[0], self.twin[1]), (self.down[0], self.twin[1])
        self.far_north, self.far_south = (self.up[0], self.far[1]), (self.down[0], self.far[1])
        self.around = (
            self.up, self.down, self.twin, self.far,
            self.near_north, self.near_south, self.far_north, self.far_south,
        )
        self.above, self.below = row > 0, row < n_row - 1
        self.aside = (col > 0) & (col < n_col - 1)
        self.over, self.under = row == n_row // 2, row == n_row // 2 - 1
        self.first, self.final = row == 0, row == n_row - 1
        self.row_first, self.row_final = (0 * row, col), (0 * row + n_row - 1, col)
        self.row_under, self.row_over = (0 * row + n_row // 2 - 1, col), (0 * row + n_row // 2, col)
        self.near_rim, self.far_rim = 3 - 3 * self.core, 3 * self.core
        self.near_edge, self.far_edge = 2 - self.core, 1 + self.core
        self.along_x = [(row, (self.x + d) % 4 * 4 + col % 4) for d in (1, 2, 3)]
        self.along_y = [(z_lo * 4 + (self.y + d) % 4, col) for d in (1, 2, 3)]
        self.along_z = []
        for d in (1, 2, 3):
            z = (self.z + d) % 4
            self.along_z.append((z % 2 * 4 + self.y, self.x * 4 + z // 2 * 2 + self.core))


def meet(peers):
    barrier = pltpu.get_barrier_semaphore()
    for peer in peers:
        pl.semaphore_signal(barrier, inc=1, device_id=peer, device_id_type=MESH)
    pl.semaphore_wait(barrier, len(peers))


def run_if(condition, action):
    if condition is None:
        action()
    else:
        pl.when(condition)(action)


class Sender:
    def __init__(self, send_sem, recv_sem):
        self.send_sem, self.recv_sem, self.used = send_sem, recv_sem, 0
        self.open = []

    def __call__(self, src, dst, peer, sends=None, gets=None):
        copy = pltpu.make_async_remote_copy(
            src_ref=src,
            dst_ref=dst,
            send_sem=self.send_sem.at[self.used],
            recv_sem=self.recv_sem.at[self.used],
            device_id=peer,
            device_id_type=MESH,
        )
        self.used += 1
        run_if(sends, copy.start)
        self.open.append((copy, sends))
        return copy, gets

    def close(self):
        for copy, sends in self.open:
            run_if(sends, copy.wait_send)


def arrive(copies):
    for copy, gets in copies:
        run_if(gets, copy.wait_recv)


INNER = pl.ds(HALF, F)
BOTH = pl.ds(1, 2)


def send_halo(send, at, ext):
    near, far = pl.ds(at.near_edge, 1), pl.ds(at.far_edge, 1)
    there_near, there_far = pl.ds(at.far_rim, 1), pl.ds(at.near_rim, 1)
    up, down, aside = (at.above, at.below), (at.below, at.above), (at.aside, at.aside)
    up_aside, down_aside = (at.above & at.aside, at.below & at.aside), (at.below & at.aside, at.above & at.aside)
    return [
        send(ext.at[:, far, INNER, :], ext.at[:, there_far, INNER, :], at.far, *aside),
        send(ext.at[:, BOTH, TOP, :], ext.at[:, BOTH, BELOW, :], at.up, *up),
        send(ext.at[:, BOTH, BOTTOM, :], ext.at[:, BOTH, ABOVE, :], at.down, *down),
        send(ext.at[:, far, TOP, :], ext.at[:, there_far, BELOW, :], at.far_north, *up_aside),
        send(ext.at[:, far, BOTTOM, :], ext.at[:, there_far, ABOVE, :], at.far_south, *down_aside),
        send(ext.at[:, near, INNER, :], ext.at[:, there_near, INNER, :], at.twin),
        send(ext.at[:, near, TOP, :], ext.at[:, there_near, BELOW, :], at.near_north, *up),
        send(ext.at[:, near, BOTTOM, :], ext.at[:, there_near, ABOVE, :], at.near_south, *down),
    ]


def clear_outside(at, ext):
    ext[:, :, 2 * F :, :] = jnp.zeros((2, 4, ROWS - 2 * F, 128), f32)

    @pl.when(at.row == 0)
    def _():
        ext[:, :, :HALF, :] = jnp.zeros((2, 4, HALF, 128), f32)

    @pl.when(at.row == at.n_row - 1)
    def _():
        ext[:, :, F + HALF : 2 * F, :] = jnp.zeros((2, 4, HALF, 128), f32)

    @pl.when(at.col == 0)
    def _():
        ext[:, 0, : 2 * F, :] = jnp.zeros((2, 2 * F, 128), f32)

    @pl.when(at.col == at.n_col - 1)
    def _():
        ext[:, 3, : 2 * F, :] = jnp.zeros((2, 2 * F, 128), f32)


def open_kernel(cells, ext, send_sem, recv_sem):
    at = Places()
    meet(at.around)
    for part in range(2):
        for j in range(2):
            ext[part, 1 + j, TILE, :] = cells[part, :, 128 * j : 128 * j + 128]
    send = Sender(send_sem, recv_sem)
    arrive(send_halo(send, at, ext))
    send.close()
    clear_outside(at, ext)


def step_kernel(last, grad, psum, old, probe, new, probe_new, *scratch):
    from_up, from_down, sides_in, far_in, side, strips, relay = scratch[:7]
    acc0, buf0, acc1, buf1, acc2, buf2, buf3, send_sem, recv_sem = scratch[7:]
    at = Places()
    meet((*at.around, *at.along_x, *at.along_y, *at.along_z))
    send = Sender(send_sem, recv_sem)
    above, below = at.above, at.below
    up, down = (above, below), (below, above)
    before, after = at.col > 0, at.col < at.n_col - 1
    base = at.core * 128
    base_x = base + at.x * 32
    base_y = base_x + at.y * 8
    near_rim, far_rim = pl.ds(at.near_rim, 1), pl.ds(at.far_rim, 1)
    far_edge = pl.ds(at.far_edge, 1)
    near_part, far_part = pl.ds(at.near_edge - 1, 1), pl.ds(at.far_edge - 1, 1)

    s0 = send(psum.at[:, pl.ds(128 - base, 128), :], buf0, at.twin)
    twins = send(grad.at[:, near_rim, : 2 * F, :], sides_in.at[at.core], at.twin)
    corners = [
        send(grad.at[:, far_rim, ABOVE, :], far_in.at[1], at.up, *up),
        send(grad.at[:, far_rim, BELOW, :], far_in.at[0], at.down, *down),
    ]
    rims = [
        send(grad.at[:, far_edge, ABOVE, :], from_down.at[:, far_part], at.up, *up),
        send(grad.at[:, far_edge, BELOW, :], from_up.at[:, far_part], at.down, *down),
    ]
    arrive([s0])
    acc0[...] = psum[:, pl.ds(base, 128), :] + buf0[...]
    s1 = [
        send(acc0.at[:, pl.ds((at.x + d) % 4 * 32, 32), :], buf1.at[d - 1], at.along_x[d - 1])
        for d in (1, 2, 3)
    ]
    arrive([twins])
    for ch in range(3):
        for k, rows in enumerate((ABOVE, BELOW)):
            strips[k, ch, 0] = grad[ch, at.near_edge, rows, :] + sides_in[1 - at.core, ch, 0, rows, :]

    relays = [
        send(strips.at[0], relay, at.row_first, at.over, at.first),
        send(strips.at[1], relay, at.row_final, at.under, at.final),
    ]

    def send_near():
        rims.extend([
            send(strips.at[0], from_down.at[:, near_part], at.up, above & ~at.over, below & ~at.under),
            send(strips.at[1], from_up.at[:, near_part], at.down, below & ~at.under, above & ~at.over),
        ])

    if not last:
        send_near()

    def send_side():
        rims.append(send(side, sides_in.at[1 - at.core, :, :, INNER, :], at.far, at.aside, at.aside))

    arrive(corners)
    for ch in range(3):
        side[ch, 0, :HALF, :] = grad[ch, at.far_rim, TOP, :] + jnp.where(above, far_in[0, ch, 0], 0.0)
        side[ch, 0, HALF:, :] = grad[ch, at.far_rim, BOTTOM, :] + jnp.where(below, far_in[1, ch, 0], 0.0)
    send_side()
    arrive(s1)
    acc1[...] = acc0[:, pl.ds(at.x * 32, 32), :] + buf1[0] + buf1[1] + buf1[2]
    s2 = [
        send(acc1.at[:, pl.ds((at.y + d) % 4 * 8, 8), :], buf2.at[d - 1], at.along_y[d - 1])
        for d in (1, 2, 3)
    ]
    if last:
        send_near()
    arrive(s2)
    acc2[...] = acc1[:, pl.ds(at.y * 8, 8), :] + buf2[0] + buf2[1] + buf2[2]
    buf3[at.z] = acc2[...]
    s3 = [send(acc2, buf3.at[at.z], at.along_z[d - 1]) for d in (1, 2, 3)]

    arrive(relays)
    rims += [
        send(relay, from_down.at[:, near_part], at.row_under, at.first, at.under),
        send(relay, from_up.at[:, near_part], at.row_over, at.final, at.over),
    ]

    def finish_object():
        arrive(rims)
        for j, beside in enumerate((before, after)):
            for half, (level, rim) in enumerate(((above, from_up), (below, from_down))):
                rows = pl.ds(HALF * half, HALF)
                place = pl.ds(HALF + HALF * half, HALF)
                sums = []
                for ch in range(3):
                    sums.append(
                        grad[ch, 1 + j, place, :]
                        + jnp.where(level, rim[ch, j], 0.0)
                        + jnp.where(beside, sides_in[j, ch, 0, place, :], 0.0)
                    )
                weight = sums[2] + 1.0
                for part in range(2):
                    cells = old[part, 1 + j, place, :] - sums[part] / weight
                    if last:
                        new[part, rows, 128 * j : 128 * j + 128] = cells
                    else:
                        new[part, 1 + j, place, :] = cells

    arrive(s3)
    total = buf3[0] + buf3[1] + buf3[2] + buf3[3]
    mine = pl.ds(base_y, 8)
    probe_new[:, mine, :] = probe[:, mine, :] - total[:2] / (total[2:] + 1.0)
    part = probe_new.at[:, mine, :]
    s4 = [send(part, part, peer) for peer in at.along_y]
    if not last:
        finish_object()
        halo = send_halo(send, at, new)
    arrive(s4)
    part = probe_new.at[:, pl.ds(base_x, 32), :]
    arrive([send(part, part, peer) for peer in at.along_x])
    part = probe_new.at[:, pl.ds(base, 128), :]
    s6 = send(part, part, at.twin)
    if last:
        finish_object()
    arrive([s6])
    if not last:
        arrive(halo)
    send.close()
    if not last:
        clear_outside(at, new)


VMEM = pl.BlockSpec(memory_space=pltpu.VMEM)
SMEM = pl.BlockSpec(memory_space=pltpu.SMEM)
LIMIT = 20 * 2**20


def open_halo(cells):
    return pl.pallas_call(
        open_kernel,
        out_shape=jax.ShapeDtypeStruct((2, 4, ROWS, 128), f32),
        in_specs=[VMEM],
        out_specs=VMEM,
        scratch_shapes=[pltpu.SemaphoreType.DMA((8,)), pltpu.SemaphoreType.DMA((8,))],
        compiler_params=pltpu.CompilerParams(
            collective_id=0, has_side_effects=True, vmem_limit_bytes=LIMIT
        ),
    )(cells)


def step(last, grad, psum, old, probe):
    shape = (2, F, F) if last else (2, 4, ROWS, 128)
    copies = 29 if last else 37
    return pl.pallas_call(
        functools.partial(step_kernel, last),
        out_shape=(jax.ShapeDtypeStruct(shape, f32), jax.ShapeDtypeStruct((2, F, F), f32)),
        in_specs=[VMEM] * 4,
        out_specs=(VMEM, VMEM),
        scratch_shapes=[
            pltpu.VMEM((3, 2, HALF, 128), f32),
            pltpu.VMEM((3, 2, HALF, 128), f32),
            pltpu.VMEM((2, 3, 1, 2 * F, 128), f32),
            pltpu.VMEM((2, 3, 1, HALF, 128), f32),
            pltpu.VMEM((3, 1, F, 128), f32),
            pltpu.VMEM((2, 3, 1, HALF, 128), f32),
            pltpu.VMEM((3, 1, HALF, 128), f32),
            pltpu.VMEM((3, 128, F), f32),
            pltpu.VMEM((3, 128, F), f32),
            pltpu.VMEM((3, 32, F), f32),
            pltpu.VMEM((3, 3, 32, F), f32),
            pltpu.VMEM((3, 8, F), f32),
            pltpu.VMEM((3, 3, 8, F), f32),
            pltpu.VMEM((4, 3, 8, F), f32),
            pltpu.SemaphoreType.DMA((copies,)),
            pltpu.SemaphoreType.DMA((copies,)),
        ],
        compiler_params=pltpu.CompilerParams(
            collective_id=2 if last else 1, has_side_effects=True, vmem_limit_bytes=LIMIT
        ),
    )(grad, psum, old, probe)


def body(positions, counts, amplitudes, object_field, probe):
    fwd, inv = tables()
    corners = positions[0, 0].T
    load = counts[0]
    ext = open_halo(object_field)
    for iteration in range(ITERS):
        grad, psum = slots(corners, load, amplitudes[0, 0], ext, probe, fwd, inv)
        ext, probe = step(iteration == ITERS - 1, grad, psum, ext, probe)
    return ext, probe


def solution(mesh):
    return jax.shard_map(
        body,
        mesh=mesh,
        in_specs=(
            P("row", "col", None, None),
            P("row", "col"),
            P("row", "col", None, None, None),
            P(None, "row", "col"),
            P(),
        ),
        out_specs=(P(None, "row", "col"), P()),
        check_vma=False,
    )
```

```python
import functools, math
import numpy as np
import jax, jax.numpy as jnp
from jax import lax
from jax.experimental import pallas as pl
from jax.experimental.pallas import tpu as pltpu
from jax.sharding import PartitionSpec as P

F = 256
ITERS = 2
f32=jnp.float32; bf16=jnp.bfloat16

def tables():
    c=np.arange(F,dtype=np.int32)
    ang=(c[:,None]*c[None,:]%F).astype(np.float32)*np.float32(2*math.pi/F)
    re=(np.cos(ang)/np.float32(16)).astype(np.float32)
    im=(-np.sin(ang)/np.float32(16)).astype(np.float32)
    fwd=np.block([[re,-im],[im,re]]); inv=np.block([[re,im],[-im,re]])
    return jnp.asarray(fwd,bf16), jnp.asarray(inv,bf16)

CH=16; B=2; ROWS=3*F
def both_sides(table, other, cells):
    re = jnp.dot(table[:F, :], cells[...], preferred_element_type=f32).astype(bf16)
    im = jnp.dot(table[F:, :], cells[...], preferred_element_type=f32).astype(bf16)
    stacked = jnp.concatenate(
        [jnp.concatenate([re[:, F * b : F * b + F], im[:, F * b : F * b + F]], 1) for b in range(B)], 0
    )
    return jnp.dot(stacked, other[...], preferred_element_type=f32)


def slots_kernel(corner, load, amp, ext, probe, fwd, inv, grad, psum,
                 patch0, patch1, cov, exit_s, miss0, miss1, chi_s):
    lane=lax.broadcasted_iota(jnp.int32,(CH,128),1)
    n=load[0]
    top=lax.axis_index("row")*F-F//2; left=lax.axis_index("col")*F-F//2
    def place(k):
        kk=jnp.minimum(k,15)
        live=k<n
        r=jnp.where(live,corner[0,kk]-top,2*F); c=jnp.where(live,corner[1,kk]-left,0)
        q=c//128; s=c-q*128
        return r,q,s,kk
    def front(g,patch,miss):
        for b in range(B):
            r,q,s,kk=place(B*g+b)
            back=jnp.where(s==0,0,128-s)
            keep=lane<128-s
            for i in range(F//CH):
                rows=pl.ds(i*CH,CH)
                got=[]
                for ch in range(2):
                    t=[pltpu.roll(ext[ch,q+j,pl.ds(r+i*CH,CH),:],back,1) for j in range(3)]
                    got.append(jnp.concatenate([jnp.where(keep,t[0],t[1]),jnp.where(keep,t[1],t[2])],1))
                re,im=got
                patch[b,0,rows,:]=re; patch[b,1,rows,:]=im
                pr=probe[0,rows,:]; pi=probe[1,rows,:]
                exit_s[rows,F*b:F*b+F]=(pr*re-pi*im).astype(bf16)
                exit_s[pl.ds(F+i*CH,CH),F*b:F*b+F]=(pr*im+pi*re).astype(bf16)
        far=both_sides(fwd,inv,exit_s)
        for b in range(B):
            kk=jnp.minimum(B*g+b,15)
            fr=far[F*b:F*b+F,:F]; fi=far[F*b:F*b+F,F:]
            ratio=1.0-amp[kk].astype(f32)*lax.rsqrt(fr*fr+fi*fi+1.0)
            miss[:F,F*b:F*b+F]=(fr*ratio).astype(bf16)
            miss[F:,F*b:F*b+F]=(fi*ratio).astype(bf16)
    def back_(g,patch,miss):
        chi=both_sides(inv,fwd,miss)
        chi_s[...]=chi
        for i in range(F//CH):
            rows=pl.ds(i*CH,CH)
            pr=probe[0,rows,:]; pi=probe[1,rows,:]
            p0=p1=p2=0.0
            for b in range(B):
                at_=pl.ds(F*b+i*CH,CH)
                cr=chi_s[at_,:F]; ci=chi_s[at_,F:]
                re=patch[b,0,rows,:]; im=patch[b,1,rows,:]
                p0+=re*cr+im*ci; p1+=re*ci-im*cr; p2+=re*re+im*im
            psum[0,rows,:]+=p0; psum[1,rows,:]+=p1; psum[2,rows,:]+=p2
        for b in range(B):
            r,q,s,kk=place(B*g+b)
            put=lane>=s
            for i in range(F//CH):
                rows=pl.ds(i*CH,CH); at_=pl.ds(F*b+i*CH,CH)
                cr=chi_s[at_,:F]; ci=chi_s[at_,F:]
                pr=probe[0,rows,:]; pi=probe[1,rows,:]
                for ch,u in ((0,pr*cr+pi*ci),(1,pr*ci-pi*cr),(2,cov[rows,:])):
                    u0=pltpu.roll(u[:,:128],s,1); u1=pltpu.roll(u[:,128:],s,1)
                    at=pl.ds(r+i*CH,CH)
                    grad[ch,q,at,:]+=jnp.where(put,u0,0.0)
                    grad[ch,q+1,at,:]+=jnp.where(put,u1,u0)
                    grad[ch,q+2,at,:]+=jnp.where(put,0.0,u1)
    for ch in range(3):
        for j in range(4):
            grad[ch,j,:2*F,:]=jnp.zeros((2*F,128),f32)
    psum[...]=jnp.zeros(psum.shape,f32)
    cov[...]=probe[0]*probe[0]+probe[1]*probe[1]
    front(0,patch0,miss0)
    pairs=(n+2*B-1)//(2*B)
    def it(j,_):
        back_(2*j,patch0,miss0)
        front(2*j+1,patch1,miss1)
        back_(2*j+1,patch1,miss1)
        front(2*j+2,patch0,miss0)
        return 0
    lax.fori_loop(0,pairs,it,0)
def slots(corner,load,amp,ext,probe,fwd,inv):
    V=pl.BlockSpec(memory_space=pltpu.VMEM); S=pl.BlockSpec(memory_space=pltpu.SMEM)
    return pl.pallas_call(slots_kernel,
        out_shape=(jax.ShapeDtypeStruct((3,4,ROWS,128),f32),jax.ShapeDtypeStruct((3,F,F),f32)),
        in_specs=[S,S,V,V,V,V,V], out_specs=(V,V),
        scratch_shapes=[pltpu.VMEM((B,2,F,F),f32),pltpu.VMEM((B,2,F,F),f32),pltpu.VMEM((F,F),f32),pltpu.VMEM((2*F,B*F),bf16),
            pltpu.VMEM((2*F,B*F),bf16),pltpu.VMEM((2*F,B*F),bf16),pltpu.VMEM((B*F,2*F),f32)],
        compiler_params=pltpu.CompilerParams(vmem_limit_bytes=24*2**20),
    )(corner,load,amp,ext,probe,fwd,inv)


MESH = pl.DeviceIdType.MESH
HALF = F // 2
TILE = slice(HALF, HALF + F)


TOP, BOTTOM = pl.ds(HALF, HALF), pl.ds(F, HALF)
ABOVE, BELOW = pl.ds(0, HALF), pl.ds(F + HALF, HALF)


class Places:
    def __init__(self):
        row, col = lax.axis_index("row"), lax.axis_index("col")
        n_row, n_col = lax.axis_size("row"), lax.axis_size("col")
        self.row, self.col, self.n_row, self.n_col = row, col, n_row, n_col
        z_lo, self.y = row // 4, row % 4
        self.x, z_hi, self.core = col // 4, col // 2 % 2, col % 2
        self.z = z_hi * 2 + z_lo
        self.up, self.down = ((row + n_row - 1) % n_row, col), ((row + 1) % n_row, col)
        self.twin = (row, col + 1 - 2 * self.core)
        self.far = (row, (col + n_col - 1 + 2 * self.core) % n_col)
        self.near_north, self.near_south = (self.up[0], self.twin[1]), (self.down[0], self.twin[1])
        self.far_north, self.far_south = (self.up[0], self.far[1]), (self.down[0], self.far[1])
        self.around = (
            self.up, self.down, self.twin, self.far,
            self.near_north, self.near_south, self.far_north, self.far_south,
        )
        self.above, self.below = row > 0, row < n_row - 1
        self.aside = (col > 0) & (col < n_col - 1)
        self.over, self.under = row == n_row // 2, row == n_row // 2 - 1
        self.first, self.final = row == 0, row == n_row - 1
        self.row_first, self.row_final = (0 * row, col), (0 * row + n_row - 1, col)
        self.row_under, self.row_over = (0 * row + n_row // 2 - 1, col), (0 * row + n_row // 2, col)
        self.near_rim, self.far_rim = 3 - 3 * self.core, 3 * self.core
        self.near_edge, self.far_edge = 2 - self.core, 1 + self.core
        self.along_x = [(row, (self.x + d) % 4 * 4 + col % 4) for d in (1, 2, 3)]
        self.along_y = [(z_lo * 4 + (self.y + d) % 4, col) for d in (1, 2, 3)]
        self.along_z = []
        for d in (1, 2, 3):
            z = (self.z + d) % 4
            self.along_z.append((z % 2 * 4 + self.y, self.x * 4 + z // 2 * 2 + self.core))


def meet(peers):
    barrier = pltpu.get_barrier_semaphore()
    for peer in peers:
        pl.semaphore_signal(barrier, inc=1, device_id=peer, device_id_type=MESH)
    pl.semaphore_wait(barrier, len(peers))


def run_if(condition, action):
    if condition is None:
        action()
    else:
        pl.when(condition)(action)


class Sender:
    def __init__(self, send_sem, recv_sem):
        self.send_sem, self.recv_sem, self.used = send_sem, recv_sem, 0
        self.open = []

    def __call__(self, src, dst, peer, sends=None, gets=None):
        copy = pltpu.make_async_remote_copy(
            src_ref=src,
            dst_ref=dst,
            send_sem=self.send_sem.at[self.used],
            recv_sem=self.recv_sem.at[self.used],
            device_id=peer,
            device_id_type=MESH,
        )
        self.used += 1
        run_if(sends, copy.start)
        self.open.append((copy, sends))
        return copy, gets

    def close(self):
        for copy, sends in self.open:
            run_if(sends, copy.wait_send)


def arrive(copies):
    for copy, gets in copies:
        run_if(gets, copy.wait_recv)


INNER = pl.ds(HALF, F)
BOTH = pl.ds(1, 2)


def send_halo(send, at, ext, relay):
    near, far = pl.ds(at.near_edge, 1), pl.ds(at.far_edge, 1)
    there_near, there_far = pl.ds(at.far_rim, 1), pl.ds(at.near_rim, 1)
    up, down, aside = (at.above, at.below), (at.below, at.above), (at.aside, at.aside)
    up_aside, down_aside = (at.above & at.aside, at.below & at.aside), (at.below & at.aside, at.above & at.aside)
    up_near = (at.above & ~at.over, at.below & ~at.under)
    down_near = (at.below & ~at.under, at.above & ~at.over)
    real, imag = pl.ds(0, 1), pl.ds(1, 1)
    relays = [
        send(ext.at[:, near, TOP, :], relay, at.row_first, at.over, at.first),
        send(ext.at[:, near, BOTTOM, :], relay, at.row_final, at.under, at.final),
    ]
    side = [send(ext.at[imag, far, INNER, :], ext.at[imag, there_far, INNER, :], at.far, *aside)]
    strips = [
        send(ext.at[:, near, TOP, :], ext.at[:, near, BELOW, :], at.up, *up_near),
        send(ext.at[:, near, BOTTOM, :], ext.at[:, near, ABOVE, :], at.down, *down_near),
    ]
    rest = [
        send(ext.at[real, far, INNER, :], ext.at[real, there_far, INNER, :], at.far, *aside),
        send(ext.at[:, far, TOP, :], ext.at[:, far, BELOW, :], at.up, *up),
        send(ext.at[:, far, BOTTOM, :], ext.at[:, far, ABOVE, :], at.down, *down),
        send(ext.at[real, far, TOP, :], ext.at[real, there_far, BELOW, :], at.far_north, *up_aside),
        send(ext.at[real, far, BOTTOM, :], ext.at[real, there_far, ABOVE, :], at.far_south, *down_aside),
        send(ext.at[:, near, INNER, :], ext.at[:, there_near, INNER, :], at.twin),
    ]
    return (relays, side, strips), rest


def pass_on_halo(send, at, ext, relay, arriving):
    relays, side, strips = arriving
    near, far, there = pl.ds(at.near_edge, 1), pl.ds(at.far_rim, 1), pl.ds(at.far_rim, 1)
    imag = pl.ds(1, 1)
    up_aside, down_aside = (at.above & at.aside, at.below & at.aside), (at.below & at.aside, at.above & at.aside)
    copies, relayed = [], []
    arrive(relays)
    for (row, col), rows, sends, gets in (
        (at.row_under, BELOW, at.first, at.under),
        (at.row_over, ABOVE, at.final, at.over),
    ):
        relayed.append(send(relay, ext.at[:, near, rows, :], (row, col), sends, gets))
    arrive(side)
    copies += [
        send(ext.at[imag, far, TOP, :], ext.at[imag, far, BELOW, :], at.up, *up_aside),
        send(ext.at[imag, far, BOTTOM, :], ext.at[imag, far, ABOVE, :], at.down, *down_aside),
    ]
    arrive(strips + relayed)
    for rows, has in ((ABOVE, at.above), (BELOW, at.below)):
        copies.append(send(ext.at[:, near, rows, :], ext.at[:, there, rows, :], at.twin, has, has))
    return copies


def clear_outside(at, ext):
    ext[:, :, 2 * F :, :] = jnp.zeros((2, 4, ROWS - 2 * F, 128), f32)

    @pl.when(at.row == 0)
    def _():
        ext[:, :, :HALF, :] = jnp.zeros((2, 4, HALF, 128), f32)

    @pl.when(at.row == at.n_row - 1)
    def _():
        ext[:, :, F + HALF : 2 * F, :] = jnp.zeros((2, 4, HALF, 128), f32)

    @pl.when(at.col == 0)
    def _():
        ext[:, 0, : 2 * F, :] = jnp.zeros((2, 2 * F, 128), f32)

    @pl.when(at.col == at.n_col - 1)
    def _():
        ext[:, 3, : 2 * F, :] = jnp.zeros((2, 2 * F, 128), f32)


def open_kernel(cells, ext, relay, send_sem, recv_sem):
    at = Places()
    meet((*at.around, *at.along_y[::2], *at.along_z[::2]))
    for part in range(2):
        for j in range(2):
            ext[part, 1 + j, TILE, :] = cells[part, :, 128 * j : 128 * j + 128]
    send = Sender(send_sem, recv_sem)
    arriving, halo = send_halo(send, at, ext, relay)
    halo += pass_on_halo(send, at, ext, relay, arriving)
    arrive(halo)
    send.close()
    clear_outside(at, ext)


def step_kernel(last, grad, psum, old, probe, new, probe_new, *scratch):
    from_up, from_down, sides_in, far_in, side, strips, relay, halo_relay = scratch[:8]
    acc0, buf0, acc1, buf1, acc2, buf2, buf3, send_sem, recv_sem = scratch[8:]
    at = Places()
    meet((*at.around, *at.along_x, *at.along_y, *at.along_z))
    send = Sender(send_sem, recv_sem)
    above, below = at.above, at.below
    up, down = (above, below), (below, above)
    before, after = at.col > 0, at.col < at.n_col - 1
    base = at.core * 128
    base_x = base + at.x * 32
    base_y = base_x + at.y * 8
    near_rim, far_rim = pl.ds(at.near_rim, 1), pl.ds(at.far_rim, 1)
    far_edge = pl.ds(at.far_edge, 1)
    near_part, far_part = pl.ds(at.near_edge - 1, 1), pl.ds(at.far_edge - 1, 1)

    s0 = send(psum.at[:, pl.ds(128 - base, 128), :], buf0, at.twin)
    twins = send(grad.at[:, near_rim, : 2 * F, :], sides_in.at[at.core], at.twin)
    corners = [
        send(grad.at[:, far_rim, ABOVE, :], far_in.at[1], at.up, *up),
        send(grad.at[:, far_rim, BELOW, :], far_in.at[0], at.down, *down),
    ]
    rims = [
        send(grad.at[:, far_edge, ABOVE, :], from_down.at[:, far_part], at.up, *up),
        send(grad.at[:, far_edge, BELOW, :], from_up.at[:, far_part], at.down, *down),
    ]
    arrive([s0])
    acc0[...] = psum[:, pl.ds(base, 128), :] + buf0[...]
    s1 = [
        send(acc0.at[:, pl.ds((at.x + d) % 4 * 32, 32), :], buf1.at[d - 1], at.along_x[d - 1])
        for d in (1, 2, 3)
    ]
    arrive([twins])
    for ch in range(3):
        for k, rows in enumerate((ABOVE, BELOW)):
            strips[k, ch, 0] = grad[ch, at.near_edge, rows, :] + sides_in[1 - at.core, ch, 0, rows, :]

    relays = [
        send(strips.at[0], relay, at.row_first, at.over, at.first),
        send(strips.at[1], relay, at.row_final, at.under, at.final),
    ]

    def send_near():
        rims.extend([
            send(strips.at[0], from_down.at[:, near_part], at.up, above & ~at.over, below & ~at.under),
            send(strips.at[1], from_up.at[:, near_part], at.down, below & ~at.under, above & ~at.over),
        ])

    if not last:
        send_near()

    def send_side():
        rims.append(send(side, sides_in.at[1 - at.core, :, :, INNER, :], at.far, at.aside, at.aside))

    arrive(corners)
    for ch in range(3):
        side[ch, 0, :HALF, :] = grad[ch, at.far_rim, TOP, :] + jnp.where(above, far_in[0, ch, 0], 0.0)
        side[ch, 0, HALF:, :] = grad[ch, at.far_rim, BOTTOM, :] + jnp.where(below, far_in[1, ch, 0], 0.0)
    send_side()
    arrive(s1)
    acc1[...] = acc0[:, pl.ds(at.x * 32, 32), :] + buf1[0] + buf1[1] + buf1[2]
    s2 = [
        send(acc1.at[:, pl.ds((at.y + d) % 4 * 8, 8), :], buf2.at[d - 1], at.along_y[d - 1])
        for d in (1, 2, 3)
    ]
    if last:
        send_near()
    arrive(s2)
    acc2[...] = acc1[:, pl.ds(at.y * 8, 8), :] + buf2[0] + buf2[1] + buf2[2]
    buf3[at.z] = acc2[...]
    s3 = [send(acc2, buf3.at[at.z], at.along_z[d - 1]) for d in (1, 2, 3)]

    arrive(relays)
    rims += [
        send(relay, from_down.at[:, near_part], at.row_under, at.first, at.under),
        send(relay, from_up.at[:, near_part], at.row_over, at.final, at.over),
    ]

    def finish_object():
        arrive(rims)
        for j, beside in enumerate((before, after)):
            for half, (level, rim) in enumerate(((above, from_up), (below, from_down))):
                rows = pl.ds(HALF * half, HALF)
                place = pl.ds(HALF + HALF * half, HALF)
                sums = []
                for ch in range(3):
                    sums.append(
                        grad[ch, 1 + j, place, :]
                        + jnp.where(level, rim[ch, j], 0.0)
                        + jnp.where(beside, sides_in[j, ch, 0, place, :], 0.0)
                    )
                weight = sums[2] + 1.0
                for part in range(2):
                    cells = old[part, 1 + j, place, :] - sums[part] / weight
                    if last:
                        new[part, rows, 128 * j : 128 * j + 128] = cells
                    else:
                        new[part, 1 + j, place, :] = cells

    arrive(s3)
    total = buf3[0] + buf3[1] + buf3[2] + buf3[3]
    mine = pl.ds(base_y, 8)
    probe_new[:, mine, :] = probe[:, mine, :] - total[:2] / (total[2:] + 1.0)
    part = probe_new.at[:, mine, :]
    s4 = [send(part, part, peer) for peer in at.along_y]
    if not last:
        finish_object()
        arriving, halo = send_halo(send, at, new, halo_relay)
    arrive(s4)
    part = probe_new.at[:, pl.ds(base_x, 32), :]
    s5 = [send(part, part, peer) for peer in at.along_x]
    if not last:
        halo += pass_on_halo(send, at, new, halo_relay, arriving)
    arrive(s5)
    part = probe_new.at[:, pl.ds(base, 128), :]
    s6 = send(part, part, at.twin)
    if last:
        finish_object()
    arrive([s6])
    if not last:
        arrive(halo)
    send.close()
    if not last:
        clear_outside(at, new)


VMEM = pl.BlockSpec(memory_space=pltpu.VMEM)
SMEM = pl.BlockSpec(memory_space=pltpu.SMEM)
LIMIT = 20 * 2**20


def open_halo(cells):
    return pl.pallas_call(
        open_kernel,
        out_shape=jax.ShapeDtypeStruct((2, 4, ROWS, 128), f32),
        in_specs=[VMEM],
        out_specs=VMEM,
        scratch_shapes=[
            pltpu.VMEM((2, 1, HALF, 128), f32),
            pltpu.SemaphoreType.DMA((20,)),
            pltpu.SemaphoreType.DMA((20,)),
        ],
        compiler_params=pltpu.CompilerParams(
            collective_id=0, has_side_effects=True, vmem_limit_bytes=LIMIT
        ),
    )(cells)


def step(last, grad, psum, old, probe):
    shape = (2, F, F) if last else (2, 4, ROWS, 128)
    copies = 29 if last else 49
    return pl.pallas_call(
        functools.partial(step_kernel, last),
        out_shape=(jax.ShapeDtypeStruct(shape, f32), jax.ShapeDtypeStruct((2, F, F), f32)),
        in_specs=[VMEM] * 4,
        out_specs=(VMEM, VMEM),
        scratch_shapes=[
            pltpu.VMEM((3, 2, HALF, 128), f32),
            pltpu.VMEM((3, 2, HALF, 128), f32),
            pltpu.VMEM((2, 3, 1, 2 * F, 128), f32),
            pltpu.VMEM((2, 3, 1, HALF, 128), f32),
            pltpu.VMEM((3, 1, F, 128), f32),
            pltpu.VMEM((2, 3, 1, HALF, 128), f32),
            pltpu.VMEM((3, 1, HALF, 128), f32),
            pltpu.VMEM((2, 1, HALF, 128), f32),
            pltpu.VMEM((3, 128, F), f32),
            pltpu.VMEM((3, 128, F), f32),
            pltpu.VMEM((3, 32, F), f32),
            pltpu.VMEM((3, 3, 32, F), f32),
            pltpu.VMEM((3, 8, F), f32),
            pltpu.VMEM((3, 3, 8, F), f32),
            pltpu.VMEM((4, 3, 8, F), f32),
            pltpu.SemaphoreType.DMA((copies,)),
            pltpu.SemaphoreType.DMA((copies,)),
        ],
        compiler_params=pltpu.CompilerParams(
            collective_id=2 if last else 1, has_side_effects=True, vmem_limit_bytes=LIMIT
        ),
    )(grad, psum, old, probe)


def body(positions, counts, amplitudes, object_field, probe):
    fwd, inv = tables()
    corners = positions[0, 0].T
    load = counts[0]
    ext = open_halo(object_field)
    for iteration in range(ITERS):
        grad, psum = slots(corners, load, amplitudes[0, 0], ext, probe, fwd, inv)
        ext, probe = step(iteration == ITERS - 1, grad, psum, ext, probe)
    return ext, probe


def solution(mesh):
    return jax.shard_map(
        body,
        mesh=mesh,
        in_specs=(
            P("row", "col", None, None),
            P("row", "col"),
            P("row", "col", None, None, None),
            P(None, "row", "col"),
            P(),
        ),
        out_specs=(P(None, "row", "col"), P()),
        check_vma=False,
    )
```

```python
import functools, math
import numpy as np
import jax, jax.numpy as jnp
from jax import lax
from jax.experimental import pallas as pl
from jax.experimental.pallas import tpu as pltpu
from jax.sharding import PartitionSpec as P

F = 256
ITERS = 2
f32=jnp.float32; bf16=jnp.bfloat16

def tables():
    c=np.arange(F,dtype=np.int32)
    ang=(c[:,None]*c[None,:]%F).astype(np.float32)*np.float32(2*math.pi/F)
    re=(np.cos(ang)/np.float32(16)).astype(np.float32)
    im=(-np.sin(ang)/np.float32(16)).astype(np.float32)
    fwd=np.block([[re,-im],[im,re]]); inv=np.block([[re,im],[-im,re]])
    return jnp.asarray(fwd,bf16), jnp.asarray(inv,bf16)

CH=16; B=2; ROWS=3*F
def both_sides(table, other, cells):
    re = jnp.dot(table[:F, :], cells[...], preferred_element_type=f32).astype(bf16)
    im = jnp.dot(table[F:, :], cells[...], preferred_element_type=f32).astype(bf16)
    stacked = jnp.concatenate(
        [jnp.concatenate([re[:, F * b : F * b + F], im[:, F * b : F * b + F]], 1) for b in range(B)], 0
    )
    return jnp.dot(stacked, other[...], preferred_element_type=f32)


def slots_kernel(corner, load, amp, ext, probe, fwd, inv, grad, psum,
                 patch0, patch1, cov, exit_s, miss0, miss1, chi_s):
    lane=lax.broadcasted_iota(jnp.int32,(CH,128),1)
    n=load[0]
    top=lax.axis_index("row")*F-F//2; left=lax.axis_index("col")*F-F//2
    def place(k):
        kk=jnp.minimum(k,15)
        live=k<n
        r=jnp.where(live,corner[0,kk]-top,2*F); c=jnp.where(live,corner[1,kk]-left,0)
        q=c//128; s=c-q*128
        return r,q,s,kk
    def front(g,patch,miss):
        for b in range(B):
            r,q,s,kk=place(B*g+b)
            back=jnp.where(s==0,0,128-s)
            keep=lane<128-s
            for i in range(F//CH):
                rows=pl.ds(i*CH,CH)
                got=[]
                for ch in range(2):
                    t=[pltpu.roll(ext[ch,q+j,pl.ds(r+i*CH,CH),:],back,1) for j in range(3)]
                    got.append(jnp.concatenate([jnp.where(keep,t[0],t[1]),jnp.where(keep,t[1],t[2])],1))
                re,im=got
                patch[b,0,rows,:]=re; patch[b,1,rows,:]=im
                pr=probe[0,rows,:]; pi=probe[1,rows,:]
                exit_s[rows,F*b:F*b+F]=(pr*re-pi*im).astype(bf16)
                exit_s[pl.ds(F+i*CH,CH),F*b:F*b+F]=(pr*im+pi*re).astype(bf16)
        far=both_sides(fwd,inv,exit_s)
        for b in range(B):
            kk=jnp.minimum(B*g+b,15)
            fr=far[F*b:F*b+F,:F]; fi=far[F*b:F*b+F,F:]
            ratio=1.0-amp[kk].astype(f32)*lax.rsqrt(fr*fr+fi*fi+1.0)
            miss[:F,F*b:F*b+F]=(fr*ratio).astype(bf16)
            miss[F:,F*b:F*b+F]=(fi*ratio).astype(bf16)
    def back_(g,patch,miss):
        chi=both_sides(inv,fwd,miss)
        chi_s[...]=chi
        for i in range(F//CH):
            rows=pl.ds(i*CH,CH)
            pr=probe[0,rows,:]; pi=probe[1,rows,:]
            p0=p1=p2=0.0
            for b in range(B):
                at_=pl.ds(F*b+i*CH,CH)
                cr=chi_s[at_,:F]; ci=chi_s[at_,F:]
                re=patch[b,0,rows,:]; im=patch[b,1,rows,:]
                p0+=re*cr+im*ci; p1+=re*ci-im*cr; p2+=re*re+im*im
            psum[0,rows,:]+=p0; psum[1,rows,:]+=p1; psum[2,rows,:]+=p2
        for b in range(B):
            r,q,s,kk=place(B*g+b)
            put=lane>=s
            for i in range(F//CH):
                rows=pl.ds(i*CH,CH); at_=pl.ds(F*b+i*CH,CH)
                cr=chi_s[at_,:F]; ci=chi_s[at_,F:]
                pr=probe[0,rows,:]; pi=probe[1,rows,:]
                for ch,u in ((0,pr*cr+pi*ci),(1,pr*ci-pi*cr),(2,cov[rows,:])):
                    u0=pltpu.roll(u[:,:128],s,1); u1=pltpu.roll(u[:,128:],s,1)
                    at=pl.ds(r+i*CH,CH)
                    grad[ch,q,at,:]+=jnp.where(put,u0,0.0)
                    grad[ch,q+1,at,:]+=jnp.where(put,u1,u0)
                    grad[ch,q+2,at,:]+=jnp.where(put,0.0,u1)
    for ch in range(3):
        for j in range(4):
            grad[ch,j,:2*F,:]=jnp.zeros((2*F,128),f32)
    psum[...]=jnp.zeros(psum.shape,f32)
    cov[...]=probe[0]*probe[0]+probe[1]*probe[1]
    front(0,patch0,miss0)
    pairs=(n+2*B-1)//(2*B)
    def it(j,_):
        back_(2*j,patch0,miss0)
        front(2*j+1,patch1,miss1)
        back_(2*j+1,patch1,miss1)
        front(2*j+2,patch0,miss0)
        return 0
    lax.fori_loop(0,pairs,it,0)
def slots(corner,load,amp,ext,probe,fwd,inv):
    V=pl.BlockSpec(memory_space=pltpu.VMEM); S=pl.BlockSpec(memory_space=pltpu.SMEM)
    return pl.pallas_call(slots_kernel,
        out_shape=(jax.ShapeDtypeStruct((3,4,ROWS,128),f32),jax.ShapeDtypeStruct((3,F,F),f32)),
        in_specs=[S,S,V,V,V,V,V], out_specs=(V,V),
        scratch_shapes=[pltpu.VMEM((B,2,F,F),f32),pltpu.VMEM((B,2,F,F),f32),pltpu.VMEM((F,F),f32),pltpu.VMEM((2*F,B*F),bf16),
            pltpu.VMEM((2*F,B*F),bf16),pltpu.VMEM((2*F,B*F),bf16),pltpu.VMEM((B*F,2*F),f32)],
        compiler_params=pltpu.CompilerParams(vmem_limit_bytes=24*2**20),
    )(corner,load,amp,ext,probe,fwd,inv)


MESH = pl.DeviceIdType.MESH
HALF = F // 2
TILE = slice(HALF, HALF + F)


TOP, BOTTOM = pl.ds(HALF, HALF), pl.ds(F, HALF)
ABOVE, BELOW = pl.ds(0, HALF), pl.ds(F + HALF, HALF)


class Places:
    def __init__(self):
        row, col = lax.axis_index("row"), lax.axis_index("col")
        n_row, n_col = lax.axis_size("row"), lax.axis_size("col")
        self.row, self.col, self.n_row, self.n_col = row, col, n_row, n_col
        z_lo, self.y = row // 4, row % 4
        self.x, z_hi, self.core = col // 4, col // 2 % 2, col % 2
        self.z = z_hi * 2 + z_lo
        self.up, self.down = ((row + n_row - 1) % n_row, col), ((row + 1) % n_row, col)
        self.twin = (row, col + 1 - 2 * self.core)
        self.far = (row, (col + n_col - 1 + 2 * self.core) % n_col)
        self.near_north, self.near_south = (self.up[0], self.twin[1]), (self.down[0], self.twin[1])
        self.far_north, self.far_south = (self.up[0], self.far[1]), (self.down[0], self.far[1])
        self.around = (
            self.up, self.down, self.twin, self.far,
            self.near_north, self.near_south, self.far_north, self.far_south,
        )
        self.above, self.below = row > 0, row < n_row - 1
        self.aside = (col > 0) & (col < n_col - 1)
        self.over, self.under = row == n_row // 2, row == n_row // 2 - 1
        self.first, self.final = row == 0, row == n_row - 1
        self.row_first, self.row_final = (0 * row, col), (0 * row + n_row - 1, col)
        self.row_under, self.row_over = (0 * row + n_row // 2 - 1, col), (0 * row + n_row // 2, col)
        self.near_rim, self.far_rim = 3 - 3 * self.core, 3 * self.core
        self.near_edge, self.far_edge = 2 - self.core, 1 + self.core
        self.along_x = [(row, (self.x + d) % 4 * 4 + col % 4) for d in (1, 2, 3)]
        self.along_y = [(z_lo * 4 + (self.y + d) % 4, col) for d in (1, 2, 3)]
        self.along_z = []
        for d in (1, 2, 3):
            z = (self.z + d) % 4
            self.along_z.append((z % 2 * 4 + self.y, self.x * 4 + z // 2 * 2 + self.core))


def meet(peers):
    barrier = pltpu.get_barrier_semaphore()
    for peer in peers:
        pl.semaphore_signal(barrier, inc=1, device_id=peer, device_id_type=MESH)
    pl.semaphore_wait(barrier, len(peers))


def run_if(condition, action):
    if condition is None:
        action()
    else:
        pl.when(condition)(action)


class Sender:
    def __init__(self, send_sem, recv_sem):
        self.send_sem, self.recv_sem, self.used = send_sem, recv_sem, 0
        self.open = []

    def __call__(self, src, dst, peer, sends=None, gets=None):
        copy = pltpu.make_async_remote_copy(
            src_ref=src,
            dst_ref=dst,
            send_sem=self.send_sem.at[self.used],
            recv_sem=self.recv_sem.at[self.used],
            device_id=peer,
            device_id_type=MESH,
        )
        self.used += 1
        run_if(sends, copy.start)
        self.open.append((copy, sends))
        return copy, gets

    def close(self):
        for copy, sends in self.open:
            run_if(sends, copy.wait_send)


def arrive(copies):
    for copy, gets in copies:
        run_if(gets, copy.wait_recv)


INNER = pl.ds(HALF, F)
BOTH = pl.ds(1, 2)


def send_far_halo(send, at, ext):
    far, there = pl.ds(at.far_edge, 1), pl.ds(at.near_rim, 1)
    up, down, aside = (at.above, at.below), (at.below, at.above), (at.aside, at.aside)
    up_aside, down_aside = (at.above & at.aside, at.below & at.aside), (at.below & at.aside, at.above & at.aside)
    real, imag = pl.ds(0, 1), pl.ds(1, 1)
    return [send(ext.at[imag, far, INNER, :], ext.at[imag, there, INNER, :], at.far, *aside)], [
        send(ext.at[real, far, INNER, :], ext.at[real, there, INNER, :], at.far, *aside),
        send(ext.at[:, far, TOP, :], ext.at[:, far, BELOW, :], at.up, *up),
        send(ext.at[:, far, BOTTOM, :], ext.at[:, far, ABOVE, :], at.down, *down),
        send(ext.at[real, far, TOP, :], ext.at[real, there, BELOW, :], at.far_north, *up_aside),
        send(ext.at[real, far, BOTTOM, :], ext.at[real, there, ABOVE, :], at.far_south, *down_aside),
    ]


def send_near_halo(send, at, ext, relay):
    near, there = pl.ds(at.near_edge, 1), pl.ds(at.far_rim, 1)
    up, down = (at.above, at.below), (at.below, at.above)
    up_near = (at.above & ~at.over, at.below & ~at.under)
    down_near = (at.below & ~at.under, at.above & ~at.over)
    real, imag = pl.ds(0, 1), pl.ds(1, 1)
    relays = [
        send(ext.at[real, near, TOP, :], relay, at.row_first, at.over, at.first),
        send(ext.at[real, near, BOTTOM, :], relay, at.row_final, at.under, at.final),
    ]
    strips = [
        send(ext.at[imag, near, TOP, :], ext.at[imag, near, BELOW, :], at.up, *up),
        send(ext.at[imag, near, BOTTOM, :], ext.at[imag, near, ABOVE, :], at.down, *down),
        send(ext.at[real, near, TOP, :], ext.at[real, near, BELOW, :], at.up, *up_near),
        send(ext.at[real, near, BOTTOM, :], ext.at[real, near, ABOVE, :], at.down, *down_near),
    ]
    return relays, strips, [send(ext.at[:, near, INNER, :], ext.at[:, there, INNER, :], at.twin)]


def pass_on_halo(send, at, ext, relay, arriving):
    relays, side, strips = arriving
    near, far, there = pl.ds(at.near_edge, 1), pl.ds(at.far_rim, 1), pl.ds(at.far_rim, 1)
    real, imag = pl.ds(0, 1), pl.ds(1, 1)
    up_aside, down_aside = (at.above & at.aside, at.below & at.aside), (at.below & at.aside, at.above & at.aside)
    copies, relayed = [], []
    arrive(relays)
    for (row, col), rows, sends, gets in (
        (at.row_under, BELOW, at.first, at.under),
        (at.row_over, ABOVE, at.final, at.over),
    ):
        relayed.append(send(relay, ext.at[real, near, rows, :], (row, col), sends, gets))
    arrive(side)
    copies += [
        send(ext.at[imag, far, TOP, :], ext.at[imag, far, BELOW, :], at.up, *up_aside),
        send(ext.at[imag, far, BOTTOM, :], ext.at[imag, far, ABOVE, :], at.down, *down_aside),
    ]
    arrive(strips + relayed)
    for rows, has in ((ABOVE, at.above), (BELOW, at.below)):
        copies.append(send(ext.at[:, near, rows, :], ext.at[:, there, rows, :], at.twin, has, has))
    return copies


def clear_outside(at, ext):
    ext[:, :, 2 * F :, :] = jnp.zeros((2, 4, ROWS - 2 * F, 128), f32)

    @pl.when(at.row == 0)
    def _():
        ext[:, :, :HALF, :] = jnp.zeros((2, 4, HALF, 128), f32)

    @pl.when(at.row == at.n_row - 1)
    def _():
        ext[:, :, F + HALF : 2 * F, :] = jnp.zeros((2, 4, HALF, 128), f32)

    @pl.when(at.col == 0)
    def _():
        ext[:, 0, : 2 * F, :] = jnp.zeros((2, 2 * F, 128), f32)

    @pl.when(at.col == at.n_col - 1)
    def _():
        ext[:, 3, : 2 * F, :] = jnp.zeros((2, 2 * F, 128), f32)


def open_kernel(cells, ext, relay, send_sem, recv_sem):
    at = Places()
    meet((*at.around, *at.along_y[::2], *at.along_z[::2]))
    for part in range(2):
        for j in range(2):
            ext[part, 1 + j, TILE, :] = cells[part, :, 128 * j : 128 * j + 128]
    send = Sender(send_sem, recv_sem)
    relays, strips, rest = send_near_halo(send, at, ext, relay)
    side, halo = send_far_halo(send, at, ext)
    halo += rest + pass_on_halo(send, at, ext, relay, (relays, side, strips))
    arrive(halo)
    send.close()
    clear_outside(at, ext)


def step_kernel(last, grad, psum, old, probe, new, probe_new, *scratch):
    from_up, from_down, sides_in, far_in, side, strips, relay, halo_relay = scratch[:8]
    acc0, buf0, acc1, buf1, acc2, buf2, buf3, send_sem, recv_sem = scratch[8:]
    at = Places()
    meet((*at.around, *at.along_x, *at.along_y, *at.along_z))
    send = Sender(send_sem, recv_sem)
    above, below = at.above, at.below
    up, down = (above, below), (below, above)
    base = at.core * 128
    base_x = base + at.x * 32
    base_y = base_x + at.y * 8
    near_rim, far_rim = pl.ds(at.near_rim, 1), pl.ds(at.far_rim, 1)
    far_edge = pl.ds(at.far_edge, 1)
    near_part, far_part = pl.ds(at.near_edge - 1, 1), pl.ds(at.far_edge - 1, 1)

    s0 = send(psum.at[:, pl.ds(128 - base, 128), :], buf0, at.twin)
    twins = send(grad.at[:, near_rim, : 2 * F, :], sides_in.at[at.core], at.twin)
    corners = [
        [
            send(grad.at[pl.ds(ch, 1), far_rim, ABOVE, :], far_in.at[1, pl.ds(ch, 1)], at.up, *up),
            send(grad.at[pl.ds(ch, 1), far_rim, BELOW, :], far_in.at[0, pl.ds(ch, 1)], at.down, *down),
        ]
        for ch in range(3)
    ]
    near_rims = []
    rims = [
        send(grad.at[:, far_edge, ABOVE, :], from_down.at[:, far_part], at.up, *up),
        send(grad.at[:, far_edge, BELOW, :], from_up.at[:, far_part], at.down, *down),
    ]
    arrive([s0])
    acc0[...] = psum[:, pl.ds(base, 128), :] + buf0[...]
    s1 = [
        send(acc0.at[:, pl.ds((at.x + d) % 4 * 32, 32), :], buf1.at[d - 1], at.along_x[d - 1])
        for d in (1, 2, 3)
    ]
    arrive([twins])
    for ch in range(3):
        for k, rows in enumerate((ABOVE, BELOW)):
            strips[k, ch, 0] = grad[ch, at.near_edge, rows, :] + sides_in[1 - at.core, ch, 0, rows, :]

    relays = [
        send(strips.at[0], relay, at.row_first, at.over, at.first),
        send(strips.at[1], relay, at.row_final, at.under, at.final),
    ]

    def send_near():
        near_rims.extend([
            send(strips.at[0], from_down.at[:, near_part], at.up, above & ~at.over, below & ~at.under),
            send(strips.at[1], from_up.at[:, near_part], at.down, below & ~at.under, above & ~at.over),
        ])

    if not last:
        send_near()

    for ch in range(3):
        arrive(corners[ch])
        side[ch, 0, :HALF, :] = grad[ch, at.far_rim, TOP, :] + jnp.where(above, far_in[0, ch, 0], 0.0)
        side[ch, 0, HALF:, :] = grad[ch, at.far_rim, BOTTOM, :] + jnp.where(below, far_in[1, ch, 0], 0.0)
        there = sides_in.at[1 - at.core, pl.ds(ch, 1), :, INNER, :]
        rims.append(send(side.at[pl.ds(ch, 1)], there, at.far, at.aside, at.aside))
    arrive(s1)
    acc1[...] = acc0[:, pl.ds(at.x * 32, 32), :] + buf1[0] + buf1[1] + buf1[2]
    s2 = [
        send(acc1.at[:, pl.ds((at.y + d) % 4 * 8, 8), :], buf2.at[d - 1], at.along_y[d - 1])
        for d in (1, 2, 3)
    ]
    if last:
        send_near()
    arrive(s2)
    acc2[...] = acc1[:, pl.ds(at.y * 8, 8), :] + buf2[0] + buf2[1] + buf2[2]
    buf3[at.z] = acc2[...]
    s3 = [send(acc2, buf3.at[at.z], at.along_z[d - 1]) for d in (1, 2, 3)]

    arrive(relays)
    near_rims += [
        send(relay, from_down.at[:, near_part], at.row_under, at.first, at.under),
        send(relay, from_up.at[:, near_part], at.row_over, at.final, at.over),
    ]

    def finish(tile, beside):
        for half, (level, rim) in enumerate(((above, from_up), (below, from_down))):
            rows = pl.ds(HALF * half, HALF)
            place = pl.ds(HALF + HALF * half, HALF)
            sums = []
            for ch in range(3):
                rims_sum = jnp.where(level, rim[ch, tile - 1], 0.0) + beside(ch, place)
                sums.append(grad[ch, tile, place, :] + rims_sum)
            share = 1.0 / (sums[2] + 1.0)
            for part in range(2):
                cells = old[part, tile, place, :] - sums[part] * share
                if last:
                    columns = pl.ds(pl.multiple_of(128 * (tile - 1), 128), 128)
                    new[part, rows, columns] = cells
                else:
                    new[part, tile, place, :] = cells

    def finish_far():
        arrive(rims)
        finish(at.far_edge, lambda ch, place: jnp.where(at.aside, sides_in[at.core, ch, 0, place, :], 0.0))

    def finish_near():
        arrive(near_rims)
        finish(at.near_edge, lambda ch, place: sides_in[1 - at.core, ch, 0, place, :])

    arrive(s3)
    total = buf3[0] + buf3[1] + buf3[2] + buf3[3]
    mine = pl.ds(base_y, 8)
    probe_new[:, mine, :] = probe[:, mine, :] - total[:2] / (total[2:] + 1.0)
    part = probe_new.at[:, mine, :]
    s4 = [send(part, part, peer) for peer in at.along_y]
    if not last:
        finish_far()
        passing, halo = send_far_halo(send, at, new)
        finish_near()
        relays, strips_out, rest = send_near_halo(send, at, new, halo_relay)
        arriving, halo = (relays, passing, strips_out), halo + rest
    arrive(s4)
    part = probe_new.at[:, pl.ds(base_x, 32), :]
    s5 = [send(part, part, peer) for peer in at.along_x]
    if not last:
        halo += pass_on_halo(send, at, new, halo_relay, arriving)
    arrive(s5)
    part = probe_new.at[:, pl.ds(base, 128), :]
    s6 = send(part, part, at.twin)
    if last:
        finish_far()
        finish_near()
    arrive([s6])
    if not last:
        arrive(halo)
    send.close()
    if not last:
        clear_outside(at, new)


VMEM = pl.BlockSpec(memory_space=pltpu.VMEM)
SMEM = pl.BlockSpec(memory_space=pltpu.SMEM)
LIMIT = 20 * 2**20


def open_halo(cells):
    return pl.pallas_call(
        open_kernel,
        out_shape=jax.ShapeDtypeStruct((2, 4, ROWS, 128), f32),
        in_specs=[VMEM],
        out_specs=VMEM,
        scratch_shapes=[
            pltpu.VMEM((1, 1, HALF, 128), f32),
            pltpu.SemaphoreType.DMA((22,)),
            pltpu.SemaphoreType.DMA((22,)),
        ],
        compiler_params=pltpu.CompilerParams(
            collective_id=0, has_side_effects=True, vmem_limit_bytes=LIMIT
        ),
    )(cells)


def step(last, grad, psum, old, probe):
    shape = (2, F, F) if last else (2, 4, ROWS, 128)
    copies = 35 if last else 57
    return pl.pallas_call(
        functools.partial(step_kernel, last),
        out_shape=(jax.ShapeDtypeStruct(shape, f32), jax.ShapeDtypeStruct((2, F, F), f32)),
        in_specs=[VMEM] * 4,
        out_specs=(VMEM, VMEM),
        scratch_shapes=[
            pltpu.VMEM((3, 2, HALF, 128), f32),
            pltpu.VMEM((3, 2, HALF, 128), f32),
            pltpu.VMEM((2, 3, 1, 2 * F, 128), f32),
            pltpu.VMEM((2, 3, 1, HALF, 128), f32),
            pltpu.VMEM((3, 1, F, 128), f32),
            pltpu.VMEM((2, 3, 1, HALF, 128), f32),
            pltpu.VMEM((3, 1, HALF, 128), f32),
            pltpu.VMEM((1, 1, HALF, 128), f32),
            pltpu.VMEM((3, 128, F), f32),
            pltpu.VMEM((3, 128, F), f32),
            pltpu.VMEM((3, 32, F), f32),
            pltpu.VMEM((3, 3, 32, F), f32),
            pltpu.VMEM((3, 8, F), f32),
            pltpu.VMEM((3, 3, 8, F), f32),
            pltpu.VMEM((4, 3, 8, F), f32),
            pltpu.SemaphoreType.DMA((copies,)),
            pltpu.SemaphoreType.DMA((copies,)),
        ],
        compiler_params=pltpu.CompilerParams(
            collective_id=2 if last else 1, has_side_effects=True, vmem_limit_bytes=LIMIT
        ),
    )(grad, psum, old, probe)


def body(positions, counts, amplitudes, object_field, probe):
    fwd, inv = tables()
    corners = positions[0, 0].T
    load = counts[0]
    ext = open_halo(object_field)
    for iteration in range(ITERS):
        grad, psum = slots(corners, load, amplitudes[0, 0], ext, probe, fwd, inv)
        ext, probe = step(iteration == ITERS - 1, grad, psum, ext, probe)
    return ext, probe


def solution(mesh):
    return jax.shard_map(
        body,
        mesh=mesh,
        in_specs=(
            P("row", "col", None, None),
            P("row", "col"),
            P("row", "col", None, None, None),
            P(None, "row", "col"),
            P(),
        ),
        out_specs=(P(None, "row", "col"), P()),
        check_vma=False,
    )
```

```python
import functools, math
import numpy as np
import jax, jax.numpy as jnp
from jax import lax
from jax.experimental import pallas as pl
from jax.experimental.pallas import tpu as pltpu
from jax.sharding import PartitionSpec as P

F = 256
ITERS = 2
f32=jnp.float32; bf16=jnp.bfloat16

def tables():
    c=np.arange(F,dtype=np.int32)
    ang=(c[:,None]*c[None,:]%F).astype(np.float32)*np.float32(2*math.pi/F)
    re=(np.cos(ang)/np.float32(16)).astype(np.float32)
    im=(-np.sin(ang)/np.float32(16)).astype(np.float32)
    fwd=np.block([[re,-im],[im,re]]); inv=np.block([[re,im],[-im,re]])
    return jnp.asarray(fwd,bf16), jnp.asarray(inv,bf16)

CH=16; B=2; ROWS=3*F
def both_sides(table, other, cells, half):
    left = jnp.dot(table[...], cells[...], preferred_element_type=f32).astype(bf16)
    for b in range(B):
        half[F * b : F * b + F, :F] = left[:F, F * b : F * b + F]
        half[F * b : F * b + F, F:] = left[F:, F * b : F * b + F]
    return jnp.dot(half[...], other[...], preferred_element_type=f32)


def slots_kernel(corner, load, amp, ext, probe, fwd, inv, grad, psum,
                 patch0, patch1, cov, exit_s, half0, half1, miss0, miss1, chi_s):
    lane=lax.broadcasted_iota(jnp.int32,(CH,128),1)
    n=load[0]
    top=lax.axis_index("row")*F-F//2; left=lax.axis_index("col")*F-F//2
    def place(k):
        kk=jnp.minimum(k,15)
        live=k<n
        r=jnp.where(live,corner[0,kk]-top,2*F); c=jnp.where(live,corner[1,kk]-left,0)
        q=c//128; s=c-q*128
        return r,q,s,kk
    def front(g,patch,miss):
        for b in range(B):
            r,q,s,kk=place(B*g+b)
            back=jnp.where(s==0,0,128-s)
            keep=lane<128-s
            for i in range(F//CH):
                rows=pl.ds(i*CH,CH)
                got=[]
                for ch in range(2):
                    t=[pltpu.roll(ext[ch,q+j,pl.ds(r+i*CH,CH),:],back,1) for j in range(3)]
                    got.append(jnp.concatenate([jnp.where(keep,t[0],t[1]),jnp.where(keep,t[1],t[2])],1))
                re,im=got
                patch[b,0,rows,:]=re; patch[b,1,rows,:]=im
                pr=probe[0,rows,:]; pi=probe[1,rows,:]
                exit_s[rows,F*b:F*b+F]=(pr*re-pi*im).astype(bf16)
                exit_s[pl.ds(F+i*CH,CH),F*b:F*b+F]=(pr*im+pi*re).astype(bf16)
        far=both_sides(fwd,inv,exit_s,half0)
        for b in range(B):
            kk=jnp.minimum(B*g+b,15)
            fr=far[F*b:F*b+F,:F]; fi=far[F*b:F*b+F,F:]
            ratio=1.0-amp[kk].astype(f32)*lax.rsqrt(fr*fr+fi*fi+1.0)
            miss[:F,F*b:F*b+F]=(fr*ratio).astype(bf16)
            miss[F:,F*b:F*b+F]=(fi*ratio).astype(bf16)
    def back_(g,patch,miss):
        chi=both_sides(inv,fwd,miss,half1)
        chi_s[...]=chi
        for i in range(F//CH):
            rows=pl.ds(i*CH,CH)
            pr=probe[0,rows,:]; pi=probe[1,rows,:]
            p0=p1=p2=0.0
            for b in range(B):
                at_=pl.ds(F*b+i*CH,CH)
                cr=chi_s[at_,:F]; ci=chi_s[at_,F:]
                re=patch[b,0,rows,:]; im=patch[b,1,rows,:]
                p0+=re*cr+im*ci; p1+=re*ci-im*cr; p2+=re*re+im*im
            psum[0,rows,:]+=p0; psum[1,rows,:]+=p1; psum[2,rows,:]+=p2
        for b in range(B):
            r,q,s,kk=place(B*g+b)
            put=lane>=s
            for i in range(F//CH):
                rows=pl.ds(i*CH,CH); at_=pl.ds(F*b+i*CH,CH)
                cr=chi_s[at_,:F]; ci=chi_s[at_,F:]
                pr=probe[0,rows,:]; pi=probe[1,rows,:]
                for ch,u in ((0,pr*cr+pi*ci),(1,pr*ci-pi*cr),(2,cov[rows,:])):
                    u0=pltpu.roll(u[:,:128],s,1); u1=pltpu.roll(u[:,128:],s,1)
                    at=pl.ds(r+i*CH,CH)
                    grad[ch,q,at,:]+=jnp.where(put,u0,0.0)
                    grad[ch,q+1,at,:]+=jnp.where(put,u1,u0)
                    grad[ch,q+2,at,:]+=jnp.where(put,0.0,u1)
    for ch in range(3):
        for j in range(4):
            grad[ch,j,:2*F,:]=jnp.zeros((2*F,128),f32)
    psum[...]=jnp.zeros(psum.shape,f32)
    cov[...]=probe[0]*probe[0]+probe[1]*probe[1]
    front(0,patch0,miss0)
    pairs=(n+2*B-1)//(2*B)
    def it(j,_):
        back_(2*j,patch0,miss0)
        front(2*j+1,patch1,miss1)
        back_(2*j+1,patch1,miss1)
        front(2*j+2,patch0,miss0)
        return 0
    lax.fori_loop(0,pairs-1,it,0)
    back_(2*pairs-2,patch0,miss0)
    front(2*pairs-1,patch1,miss1)
    back_(2*pairs-1,patch1,miss1)
def slots(corner,load,amp,ext,probe,fwd,inv):
    V=pl.BlockSpec(memory_space=pltpu.VMEM); S=pl.BlockSpec(memory_space=pltpu.SMEM)
    return pl.pallas_call(slots_kernel,
        out_shape=(jax.ShapeDtypeStruct((3,4,ROWS,128),f32),jax.ShapeDtypeStruct((3,F,F),f32)),
        in_specs=[S,S,V,V,V,V,V], out_specs=(V,V),
        scratch_shapes=[pltpu.VMEM((B,2,F,F),f32),pltpu.VMEM((B,2,F,F),f32),pltpu.VMEM((F,F),f32),pltpu.VMEM((2*F,B*F),bf16),
            pltpu.VMEM((B*F,2*F),bf16),pltpu.VMEM((B*F,2*F),bf16),
            pltpu.VMEM((2*F,B*F),bf16),pltpu.VMEM((2*F,B*F),bf16),pltpu.VMEM((B*F,2*F),f32)],
        compiler_params=pltpu.CompilerParams(vmem_limit_bytes=24*2**20),
    )(corner,load,amp,ext,probe,fwd,inv)


MESH = pl.DeviceIdType.MESH
HALF = F // 2
TILE = slice(HALF, HALF + F)


TOP, BOTTOM = pl.ds(HALF, HALF), pl.ds(F, HALF)
ABOVE, BELOW = pl.ds(0, HALF), pl.ds(F + HALF, HALF)


class Places:
    def __init__(self):
        row, col = lax.axis_index("row"), lax.axis_index("col")
        n_row, n_col = lax.axis_size("row"), lax.axis_size("col")
        self.row, self.col, self.n_row, self.n_col = row, col, n_row, n_col
        z_lo, self.y = row // 4, row % 4
        self.x, z_hi, self.core = col // 4, col // 2 % 2, col % 2
        self.z = z_hi * 2 + z_lo
        self.up, self.down = ((row + n_row - 1) % n_row, col), ((row + 1) % n_row, col)
        self.twin = (row, col + 1 - 2 * self.core)
        self.far = (row, (col + n_col - 1 + 2 * self.core) % n_col)
        self.near_north, self.near_south = (self.up[0], self.twin[1]), (self.down[0], self.twin[1])
        self.far_north, self.far_south = (self.up[0], self.far[1]), (self.down[0], self.far[1])
        self.around = (
            self.up, self.down, self.twin, self.far,
            self.near_north, self.near_south, self.far_north, self.far_south,
        )
        self.above, self.below = row > 0, row < n_row - 1
        self.aside = (col > 0) & (col < n_col - 1)
        self.over, self.under = row == n_row // 2, row == n_row // 2 - 1
        self.first, self.final = row == 0, row == n_row - 1
        self.row_first, self.row_final = (0 * row, col), (0 * row + n_row - 1, col)
        self.row_under, self.row_over = (0 * row + n_row // 2 - 1, col), (0 * row + n_row // 2, col)
        self.near_rim, self.far_rim = 3 - 3 * self.core, 3 * self.core
        self.near_edge, self.far_edge = 2 - self.core, 1 + self.core
        self.along_x = [(row, (self.x + d) % 4 * 4 + col % 4) for d in (1, 2, 3)]
        self.along_y = [(z_lo * 4 + (self.y + d) % 4, col) for d in (1, 2, 3)]
        self.along_z = []
        for d in (1, 2, 3):
            z = (self.z + d) % 4
            self.along_z.append((z % 2 * 4 + self.y, self.x * 4 + z // 2 * 2 + self.core))


def meet(peers):
    barrier = pltpu.get_barrier_semaphore()
    for peer in peers:
        pl.semaphore_signal(barrier, inc=1, device_id=peer, device_id_type=MESH)
    pl.semaphore_wait(barrier, len(peers))


def run_if(condition, action):
    if condition is None:
        action()
    else:
        pl.when(condition)(action)


class Sender:
    def __init__(self, send_sem, recv_sem):
        self.send_sem, self.recv_sem, self.used = send_sem, recv_sem, 0
        self.open = []

    def __call__(self, src, dst, peer, sends=None, gets=None):
        copy = pltpu.make_async_remote_copy(
            src_ref=src,
            dst_ref=dst,
            send_sem=self.send_sem.at[self.used],
            recv_sem=self.recv_sem.at[self.used],
            device_id=peer,
            device_id_type=MESH,
        )
        self.used += 1
        run_if(sends, copy.start)
        self.open.append((copy, sends))
        return copy, gets

    def close(self):
        for copy, sends in self.open:
            run_if(sends, copy.wait_send)


def arrive(copies):
    for copy, gets in copies:
        run_if(gets, copy.wait_recv)


INNER = pl.ds(HALF, F)
BOTH = pl.ds(1, 2)


def send_far_halo(send, at, ext):
    far, there = pl.ds(at.far_edge, 1), pl.ds(at.near_rim, 1)
    up, down, aside = (at.above, at.below), (at.below, at.above), (at.aside, at.aside)
    up_aside, down_aside = (at.above & at.aside, at.below & at.aside), (at.below & at.aside, at.above & at.aside)
    real, imag = pl.ds(0, 1), pl.ds(1, 1)
    return [send(ext.at[imag, far, INNER, :], ext.at[imag, there, INNER, :], at.far, *aside)], [
        send(ext.at[real, far, INNER, :], ext.at[real, there, INNER, :], at.far, *aside),
        send(ext.at[:, far, TOP, :], ext.at[:, far, BELOW, :], at.up, *up),
        send(ext.at[:, far, BOTTOM, :], ext.at[:, far, ABOVE, :], at.down, *down),
        send(ext.at[real, far, TOP, :], ext.at[real, there, BELOW, :], at.far_north, *up_aside),
        send(ext.at[real, far, BOTTOM, :], ext.at[real, there, ABOVE, :], at.far_south, *down_aside),
    ]


def send_near_halo(send, at, ext, relay):
    near, there = pl.ds(at.near_edge, 1), pl.ds(at.far_rim, 1)
    up, down = (at.above, at.below), (at.below, at.above)
    up_near = (at.above & ~at.over, at.below & ~at.under)
    down_near = (at.below & ~at.under, at.above & ~at.over)
    real, imag = pl.ds(0, 1), pl.ds(1, 1)
    relays = [
        send(ext.at[real, near, TOP, :], relay, at.row_first, at.over, at.first),
        send(ext.at[real, near, BOTTOM, :], relay, at.row_final, at.under, at.final),
    ]
    strips = [
        send(ext.at[imag, near, TOP, :], ext.at[imag, near, BELOW, :], at.up, *up),
        send(ext.at[imag, near, BOTTOM, :], ext.at[imag, near, ABOVE, :], at.down, *down),
        send(ext.at[real, near, TOP, :], ext.at[real, near, BELOW, :], at.up, *up_near),
        send(ext.at[real, near, BOTTOM, :], ext.at[real, near, ABOVE, :], at.down, *down_near),
    ]
    return relays, strips, [send(ext.at[:, near, INNER, :], ext.at[:, there, INNER, :], at.twin)]


def pass_on_halo(send, at, ext, relay, arriving):
    relays, side, strips = arriving
    near, far, there = pl.ds(at.near_edge, 1), pl.ds(at.far_rim, 1), pl.ds(at.far_rim, 1)
    real, imag = pl.ds(0, 1), pl.ds(1, 1)
    up_aside, down_aside = (at.above & at.aside, at.below & at.aside), (at.below & at.aside, at.above & at.aside)
    copies, relayed = [], []
    arrive(relays)
    for (row, col), rows, sends, gets in (
        (at.row_under, BELOW, at.first, at.under),
        (at.row_over, ABOVE, at.final, at.over),
    ):
        relayed.append(send(relay, ext.at[real, near, rows, :], (row, col), sends, gets))
    arrive(side)
    copies += [
        send(ext.at[imag, far, TOP, :], ext.at[imag, far, BELOW, :], at.up, *up_aside),
        send(ext.at[imag, far, BOTTOM, :], ext.at[imag, far, ABOVE, :], at.down, *down_aside),
    ]
    arrive(strips + relayed)
    for rows, has in ((ABOVE, at.above), (BELOW, at.below)):
        copies.append(send(ext.at[:, near, rows, :], ext.at[:, there, rows, :], at.twin, has, has))
    return copies


def clear_outside(at, ext):
    ext[:, :, 2 * F :, :] = jnp.zeros((2, 4, ROWS - 2 * F, 128), f32)

    @pl.when(at.row == 0)
    def _():
        ext[:, :, :HALF, :] = jnp.zeros((2, 4, HALF, 128), f32)

    @pl.when(at.row == at.n_row - 1)
    def _():
        ext[:, :, F + HALF : 2 * F, :] = jnp.zeros((2, 4, HALF, 128), f32)

    @pl.when(at.col == 0)
    def _():
        ext[:, 0, : 2 * F, :] = jnp.zeros((2, 2 * F, 128), f32)

    @pl.when(at.col == at.n_col - 1)
    def _():
        ext[:, 3, : 2 * F, :] = jnp.zeros((2, 2 * F, 128), f32)


def open_kernel(cells, ext, relay, send_sem, recv_sem):
    at = Places()
    meet((*at.around, *at.along_y[::2], *at.along_z[::2]))
    for part in range(2):
        for j in range(2):
            ext[part, 1 + j, TILE, :] = cells[part, :, 128 * j : 128 * j + 128]
    send = Sender(send_sem, recv_sem)
    relays, strips, rest = send_near_halo(send, at, ext, relay)
    side, halo = send_far_halo(send, at, ext)
    halo += rest + pass_on_halo(send, at, ext, relay, (relays, side, strips))
    arrive(halo)
    send.close()
    clear_outside(at, ext)


def step_kernel(last, grad, psum, old, probe, new, probe_new, *scratch):
    from_up, from_down, sides_in, far_in, side, strips, relay, halo_relay = scratch[:8]
    acc0, buf0, acc1, buf1, acc2, buf2, buf3, send_sem, recv_sem = scratch[8:]
    at = Places()
    meet((*at.around, *at.along_x, *at.along_y, *at.along_z))
    send = Sender(send_sem, recv_sem)
    above, below = at.above, at.below
    up, down = (above, below), (below, above)
    base = at.core * 128
    base_x = base + at.x * 32
    base_y = base_x + at.y * 8
    near_rim, far_rim = pl.ds(at.near_rim, 1), pl.ds(at.far_rim, 1)
    far_edge = pl.ds(at.far_edge, 1)
    near_part, far_part = pl.ds(at.near_edge - 1, 1), pl.ds(at.far_edge - 1, 1)

    s0 = send(psum.at[:, pl.ds(128 - base, 128), :], buf0, at.twin)
    twins = send(grad.at[:, near_rim, : 2 * F, :], sides_in.at[at.core], at.twin)
    corners = [
        [
            send(grad.at[pl.ds(ch, 1), far_rim, ABOVE, :], far_in.at[1, pl.ds(ch, 1)], at.up, *up),
            send(grad.at[pl.ds(ch, 1), far_rim, BELOW, :], far_in.at[0, pl.ds(ch, 1)], at.down, *down),
        ]
        for ch in range(3)
    ]
    near_rims = []
    rims = [
        send(grad.at[:, far_edge, ABOVE, :], from_down.at[:, far_part], at.up, *up),
        send(grad.at[:, far_edge, BELOW, :], from_up.at[:, far_part], at.down, *down),
    ]
    arrive([s0])
    acc0[...] = psum[:, pl.ds(base, 128), :] + buf0[...]
    s1 = [
        send(acc0.at[:, pl.ds((at.x + d) % 4 * 32, 32), :], buf1.at[d - 1], at.along_x[d - 1])
        for d in (1, 2, 3)
    ]
    arrive([twins])
    for ch in range(3):
        for k, rows in enumerate((ABOVE, BELOW)):
            strips[k, ch, 0] = grad[ch, at.near_edge, rows, :] + sides_in[1 - at.core, ch, 0, rows, :]

    relays = [
        send(strips.at[0], relay, at.row_first, at.over, at.first),
        send(strips.at[1], relay, at.row_final, at.under, at.final),
    ]

    def send_near():
        near_rims.extend([
            send(strips.at[0], from_down.at[:, near_part], at.up, above & ~at.over, below & ~at.under),
            send(strips.at[1], from_up.at[:, near_part], at.down, below & ~at.under, above & ~at.over),
        ])

    if not last:
        send_near()

    for ch in range(3):
        arrive(corners[ch])
        side[ch, 0, :HALF, :] = grad[ch, at.far_rim, TOP, :] + jnp.where(above, far_in[0, ch, 0], 0.0)
        side[ch, 0, HALF:, :] = grad[ch, at.far_rim, BOTTOM, :] + jnp.where(below, far_in[1, ch, 0], 0.0)
        there = sides_in.at[1 - at.core, pl.ds(ch, 1), :, INNER, :]
        rims.append(send(side.at[pl.ds(ch, 1)], there, at.far, at.aside, at.aside))
    arrive(s1)
    acc1[...] = acc0[:, pl.ds(at.x * 32, 32), :] + buf1[0] + buf1[1] + buf1[2]
    s2 = [
        send(acc1.at[:, pl.ds((at.y + d) % 4 * 8, 8), :], buf2.at[d - 1], at.along_y[d - 1])
        for d in (1, 2, 3)
    ]
    if last:
        send_near()
    arrive(s2)
    acc2[...] = acc1[:, pl.ds(at.y * 8, 8), :] + buf2[0] + buf2[1] + buf2[2]
    buf3[at.z] = acc2[...]
    s3 = [send(acc2, buf3.at[at.z], at.along_z[d - 1]) for d in (1, 2, 3)]

    arrive(relays)
    near_rims += [
        send(relay, from_down.at[:, near_part], at.row_under, at.first, at.under),
        send(relay, from_up.at[:, near_part], at.row_over, at.final, at.over),
    ]

    def finish(tile, beside):
        for half, (level, rim) in enumerate(((above, from_up), (below, from_down))):
            rows = pl.ds(HALF * half, HALF)
            place = pl.ds(HALF + HALF * half, HALF)
            sums = []
            for ch in range(3):
                rims_sum = jnp.where(level, rim[ch, tile - 1], 0.0) + beside(ch, place)
                sums.append(grad[ch, tile, place, :] + rims_sum)
            share = 1.0 / (sums[2] + 1.0)
            for part in range(2):
                cells = old[part, tile, place, :] - sums[part] * share
                if last:
                    columns = pl.ds(pl.multiple_of(128 * (tile - 1), 128), 128)
                    new[part, rows, columns] = cells
                else:
                    new[part, tile, place, :] = cells

    def finish_far():
        arrive(rims)
        finish(at.far_edge, lambda ch, place: jnp.where(at.aside, sides_in[at.core, ch, 0, place, :], 0.0))

    def finish_near():
        arrive(near_rims)
        finish(at.near_edge, lambda ch, place: sides_in[1 - at.core, ch, 0, place, :])

    arrive(s3)
    total = buf3[0] + buf3[1] + buf3[2] + buf3[3]
    mine = pl.ds(base_y, 8)
    probe_new[:, mine, :] = probe[:, mine, :] - total[:2] / (total[2:] + 1.0)
    part = probe_new.at[:, mine, :]
    s4 = [send(part, part, peer) for peer in at.along_y]
    if not last:
        finish_far()
        passing, halo = send_far_halo(send, at, new)
        finish_near()
        relays, strips_out, rest = send_near_halo(send, at, new, halo_relay)
        arriving, halo = (relays, passing, strips_out), halo + rest
    arrive(s4)
    part = probe_new.at[:, pl.ds(base_x, 32), :]
    s5 = [send(part, part, peer) for peer in at.along_x]
    if not last:
        halo += pass_on_halo(send, at, new, halo_relay, arriving)
    arrive(s5)
    part = probe_new.at[:, pl.ds(base, 128), :]
    s6 = send(part, part, at.twin)
    if last:
        finish_far()
        finish_near()
    arrive([s6])
    if not last:
        arrive(halo)
    send.close()
    if not last:
        clear_outside(at, new)


VMEM = pl.BlockSpec(memory_space=pltpu.VMEM)
SMEM = pl.BlockSpec(memory_space=pltpu.SMEM)
LIMIT = 20 * 2**20


def open_halo(cells):
    return pl.pallas_call(
        open_kernel,
        out_shape=jax.ShapeDtypeStruct((2, 4, ROWS, 128), f32),
        in_specs=[VMEM],
        out_specs=VMEM,
        scratch_shapes=[
            pltpu.VMEM((1, 1, HALF, 128), f32),
            pltpu.SemaphoreType.DMA((22,)),
            pltpu.SemaphoreType.DMA((22,)),
        ],
        compiler_params=pltpu.CompilerParams(
            collective_id=0, has_side_effects=True, vmem_limit_bytes=LIMIT
        ),
    )(cells)


def step(last, grad, psum, old, probe):
    shape = (2, F, F) if last else (2, 4, ROWS, 128)
    copies = 35 if last else 57
    return pl.pallas_call(
        functools.partial(step_kernel, last),
        out_shape=(jax.ShapeDtypeStruct(shape, f32), jax.ShapeDtypeStruct((2, F, F), f32)),
        in_specs=[VMEM] * 4,
        out_specs=(VMEM, VMEM),
        scratch_shapes=[
            pltpu.VMEM((3, 2, HALF, 128), f32),
            pltpu.VMEM((3, 2, HALF, 128), f32),
            pltpu.VMEM((2, 3, 1, 2 * F, 128), f32),
            pltpu.VMEM((2, 3, 1, HALF, 128), f32),
            pltpu.VMEM((3, 1, F, 128), f32),
            pltpu.VMEM((2, 3, 1, HALF, 128), f32),
            pltpu.VMEM((3, 1, HALF, 128), f32),
            pltpu.VMEM((1, 1, HALF, 128), f32),
            pltpu.VMEM((3, 128, F), f32),
            pltpu.VMEM((3, 128, F), f32),
            pltpu.VMEM((3, 32, F), f32),
            pltpu.VMEM((3, 3, 32, F), f32),
            pltpu.VMEM((3, 8, F), f32),
            pltpu.VMEM((3, 3, 8, F), f32),
            pltpu.VMEM((4, 3, 8, F), f32),
            pltpu.SemaphoreType.DMA((copies,)),
            pltpu.SemaphoreType.DMA((copies,)),
        ],
        compiler_params=pltpu.CompilerParams(
            collective_id=2 if last else 1, has_side_effects=True, vmem_limit_bytes=LIMIT
        ),
    )(grad, psum, old, probe)


def body(positions, counts, amplitudes, object_field, probe):
    fwd, inv = tables()
    corners = positions[0, 0].T
    load = counts[0]
    ext = open_halo(object_field)
    for iteration in range(ITERS):
        grad, psum = slots(corners, load, amplitudes[0, 0], ext, probe, fwd, inv)
        ext, probe = step(iteration == ITERS - 1, grad, psum, ext, probe)
    return ext, probe


def solution(mesh):
    return jax.shard_map(
        body,
        mesh=mesh,
        in_specs=(
            P("row", "col", None, None),
            P("row", "col"),
            P("row", "col", None, None, None),
            P(None, "row", "col"),
            P(),
        ),
        out_specs=(P(None, "row", "col"), P()),
        check_vma=False,
    )
```

```python
import functools, math
import numpy as np
import jax, jax.numpy as jnp
from jax import lax
from jax.experimental import pallas as pl
from jax.experimental.pallas import tpu as pltpu
from jax.sharding import PartitionSpec as P

F = 256
ITERS = 2
f32=jnp.float32; bf16=jnp.bfloat16

def tables():
    c=np.arange(F,dtype=np.int32)
    ang=(c[:,None]*c[None,:]%F).astype(np.float32)*np.float32(2*math.pi/F)
    re=(np.cos(ang)/np.float32(16)).astype(np.float32)
    im=(-np.sin(ang)/np.float32(16)).astype(np.float32)
    fwd=np.block([[re,-im],[im,re]]); inv=np.block([[re,im],[-im,re]])
    return jnp.asarray(fwd,bf16), jnp.asarray(inv,bf16)

CH=16; B=2; ROWS=3*F
def both_sides(table, other, cells, half):
    left = jnp.dot(table[...], cells[...], preferred_element_type=f32).astype(bf16)
    for b in range(B):
        half[F * b : F * b + F, :F] = left[:F, F * b : F * b + F]
        half[F * b : F * b + F, F:] = left[F:, F * b : F * b + F]
    return jnp.dot(half[...], other[...], preferred_element_type=f32)


def slots_kernel(corner, load, amp, ext, probe, fwd, inv, grad, psum,
                 patch0, patch1, cov, exit_s, half0, half1, miss0, miss1, chi_s):
    lane=lax.broadcasted_iota(jnp.int32,(CH,128),1)
    n=load[0]
    top=lax.axis_index("row")*F-F//2; left=lax.axis_index("col")*F-F//2
    def place(k):
        kk=jnp.minimum(k,15)
        live=k<n
        r=jnp.where(live,corner[0,kk]-top,2*F); c=jnp.where(live,corner[1,kk]-left,0)
        q=c//128; s=c-q*128
        return r,q,s,kk
    def front(g,patch,miss):
        for b in range(B):
            r,q,s,kk=place(B*g+b)
            back=jnp.where(s==0,0,128-s)
            keep=lane<128-s
            for i in range(F//CH):
                rows=pl.ds(i*CH,CH)
                got=[]
                for ch in range(2):
                    t=[pltpu.roll(ext[ch,q+j,pl.ds(r+i*CH,CH),:],back,1) for j in range(3)]
                    got.append(jnp.concatenate([jnp.where(keep,t[0],t[1]),jnp.where(keep,t[1],t[2])],1))
                re,im=got
                patch[b,0,rows,:]=re; patch[b,1,rows,:]=im
                pr=probe[0,rows,:]; pi=probe[1,rows,:]
                exit_s[rows,F*b:F*b+F]=(pr*re-pi*im).astype(bf16)
                exit_s[pl.ds(F+i*CH,CH),F*b:F*b+F]=(pr*im+pi*re).astype(bf16)
        far=both_sides(fwd,inv,exit_s,half0)
        for b in range(B):
            kk=jnp.minimum(B*g+b,15)
            fr=far[F*b:F*b+F,:F]; fi=far[F*b:F*b+F,F:]
            ratio=1.0-amp[kk].astype(f32)*lax.rsqrt(fr*fr+fi*fi+1.0)
            miss[:F,F*b:F*b+F]=(fr*ratio).astype(bf16)
            miss[F:,F*b:F*b+F]=(fi*ratio).astype(bf16)
    def back_(g,patch,miss):
        chi=both_sides(inv,fwd,miss,half1)
        chi_s[...]=chi
        for i in range(F//CH):
            rows=pl.ds(i*CH,CH)
            pr=probe[0,rows,:]; pi=probe[1,rows,:]
            p0=p1=p2=0.0
            for b in range(B):
                at_=pl.ds(F*b+i*CH,CH)
                cr=chi_s[at_,:F]; ci=chi_s[at_,F:]
                re=patch[b,0,rows,:]; im=patch[b,1,rows,:]
                p0+=re*cr+im*ci; p1+=re*ci-im*cr; p2+=re*re+im*im
            psum[0,rows,:]+=p0; psum[1,rows,:]+=p1; psum[2,rows,:]+=p2
        for b in range(B):
            r,q,s,kk=place(B*g+b)
            put=lane>=s
            for i in range(F//CH):
                rows=pl.ds(i*CH,CH); at_=pl.ds(F*b+i*CH,CH)
                cr=chi_s[at_,:F]; ci=chi_s[at_,F:]
                pr=probe[0,rows,:]; pi=probe[1,rows,:]
                for ch,u in ((0,pr*cr+pi*ci),(1,pr*ci-pi*cr),(2,cov[rows,:])):
                    u0=pltpu.roll(u[:,:128],s,1); u1=pltpu.roll(u[:,128:],s,1)
                    at=pl.ds(r+i*CH,CH)
                    grad[ch,q,at,:]+=jnp.where(put,u0,0.0)
                    grad[ch,q+1,at,:]+=jnp.where(put,u1,u0)
                    grad[ch,q+2,at,:]+=jnp.where(put,0.0,u1)
    for ch in range(3):
        for j in range(4):
            grad[ch,j,:2*F,:]=jnp.zeros((2*F,128),f32)
    psum[...]=jnp.zeros(psum.shape,f32)
    cov[...]=probe[0]*probe[0]+probe[1]*probe[1]
    front(0,patch0,miss0)
    pairs=(n+2*B-1)//(2*B)
    def it(j,_):
        back_(2*j,patch0,miss0)
        front(2*j+1,patch1,miss1)
        back_(2*j+1,patch1,miss1)
        front(2*j+2,patch0,miss0)
        return 0
    lax.fori_loop(0,pairs-1,it,0)
    back_(2*pairs-2,patch0,miss0)
    front(2*pairs-1,patch1,miss1)
    back_(2*pairs-1,patch1,miss1)
def slots(corner,load,amp,ext,probe,fwd,inv):
    V=pl.BlockSpec(memory_space=pltpu.VMEM); S=pl.BlockSpec(memory_space=pltpu.SMEM)
    return pl.pallas_call(slots_kernel,
        out_shape=(jax.ShapeDtypeStruct((3,4,ROWS,128),f32),jax.ShapeDtypeStruct((3,F,F),f32)),
        in_specs=[S,S,V,V,V,V,V], out_specs=(V,V),
        scratch_shapes=[pltpu.VMEM((B,2,F,F),f32),pltpu.VMEM((B,2,F,F),f32),pltpu.VMEM((F,F),f32),pltpu.VMEM((2*F,B*F),bf16),
            pltpu.VMEM((B*F,2*F),bf16),pltpu.VMEM((B*F,2*F),bf16),
            pltpu.VMEM((2*F,B*F),bf16),pltpu.VMEM((2*F,B*F),bf16),pltpu.VMEM((B*F,2*F),f32)],
        compiler_params=pltpu.CompilerParams(vmem_limit_bytes=24*2**20),
    )(corner,load,amp,ext,probe,fwd,inv)


MESH = pl.DeviceIdType.MESH
HALF = F // 2
TILE = slice(HALF, HALF + F)


TOP, BOTTOM = pl.ds(HALF, HALF), pl.ds(F, HALF)
ABOVE, BELOW = pl.ds(0, HALF), pl.ds(F + HALF, HALF)


class Places:
    def __init__(self):
        row, col = lax.axis_index("row"), lax.axis_index("col")
        n_row, n_col = lax.axis_size("row"), lax.axis_size("col")
        self.row, self.col, self.n_row, self.n_col = row, col, n_row, n_col
        z_lo, self.y = row // 4, row % 4
        self.x, z_hi, self.core = col // 4, col // 2 % 2, col % 2
        self.z = z_hi * 2 + z_lo
        self.up, self.down = ((row + n_row - 1) % n_row, col), ((row + 1) % n_row, col)
        self.twin = (row, col + 1 - 2 * self.core)
        self.far = (row, (col + n_col - 1 + 2 * self.core) % n_col)
        self.near_north, self.near_south = (self.up[0], self.twin[1]), (self.down[0], self.twin[1])
        self.far_north, self.far_south = (self.up[0], self.far[1]), (self.down[0], self.far[1])
        self.around = (
            self.up, self.down, self.twin, self.far,
            self.near_north, self.near_south, self.far_north, self.far_south,
        )
        self.above, self.below = row > 0, row < n_row - 1
        self.aside = (col > 0) & (col < n_col - 1)
        self.over, self.under = row == n_row // 2, row == n_row // 2 - 1
        self.first, self.final = row == 0, row == n_row - 1
        self.row_first, self.row_final = (0 * row, col), (0 * row + n_row - 1, col)
        self.row_under, self.row_over = (0 * row + n_row // 2 - 1, col), (0 * row + n_row // 2, col)
        self.near_rim, self.far_rim = 3 - 3 * self.core, 3 * self.core
        self.near_edge, self.far_edge = 2 - self.core, 1 + self.core
        self.along_x = [(row, (self.x + d) % 4 * 4 + col % 4) for d in (1, 2, 3)]
        self.across = [(row, (self.x + d) % 4 * 4 + col % 4 + 1 - 2 * self.core) for d in (1, 2, 3)]
        self.along_y = [(z_lo * 4 + (self.y + d) % 4, col) for d in (1, 2, 3)]
        self.along_z = []
        for d in (1, 2, 3):
            z = (self.z + d) % 4
            self.along_z.append((z % 2 * 4 + self.y, self.x * 4 + z // 2 * 2 + self.core))


def meet(peers):
    barrier = pltpu.get_barrier_semaphore()
    for peer in peers:
        pl.semaphore_signal(barrier, inc=1, device_id=peer, device_id_type=MESH)
    pl.semaphore_wait(barrier, len(peers))


def run_if(condition, action):
    if condition is None:
        action()
    else:
        pl.when(condition)(action)


class Sender:
    def __init__(self, send_sem, recv_sem):
        self.send_sem, self.recv_sem, self.used = send_sem, recv_sem, 0
        self.open = []

    def __call__(self, src, dst, peer, sends=None, gets=None):
        copy = pltpu.make_async_remote_copy(
            src_ref=src,
            dst_ref=dst,
            send_sem=self.send_sem.at[self.used],
            recv_sem=self.recv_sem.at[self.used],
            device_id=peer,
            device_id_type=MESH,
        )
        self.used += 1
        run_if(sends, copy.start)
        self.open.append((copy, sends))
        return copy, gets

    def close(self):
        for copy, sends in self.open:
            run_if(sends, copy.wait_send)


def arrive(copies):
    for copy, gets in copies:
        run_if(gets, copy.wait_recv)


INNER = pl.ds(HALF, F)
BOTH = pl.ds(1, 2)


def send_far_halo(send, at, ext):
    far, there = pl.ds(at.far_edge, 1), pl.ds(at.near_rim, 1)
    up, down, aside = (at.above, at.below), (at.below, at.above), (at.aside, at.aside)
    up_aside, down_aside = (at.above & at.aside, at.below & at.aside), (at.below & at.aside, at.above & at.aside)
    real, imag = pl.ds(0, 1), pl.ds(1, 1)
    return [send(ext.at[imag, far, INNER, :], ext.at[imag, there, INNER, :], at.far, *aside)], [
        send(ext.at[real, far, INNER, :], ext.at[real, there, INNER, :], at.far, *aside),
        send(ext.at[:, far, TOP, :], ext.at[:, far, BELOW, :], at.up, *up),
        send(ext.at[:, far, BOTTOM, :], ext.at[:, far, ABOVE, :], at.down, *down),
        send(ext.at[real, far, TOP, :], ext.at[real, there, BELOW, :], at.far_north, *up_aside),
        send(ext.at[real, far, BOTTOM, :], ext.at[real, there, ABOVE, :], at.far_south, *down_aside),
    ]


def send_near_halo(send, at, ext, relay):
    near, there = pl.ds(at.near_edge, 1), pl.ds(at.far_rim, 1)
    up, down = (at.above, at.below), (at.below, at.above)
    up_near = (at.above & ~at.over, at.below & ~at.under)
    down_near = (at.below & ~at.under, at.above & ~at.over)
    real, imag = pl.ds(0, 1), pl.ds(1, 1)
    relays = [
        send(ext.at[real, near, TOP, :], relay, at.row_first, at.over, at.first),
        send(ext.at[real, near, BOTTOM, :], relay, at.row_final, at.under, at.final),
    ]
    strips = [
        send(ext.at[imag, near, TOP, :], ext.at[imag, near, BELOW, :], at.up, *up),
        send(ext.at[imag, near, BOTTOM, :], ext.at[imag, near, ABOVE, :], at.down, *down),
        send(ext.at[real, near, TOP, :], ext.at[real, near, BELOW, :], at.up, *up_near),
        send(ext.at[real, near, BOTTOM, :], ext.at[real, near, ABOVE, :], at.down, *down_near),
    ]
    return relays, strips, [send(ext.at[:, near, INNER, :], ext.at[:, there, INNER, :], at.twin)]


def pass_on_halo(send, at, ext, relay, arriving):
    relays, side, strips = arriving
    near, far, there = pl.ds(at.near_edge, 1), pl.ds(at.far_rim, 1), pl.ds(at.far_rim, 1)
    real, imag = pl.ds(0, 1), pl.ds(1, 1)
    up_aside, down_aside = (at.above & at.aside, at.below & at.aside), (at.below & at.aside, at.above & at.aside)
    copies, relayed = [], []
    arrive(relays)
    for (row, col), rows, sends, gets in (
        (at.row_under, BELOW, at.first, at.under),
        (at.row_over, ABOVE, at.final, at.over),
    ):
        relayed.append(send(relay, ext.at[real, near, rows, :], (row, col), sends, gets))
    arrive(side)
    copies += [
        send(ext.at[imag, far, TOP, :], ext.at[imag, far, BELOW, :], at.up, *up_aside),
        send(ext.at[imag, far, BOTTOM, :], ext.at[imag, far, ABOVE, :], at.down, *down_aside),
    ]
    arrive(strips + relayed)
    for rows, has in ((ABOVE, at.above), (BELOW, at.below)):
        copies.append(send(ext.at[:, near, rows, :], ext.at[:, there, rows, :], at.twin, has, has))
    return copies


def clear_outside(at, ext):
    ext[:, :, 2 * F :, :] = jnp.zeros((2, 4, ROWS - 2 * F, 128), f32)

    @pl.when(at.row == 0)
    def _():
        ext[:, :, :HALF, :] = jnp.zeros((2, 4, HALF, 128), f32)

    @pl.when(at.row == at.n_row - 1)
    def _():
        ext[:, :, F + HALF : 2 * F, :] = jnp.zeros((2, 4, HALF, 128), f32)

    @pl.when(at.col == 0)
    def _():
        ext[:, 0, : 2 * F, :] = jnp.zeros((2, 2 * F, 128), f32)

    @pl.when(at.col == at.n_col - 1)
    def _():
        ext[:, 3, : 2 * F, :] = jnp.zeros((2, 2 * F, 128), f32)


def open_kernel(cells, ext, relay, send_sem, recv_sem):
    at = Places()
    meet((*at.around, *at.along_y[::2], *at.along_z[::2]))
    for part in range(2):
        for j in range(2):
            ext[part, 1 + j, TILE, :] = cells[part, :, 128 * j : 128 * j + 128]
    send = Sender(send_sem, recv_sem)
    relays, strips, rest = send_near_halo(send, at, ext, relay)
    side, halo = send_far_halo(send, at, ext)
    halo += rest + pass_on_halo(send, at, ext, relay, (relays, side, strips))
    arrive(halo)
    send.close()
    clear_outside(at, ext)


def step_kernel(last, grad, psum, old, probe, new, probe_new, *scratch):
    from_up, from_down, sides_in, far_in, side, strips, relay, halo_relay = scratch[:8]
    acc1, buf1, acc2, buf2, buf3, send_sem, recv_sem = scratch[8:]
    at = Places()
    meet((*at.around, *at.along_x, *at.across, *at.along_y, *at.along_z))
    send = Sender(send_sem, recv_sem)
    above, below = at.above, at.below
    up, down = (above, below), (below, above)
    base = at.core * 128
    base_x = base + at.x * 32
    base_y = base_x + at.y * 8
    near_rim, far_rim = pl.ds(at.near_rim, 1), pl.ds(at.far_rim, 1)
    far_edge = pl.ds(at.far_edge, 1)
    near_part, far_part = pl.ds(at.near_edge - 1, 1), pl.ds(at.far_edge - 1, 1)

    s1 = []
    for k, (peer, core, d) in enumerate(
        [(at.along_x[d - 1], at.core, d) for d in (1, 2, 3)]
        + [(at.across[d - 1], 1 - at.core, d) for d in (1, 2, 3)]
        + [(at.twin, 1 - at.core, 0)]
    ):
        rows = pl.ds(core * 128 + (at.x + d) % 4 * 32, 32)
        s1.append(send(psum.at[:, rows, :], buf1.at[k], peer))
    twins = send(grad.at[:, near_rim, : 2 * F, :], sides_in.at[at.core], at.twin)
    corners = [
        [
            send(grad.at[pl.ds(ch, 1), far_rim, ABOVE, :], far_in.at[1, pl.ds(ch, 1)], at.up, *up),
            send(grad.at[pl.ds(ch, 1), far_rim, BELOW, :], far_in.at[0, pl.ds(ch, 1)], at.down, *down),
        ]
        for ch in range(3)
    ]
    near_rims = []
    rims = [
        send(grad.at[:, far_edge, ABOVE, :], from_down.at[:, far_part], at.up, *up),
        send(grad.at[:, far_edge, BELOW, :], from_up.at[:, far_part], at.down, *down),
    ]
    arrive([twins])
    for ch in range(3):
        for k, rows in enumerate((ABOVE, BELOW)):
            strips[k, ch, 0] = grad[ch, at.near_edge, rows, :] + sides_in[1 - at.core, ch, 0, rows, :]

    relays = [
        send(strips.at[0], relay, at.row_first, at.over, at.first),
        send(strips.at[1], relay, at.row_final, at.under, at.final),
    ]

    def send_near():
        near_rims.extend([
            send(strips.at[0], from_down.at[:, near_part], at.up, above & ~at.over, below & ~at.under),
            send(strips.at[1], from_up.at[:, near_part], at.down, below & ~at.under, above & ~at.over),
        ])

    if not last:
        send_near()

    for ch in range(3):
        arrive(corners[ch])
        side[ch, 0, :HALF, :] = grad[ch, at.far_rim, TOP, :] + jnp.where(above, far_in[0, ch, 0], 0.0)
        side[ch, 0, HALF:, :] = grad[ch, at.far_rim, BOTTOM, :] + jnp.where(below, far_in[1, ch, 0], 0.0)
        there = sides_in.at[1 - at.core, pl.ds(ch, 1), :, INNER, :]
        rims.append(send(side.at[pl.ds(ch, 1)], there, at.far, at.aside, at.aside))
    arrive(s1)
    total = psum[:, pl.ds(base_x, 32), :]
    for k in range(7):
        total = total + buf1[k]
    acc1[...] = total
    s2 = [
        send(acc1.at[:, pl.ds((at.y + d) % 4 * 8, 8), :], buf2.at[d - 1], at.along_y[d - 1])
        for d in (1, 2, 3)
    ]
    if last:
        send_near()
    arrive(s2)
    acc2[...] = acc1[:, pl.ds(at.y * 8, 8), :] + buf2[0] + buf2[1] + buf2[2]
    buf3[at.z] = acc2[...]
    s3 = [send(acc2, buf3.at[at.z], at.along_z[d - 1]) for d in (1, 2, 3)]

    arrive(relays)
    near_rims += [
        send(relay, from_down.at[:, near_part], at.row_under, at.first, at.under),
        send(relay, from_up.at[:, near_part], at.row_over, at.final, at.over),
    ]

    def finish(tile, beside):
        for half, (level, rim) in enumerate(((above, from_up), (below, from_down))):
            rows = pl.ds(HALF * half, HALF)
            place = pl.ds(HALF + HALF * half, HALF)
            sums = []
            for ch in range(3):
                rims_sum = jnp.where(level, rim[ch, tile - 1], 0.0) + beside(ch, place)
                sums.append(grad[ch, tile, place, :] + rims_sum)
            share = 1.0 / (sums[2] + 1.0)
            for part in range(2):
                cells = old[part, tile, place, :] - sums[part] * share
                if last:
                    columns = pl.ds(pl.multiple_of(128 * (tile - 1), 128), 128)
                    new[part, rows, columns] = cells
                else:
                    new[part, tile, place, :] = cells

    def finish_far():
        arrive(rims)
        finish(at.far_edge, lambda ch, place: jnp.where(at.aside, sides_in[at.core, ch, 0, place, :], 0.0))

    def finish_near():
        arrive(near_rims)
        finish(at.near_edge, lambda ch, place: sides_in[1 - at.core, ch, 0, place, :])

    arrive(s3)
    total = buf3[0] + buf3[1] + buf3[2] + buf3[3]
    mine = pl.ds(base_y, 8)
    probe_new[:, mine, :] = probe[:, mine, :] - total[:2] / (total[2:] + 1.0)
    part = probe_new.at[:, mine, :]
    s4 = [send(part, part, peer) for peer in at.along_y]
    if not last:
        finish_far()
        passing, halo = send_far_halo(send, at, new)
        finish_near()
        relays, strips_out, rest = send_near_halo(send, at, new, halo_relay)
        arriving, halo = (relays, passing, strips_out), halo + rest
    arrive(s4)
    part = probe_new.at[:, pl.ds(base_x, 32), :]
    s5 = [send(part, part, peer) for peer in (*at.along_x, *at.across, at.twin)]
    if not last:
        halo += pass_on_halo(send, at, new, halo_relay, arriving)
    if last:
        finish_far()
        finish_near()
    arrive(s5)
    if not last:
        arrive(halo)
    send.close()
    if not last:
        clear_outside(at, new)


VMEM = pl.BlockSpec(memory_space=pltpu.VMEM)
SMEM = pl.BlockSpec(memory_space=pltpu.SMEM)
LIMIT = 20 * 2**20


def open_halo(cells):
    return pl.pallas_call(
        open_kernel,
        out_shape=jax.ShapeDtypeStruct((2, 4, ROWS, 128), f32),
        in_specs=[VMEM],
        out_specs=VMEM,
        scratch_shapes=[
            pltpu.VMEM((1, 1, HALF, 128), f32),
            pltpu.SemaphoreType.DMA((22,)),
            pltpu.SemaphoreType.DMA((22,)),
        ],
        compiler_params=pltpu.CompilerParams(
            collective_id=0, has_side_effects=True, vmem_limit_bytes=LIMIT
        ),
    )(cells)


def step(last, grad, psum, old, probe):
    shape = (2, F, F) if last else (2, 4, ROWS, 128)
    copies = 41 if last else 63
    return pl.pallas_call(
        functools.partial(step_kernel, last),
        out_shape=(jax.ShapeDtypeStruct(shape, f32), jax.ShapeDtypeStruct((2, F, F), f32)),
        in_specs=[VMEM] * 4,
        out_specs=(VMEM, VMEM),
        scratch_shapes=[
            pltpu.VMEM((3, 2, HALF, 128), f32),
            pltpu.VMEM((3, 2, HALF, 128), f32),
            pltpu.VMEM((2, 3, 1, 2 * F, 128), f32),
            pltpu.VMEM((2, 3, 1, HALF, 128), f32),
            pltpu.VMEM((3, 1, F, 128), f32),
            pltpu.VMEM((2, 3, 1, HALF, 128), f32),
            pltpu.VMEM((3, 1, HALF, 128), f32),
            pltpu.VMEM((1, 1, HALF, 128), f32),
            pltpu.VMEM((3, 32, F), f32),
            pltpu.VMEM((7, 3, 32, F), f32),
            pltpu.VMEM((3, 8, F), f32),
            pltpu.VMEM((3, 3, 8, F), f32),
            pltpu.VMEM((4, 3, 8, F), f32),
            pltpu.SemaphoreType.DMA((copies,)),
            pltpu.SemaphoreType.DMA((copies,)),
        ],
        compiler_params=pltpu.CompilerParams(
            collective_id=2 if last else 1, has_side_effects=True, vmem_limit_bytes=LIMIT
        ),
    )(grad, psum, old, probe)


def body(positions, counts, amplitudes, object_field, probe):
    fwd, inv = tables()
    corners = positions[0, 0].T
    load = counts[0]
    ext = open_halo(object_field)
    for iteration in range(ITERS):
        grad, psum = slots(corners, load, amplitudes[0, 0], ext, probe, fwd, inv)
        ext, probe = step(iteration == ITERS - 1, grad, psum, ext, probe)
    return ext, probe


def solution(mesh):
    return jax.shard_map(
        body,
        mesh=mesh,
        in_specs=(
            P("row", "col", None, None),
            P("row", "col"),
            P("row", "col", None, None, None),
            P(None, "row", "col"),
            P(),
        ),
        out_specs=(P(None, "row", "col"), P()),
        check_vma=False,
    )
```
